128 devices in a mesh: grp: 4 (over z), mem: 32 (over y, x, core).
Axes of the slice: x: 4, y: 4, z: 4, core: 2. Of those that a mesh axis runs over, the one named last changes fastest.
Arguments:
- volume: float32 [4, 32, 8, 512, 1024], P('grp', 'mem'), may hold values from -1 to 1
- transfer_coef: float32 [4, 4], replicated, may hold values from -3 to 3
- group_order: int32 [4], replicated, may hold values from 0 to 3, each once
- member_order: int32 [4, 32], replicated, may hold values from 0 to 31, each once within a row
- active_mask: int32 [4, 32], P('grp', 'mem'), may hold values 0 or 1
Outputs:
- picture: float32 [4, 512, 1024], P(None, 'mem', 'grp')
The draws below stay inside these ranges and needn't reach their ends.
All inputs are finite; a program needn't handle non-finite values. No bound on the sum of `active_mask` on one device may be relied on, other than what follows from the above.
Results may differ from the reference program's by a relative error of at most 0.0003.
Values sent between devices are 32-bit elements; how exact they have to be, the bound alone decides.
No kernel may reach another device: no remote copies, remote signals or barrier semaphores. Data moves between devices by JAX's collectives and lax.ppermute only.
A program may use at most 192 MiB of HBM per device.

```python
import jax
import jax.numpy as jnp
from jax import lax

SAMPLES = 8
ROWS = 512
COLS = 1024
N_GRP = 4
N_MEM = 32


def touch_ends(result, own_key, smallest, top_value):
    longest = result.shape.index(max(result.shape))
    spots = []
    for shift in (0, 1):
        where = [jax.random.randint(jax.random.fold_in(own_key, axis), (), 0, length) for axis, length in enumerate(result.shape)]
        where[longest] = (where[longest] + shift) % result.shape[longest]
        spots.append(tuple(where))
    return result.at[spots[0]].set(smallest).at[spots[1]].set(top_value)


def steps_of(stream_key, dims, shards, low, top_value):
    loudness, own = 1.0, jax.random.fold_in(stream_key, 6)
    for axis_at, shards_of in shards:
        steps = jnp.exp(jax.random.uniform(jax.random.fold_in(own, axis_at), (shards_of,), jnp.float32, low / len(shards), top_value / len(shards)))
        loudness = loudness * jnp.repeat(steps, dims[axis_at] // shards_of).reshape([-1 if axis == axis_at else 1 for axis in range(len(dims))])
    return loudness


def gaussian(stream_key, extent, width, reach, kind=jnp.bfloat16):
    values = jax.random.normal(stream_key, extent, jnp.float32) * width
    return jnp.minimum(jnp.maximum(values, -reach), reach).astype(kind)


def setup_inputs(seed: int = 0) -> dict:
    key_of = jax.random.split(jax.random.key(seed), 6)
    return {
        "volume": jnp.clip(jax.random.uniform(key_of[0], (N_GRP, N_MEM, SAMPLES, ROWS, COLS), jnp.float32, -1.0, 1.0) * steps_of(key_of[0], (N_GRP, N_MEM, SAMPLES, ROWS, COLS), ((0, 4), (1, 32)), -0.4, 0.0), -1.0, 1.0),
        "transfer_coef": gaussian(key_of[1], (4, 4), 0.6, 3.0, jnp.float32),
        "group_order": jax.random.permutation(key_of[2], N_GRP).astype(jnp.int32),
        "member_order": jax.vmap(lambda own: jax.random.permutation(own, N_MEM))(jax.random.split(key_of[3], N_GRP)).reshape((N_GRP, N_MEM)).astype(jnp.int32),
        "active_mask": touch_ends((jax.random.randint(key_of[4], (N_GRP, N_MEM), 0, 4) < 3).astype(jnp.int32), jax.random.fold_in(key_of[4], 1), 0, 1),
    }


def polynomial(coef_row, values):
    return coef_row[0] + values * (coef_row[1] + values * (coef_row[2] + values * coef_row[3]))


def march_brick(samples, transfer_coef, active_flag):
    density_scale = 3.0 / (SAMPLES * N_GRP * N_MEM)

    def march_step(state_pair, values):
        optical_depth, colour = state_pair
        extinction = polynomial(transfer_coef[3], values) ** 2 * density_scale
        opacity = 1.0 - jnp.exp(-extinction)
        tinted = jax.nn.sigmoid(jnp.stack([polynomial(transfer_coef[channel], values) for channel in range(3)]))
        colour = colour + (jnp.exp(-optical_depth) * opacity)[None] * tinted
        return (optical_depth + extinction, colour), None

    start = (jnp.zeros(samples.shape[1:], jnp.float32), jnp.zeros((3,) + samples.shape[1:], jnp.float32))
    (optical_depth, colour), unused = lax.scan(march_step, start, samples)
    coverage = 1.0 - jnp.exp(-optical_depth)
    return jnp.concatenate([colour, coverage[None]], 0) * active_flag


def reference(volume, transfer_coef, group_order, member_order, active_mask):
    global_rank = (group_order[:, None] * N_MEM + member_order).reshape(-1).astype(jnp.int32)
    total = N_GRP * N_MEM
    positions = jnp.arange(total, dtype=jnp.int32)
    inverse = jnp.sum(positions[:, None] * (global_rank[:, None] == positions[None, :]).astype(jnp.int32), axis=0).astype(jnp.int32)

    def composite_step(picture, brick_index):
        group_index = brick_index // N_MEM
        member_index = brick_index % N_MEM
        samples = volume[group_index, member_index]
        active_flag = active_mask[group_index, member_index].astype(jnp.float32)
        layer = march_brick(samples, transfer_coef, active_flag)
        return picture + (1.0 - picture[3:4]) * layer, None

    picture, unused = lax.scan(composite_step, jnp.zeros((4, ROWS, COLS), jnp.float32), inverse)
    return picture
```

```python
import functools
import math

import jax
import jax.numpy as jnp
from jax import lax
from jax.experimental import pallas as pl
from jax.experimental.pallas import tpu as pltpu
from jax.sharding import PartitionSpec as P

SAMPLES = 8
ROWS = 512
COLS = 1024
N_GRP = 4
N_MEM = 32
TILE = ROWS // N_MEM
CHUNKS = 2
SUB = TILE // CHUNKS
STRIP = COLS // N_GRP
WIDTH = 512
VMEM = 48 << 20


def cubic(q, v):
    return q[0] + v * (q[1] + v * (q[2] + v * q[3]))


def march_kernel(coef_ref, flag_ref, vol_ref, out_ref, *, tiles):
    q = [[coef_ref[c, k] for k in range(4)] for c in range(4)]
    flag = flag_ref[0, 0].astype(jnp.float32)
    per = COLS // WIDTH

    def step(i, carry):
        t = i // per
        cols = pl.ds(pl.multiple_of((i % per) * WIDTH, 128), WIDTH)
        depth = clear = None
        acc = [None] * 3
        for s in range(SAMPLES):
            v = vol_ref[s, t, 0, :, cols]
            d = cubic(q[3], v)
            depth = -(d * d) if depth is None else depth - d * d
            ahead = jnp.exp2(depth)
            weight = 1.0 - ahead if clear is None else clear - ahead
            clear = ahead
            for ch in range(3):
                x = weight * jnp.tanh(cubic(q[ch], v))
                acc[ch] = x if acc[ch] is None else acc[ch] + x
        cover = 1.0 - clear
        half = 0.5 * flag
        for ch in range(3):
            out_ref[t, ch, :, cols] = (acc[ch] + cover) * half
        out_ref[t, 3, :, cols] = cover * flag
        return carry

    lax.fori_loop(0, tiles * per, step, 0)


def march(coef, flag, volume, chunk, tiles=8):
    return pl.pallas_call(
        functools.partial(march_kernel, tiles=tiles),
        grid=(N_MEM // tiles,),
        in_specs=[
            pl.BlockSpec(memory_space=pltpu.SMEM),
            pl.BlockSpec(memory_space=pltpu.SMEM),
            pl.BlockSpec((SAMPLES, tiles, 1, SUB, COLS), lambda i: (0, i, chunk, 0, 0)),
        ],
        out_specs=pl.BlockSpec((tiles, 4, SUB, COLS), lambda i: (i, 0, 0, 0)),
        out_shape=jax.ShapeDtypeStruct((N_MEM, 4, SUB, COLS), jnp.float32),
        compiler_params=pltpu.CompilerParams(vmem_limit_bytes=VMEM),
        cost_estimate=pl.CostEstimate(
            flops=40 * SAMPLES * ROWS * COLS // CHUNKS,
            bytes_accessed=12 * ROWS * COLS * 4 // CHUNKS,
            transcendentals=4 * SAMPLES * ROWS * COLS // CHUNKS,
        ),
        name="march",
    )(coef, flag, volume)


def slab_kernel(order_ref, layer_ref, out_ref):
    for g in range(N_GRP):
        cols = slice(g * STRIP, (g + 1) * STRIP)

        def step(r, pic):
            j = order_ref[r]
            free = 1.0 - pic[3]
            return tuple(pic[c] + free * layer_ref[j, c, :, cols] for c in range(4))

        zero = jnp.zeros((SUB, STRIP), jnp.float32)
        pic = lax.fori_loop(0, N_MEM, step, (zero,) * 4, unroll=4)
        for c in range(4):
            out_ref[g, c] = pic[c]


def slab(order, layers):
    return pl.pallas_call(
        slab_kernel,
        in_specs=[pl.BlockSpec(memory_space=pltpu.SMEM), pl.BlockSpec(memory_space=pltpu.VMEM)],
        out_specs=pl.BlockSpec(memory_space=pltpu.VMEM),
        out_shape=jax.ShapeDtypeStruct((N_GRP, 4, SUB, STRIP), jnp.float32),
        compiler_params=pltpu.CompilerParams(vmem_limit_bytes=VMEM),
        cost_estimate=pl.CostEstimate(flops=N_MEM * 8 * SUB * COLS, bytes_accessed=N_MEM * 16 * SUB * COLS, transcendentals=0),
        name="slab",
    )(order, layers)


def final_kernel(order_ref, *refs):
    out_ref = refs[-1]
    for k in range(CHUNKS):
        ref = refs[k]
        pic = [jnp.zeros((SUB, STRIP), jnp.float32)] * 4
        for r in range(N_GRP):
            j = order_ref[r]
            free = 1.0 - pic[3]
            pic = [pic[c] + free * ref[j, c] for c in range(4)]
        for c in range(4):
            out_ref[c, k * SUB:(k + 1) * SUB, :] = pic[c]


def final(order, parts):
    return pl.pallas_call(
        final_kernel,
        in_specs=[pl.BlockSpec(memory_space=pltpu.SMEM)] + [pl.BlockSpec(memory_space=pltpu.VMEM)] * CHUNKS,
        out_specs=pl.BlockSpec(memory_space=pltpu.VMEM),
        out_shape=jax.ShapeDtypeStruct((4, TILE, STRIP), jnp.float32),
        name="final",
    )(order, *parts)


def inverse(ranks):
    total = ranks.shape[0]
    spots = jnp.arange(total, dtype=jnp.int32)
    return jnp.sum(spots[:, None] * (ranks[:, None] == spots[None, :]).astype(jnp.int32), axis=0)


def body(volume, transfer_coef, group_order, member_order, active_mask):
    scale = 3.0 / (SAMPLES * N_GRP * N_MEM)
    rows = jnp.array([0.5, 0.5, 0.5, math.sqrt(scale * math.log2(math.e))], jnp.float32)
    coef = transfer_coef * rows[:, None]
    order = inverse(lax.dynamic_index_in_dim(member_order, lax.axis_index("grp"), 0, False))
    groups = inverse(group_order)
    view = volume.reshape(SAMPLES, N_MEM, CHUNKS, SUB, COLS)
    parts = []
    for k in range(CHUNKS):
        layer = march(coef, active_mask, view, k)
        layers = lax.all_to_all(layer, "mem", 0, 0, tiled=True)
        parts.append(lax.all_to_all(slab(order, layers), "grp", 0, 0, tiled=True))
    return final(groups, parts)


def solution(mesh):
    in_specs = (P("grp", "mem", None, None, None), P(), P(), P(), P("grp", "mem"))
    out_specs = P(None, "mem", "grp")
    return jax.shard_map(body, mesh=mesh, in_specs=in_specs, out_specs=out_specs, check_vma=False)
```

```python
import functools
import math

import jax
import jax.numpy as jnp
import numpy as np
from jax import lax
from jax.experimental import pallas as pl
from jax.experimental.pallas import tpu as pltpu
from jax.sharding import PartitionSpec as P

SAMPLES = 8
ROWS = 512
COLS = 1024
N_GRP = 4
N_MEM = 32
SIDE = 4
TILE = ROWS // N_MEM
STRIP = COLS // N_GRP
WIDTH = 512
VMEM = 48 << 20


def cubic(q, v):
    return q[0] + v * (q[1] + v * (q[2] + v * q[3]))


def depth_kernel(coef_ref, flag_ref, vol_ref, out_ref, *, rows, width):
    q = [coef_ref[3, k] for k in range(4)]
    flag = flag_ref[0, 0].astype(jnp.float32)
    per = COLS // width

    def step(i, carry):
        block = pl.ds(pl.multiple_of((i // per) * 8, 8), 8)
        cols = pl.ds(pl.multiple_of((i % per) * width, 128), width)
        total = None
        for s in range(SAMPLES):
            d = cubic(q, vol_ref[s, block, cols])
            total = d * d if total is None else total + d * d
        out_ref[block, cols] = total * flag
        return carry

    lax.fori_loop(0, (rows // 8) * per, step, 0, unroll=2)


def depth(coef, flag, volume, rows=128, width=256):
    return pl.pallas_call(
        functools.partial(depth_kernel, rows=rows, width=width),
        grid=(ROWS // rows,),
        in_specs=[
            pl.BlockSpec(memory_space=pltpu.SMEM),
            pl.BlockSpec(memory_space=pltpu.SMEM),
            pl.BlockSpec((SAMPLES, rows, COLS), lambda i: (0, i, 0)),
        ],
        out_specs=pl.BlockSpec((rows, COLS), lambda i: (i, 0)),
        out_shape=jax.ShapeDtypeStruct((ROWS, COLS), jnp.float32),
        compiler_params=pltpu.CompilerParams(vmem_limit_bytes=VMEM),
        cost_estimate=pl.CostEstimate(flops=8 * SAMPLES * ROWS * COLS, bytes_accessed=9 * 4 * ROWS * COLS, transcendentals=0),
        name="depth",
    )(coef, flag, volume)


def march_kernel(table_ref, coef_ref, flag_ref, vol_ref, out_ref):
    q = [[coef_ref[c, k] for k in range(4)] for c in range(4)]
    half = 0.5 * flag_ref[0, 0].astype(jnp.float32)
    per = COLS // WIDTH

    def step(i, carry):
        block = pl.ds(pl.multiple_of((i // per) * 8, 8), 8)
        cols = pl.ds(pl.multiple_of((i % per) * WIDTH, 128), WIDTH)
        depth = clear = None
        acc = [None] * 3
        for s in range(SAMPLES):
            v = vol_ref[s, 0, block, cols]
            d = cubic(q[3], v)
            depth = -(d * d) if depth is None else depth - d * d
            ahead = jnp.exp2(depth)
            weight = 1.0 - ahead if clear is None else clear - ahead
            clear = ahead
            for ch in range(3):
                x = weight * jnp.tanh(cubic(q[ch], v))
                acc[ch] = x if acc[ch] is None else acc[ch] + x
        cover = 1.0 - clear
        for ch in range(3):
            out_ref[0, ch, block, cols] = (acc[ch] + cover) * half
        return carry

    lax.fori_loop(0, (TILE // 8) * per, step, 0)


def march(table, n, coef, flag, view):
    pixels = SIDE * TILE * COLS
    spec = pltpu.PrefetchScalarGridSpec(
        num_scalar_prefetch=1,
        grid=(SIDE,),
        in_specs=[
            pl.BlockSpec(memory_space=pltpu.SMEM),
            pl.BlockSpec(memory_space=pltpu.SMEM),
            pl.BlockSpec((SAMPLES, 1, TILE, COLS), lambda i, table: (0, table[2 * n] + table[2 * n + 1] * i, 0, 0)),
        ],
        out_specs=pl.BlockSpec((1, 3, TILE, COLS), lambda i, table: (i, 0, 0, 0)),
    )
    return pl.pallas_call(
        march_kernel,
        grid_spec=spec,
        out_shape=jax.ShapeDtypeStruct((SIDE, 3, TILE, COLS), jnp.float32),
        compiler_params=pltpu.CompilerParams(vmem_limit_bytes=VMEM),
        cost_estimate=pl.CostEstimate(
            flops=40 * SAMPLES * pixels, bytes_accessed=11 * 4 * pixels, transcendentals=4 * SAMPLES * pixels
        ),
        name="march",
    )(table, coef, flag, view)


def prefix_kernel(order_ref, table_ref, depth_ref, before_ref, total_ref):
    def strip(i, carry):
        cols = pl.ds(pl.multiple_of(i * STRIP, 128), STRIP)

        def step(r, running):
            j = order_ref[r]
            before_ref[table_ref[SPOT + j], :, cols] = running
            return running + depth_ref[j, :, cols]

        total_ref[:, cols] = lax.fori_loop(0, N_MEM, step, jnp.zeros((TILE, STRIP), jnp.float32), unroll=4)
        return carry

    lax.fori_loop(0, COLS // STRIP, strip, 0)


def prefix(order, table, depths):
    return pl.pallas_call(
        prefix_kernel,
        in_specs=[pl.BlockSpec(memory_space=pltpu.SMEM)] * 2 + [pl.BlockSpec(memory_space=pltpu.VMEM)],
        out_specs=[pl.BlockSpec(memory_space=pltpu.VMEM)] * 2,
        out_shape=[
            jax.ShapeDtypeStruct((N_MEM, TILE, COLS), jnp.float32),
            jax.ShapeDtypeStruct((TILE, COLS), jnp.float32),
        ],
        compiler_params=pltpu.CompilerParams(vmem_limit_bytes=VMEM),
        cost_estimate=pl.CostEstimate(
            flops=N_MEM * TILE * COLS, bytes_accessed=8 * N_MEM * TILE * COLS, transcendentals=0
        ),
        name="prefix",
    )(order, table, depths)


def weigh_kernel(table_ref, *refs):
    colours, before_ref, out_ref = refs[:8], refs[8], refs[9]

    def step(i, carry):
        block = pl.ds(pl.multiple_of((i // 4) * 8, 8), 8)
        cols = pl.ds(pl.multiple_of((i % 4) * 256, 128), 256)
        acc = [None] * 3
        for n in range(8):
            light = jnp.exp2(-before_ref[0, table_ref[SLOT + n], block, cols])
            for ch in range(3):
                x = light * colours[n][0, ch, block, cols]
                acc[ch] = x if acc[ch] is None else acc[ch] + x
        for ch in range(3):
            out_ref[0, ch, block, cols] = acc[ch]
        return carry

    lax.fori_loop(0, 8, step, 0)


def weigh(table, colours, before):
    block = pl.BlockSpec((1, 3, TILE, COLS), lambda i: (i, 0, 0, 0))
    return pl.pallas_call(
        weigh_kernel,
        grid=(SIDE,),
        in_specs=[pl.BlockSpec(memory_space=pltpu.SMEM)]
        + [block] * 8
        + [pl.BlockSpec((1, 8, TILE, COLS), lambda i: (i, 0, 0, 0))],
        out_specs=block,
        out_shape=jax.ShapeDtypeStruct((SIDE, 3, TILE, COLS), jnp.float32),
        compiler_params=pltpu.CompilerParams(vmem_limit_bytes=VMEM),
        cost_estimate=pl.CostEstimate(
            flops=8 * 7 * SIDE * TILE * COLS, bytes_accessed=35 * 4 * SIDE * TILE * COLS, transcendentals=8 * SIDE * TILE * COLS
        ),
        name="weigh",
    )(table, *colours, before)


def slab_kernel(parts_ref, total_ref, out_ref):
    for g in range(N_GRP):
        cols = slice(g * STRIP, (g + 1) * STRIP)
        for ch in range(3):
            out_ref[g, ch] = (parts_ref[0, ch, :, cols] + parts_ref[1, ch, :, cols]) + (
                parts_ref[2, ch, :, cols] + parts_ref[3, ch, :, cols]
            )
        out_ref[g, 3] = 1.0 - jnp.exp2(-total_ref[:, cols])


def slab(parts, total):
    return pl.pallas_call(
        slab_kernel,
        in_specs=[pl.BlockSpec(memory_space=pltpu.VMEM)] * 2,
        out_specs=pl.BlockSpec(memory_space=pltpu.VMEM),
        out_shape=jax.ShapeDtypeStruct((N_GRP, 4, TILE, STRIP), jnp.float32),
        name="slab",
    )(parts, total)


def final_kernel(order_ref, ref, out_ref):
    pic = [jnp.zeros((TILE, STRIP), jnp.float32)] * 4
    for r in range(N_GRP):
        j = order_ref[r]
        free = 1.0 - pic[3]
        pic = [pic[c] + free * ref[j, c] for c in range(4)]
    for c in range(4):
        out_ref[c] = pic[c]


def final(order, slabs):
    return pl.pallas_call(
        final_kernel,
        in_specs=[pl.BlockSpec(memory_space=pltpu.SMEM), pl.BlockSpec(memory_space=pltpu.VMEM)],
        out_specs=pl.BlockSpec(memory_space=pltpu.VMEM),
        out_shape=jax.ShapeDtypeStruct((4, TILE, STRIP), jnp.float32),
        name="final",
    )(order, slabs)


def inverse(ranks):
    total = ranks.shape[0]
    spots = jnp.arange(total, dtype=jnp.int32)
    return jnp.sum(spots[:, None] * (ranks[:, None] == spots[None, :]).astype(jnp.int32), axis=0)


def number(y, x, core):
    return 8 * (y % SIDE) + 2 * (x % SIDE) + core


def pairs(swap, shift):
    out = []
    for y in range(SIDE):
        for x in range(SIDE):
            for core in range(2):
                to = 1 - core if swap else core
                goal = number(y, x + shift, to) if to == 0 else number(y + shift, x, to)
                out.append((number(y, x, core), goal))
    return out


LINES = [[number(y, x, 0) for y in range(SIDE)] for x in range(SIDE)] + [
    [number(y, x, 1) for x in range(SIDE)] for y in range(SIDE)
]


SENDS = [(swap, shift) for swap in (1, 0) for shift in (2, 1, 3, 0)]
SLOT = 16
SPOT = 32


def tables():
    table = np.zeros((N_MEM, SPOT + N_MEM), np.int32)
    for y in range(SIDE):
        for x in range(SIDE):
            for core in range(2):
                row = table[number(y, x, core)]
                for n, (swap, shift) in enumerate(SENDS):
                    to = 1 - core if swap else core
                    row[2 * n] = number(0, x + shift, 0) if to == 0 else number(y + shift, 0, 1)
                    row[2 * n + 1] = 8 if to == 0 else 2
                    row[SLOT + n] = 2 * (((x if core == 0 else y) - shift) % SIDE) + to
                for j in range(N_MEM):
                    row[SPOT + j] = j if core == 0 else 8 * (j // 2 % SIDE) + 2 * (j // 8) + j % 2
    return table


def body(volume, transfer_coef, group_order, member_order, active_mask):
    scale = 3.0 / (SAMPLES * N_GRP * N_MEM)
    rows = jnp.array([0.5, 0.5, 0.5, math.sqrt(scale * math.log2(math.e))], jnp.float32)
    coef = transfer_coef * rows[:, None]
    order = inverse(lax.dynamic_index_in_dim(member_order, lax.axis_index("grp"), 0, False))
    groups = inverse(group_order)
    table = lax.dynamic_index_in_dim(jnp.asarray(tables()), lax.axis_index("mem"), 0, False)

    depths = depth(coef, active_mask, volume.reshape(SAMPLES, ROWS, COLS))
    depths, table = lax.optimization_barrier((depths, table))
    depths = lax.all_to_all(depths.reshape(N_MEM, TILE, COLS), "mem", 0, 0, tiled=True)

    view = volume.reshape(SAMPLES, N_MEM, TILE, COLS)
    colours = []
    for n, (swap, shift) in enumerate(SENDS):
        tiles = march(table, n, coef, active_mask, view)
        if swap or shift:
            tiles = lax.ppermute(tiles, "mem", pairs(swap, shift))
        colours.append(tiles)

    before, total = prefix(order, table, depths)
    before = before.reshape(SIDE, 8, TILE, COLS)
    before = lax.all_to_all(before, "mem", 0, 0, axis_index_groups=LINES, tiled=True)
    parts = weigh(table, colours, before)
    parts = lax.all_to_all(parts, "mem", 0, 0, axis_index_groups=LINES, tiled=True)
    slabs = lax.all_to_all(slab(parts, total), "grp", 0, 0, tiled=True)
    return final(groups, slabs)


def solution(mesh):
    in_specs = (P("grp", "mem", None, None, None), P(), P(), P(), P("grp", "mem"))
    out_specs = P(None, "mem", "grp")
    return jax.shard_map(body, mesh=mesh, in_specs=in_specs, out_specs=out_specs, check_vma=False)
```

```python
import functools
import math

import jax
import jax.numpy as jnp
from jax import lax
from jax.experimental import pallas as pl
from jax.experimental.pallas import tpu as pltpu
from jax.sharding import PartitionSpec as P

SAMPLES = 8
ROWS = 512
COLS = 1024
N_GRP = 4
N_MEM = 32
SIDE = 4
TILE = ROWS // N_MEM
STRIP = COLS // N_GRP
VMEM = 16 << 20
DENSITY = math.sqrt(3.0 / (SAMPLES * N_GRP * N_MEM) * math.log2(math.e))


CALLS = [[(1, 2)], [(1, 1), (1, 3)], [(0, 2), (0, 1)], [(0, 3), (1, 0)], [(0, 0)]]
SENDS = [send for call in CALLS for send in call]

SMEM_SPEC = pl.BlockSpec(memory_space=pltpu.SMEM)
ANY_SPEC = pl.BlockSpec(memory_space=pl.ANY)
VMEM_SPEC = pl.BlockSpec(memory_space=pltpu.VMEM)
HBM_SPEC = pl.BlockSpec(memory_space=pltpu.HBM)


def params():
    return pltpu.CompilerParams(vmem_limit_bytes=VMEM)


def place():
    me = lax.axis_index("mem")
    return me >> 3, (me >> 1) & 3, me & 1


def cubic(q, v):
    return q[0] + v * (q[1] + v * (q[2] + v * q[3]))


def patch(i, width):
    per = COLS // width
    return pl.ds(pl.multiple_of((i // per) * 8, 8), 8), pl.ds(pl.multiple_of((i % per) * width, 128), width)


DEPTH_ROWS = 32
DEPTH_STEPS = ROWS // DEPTH_ROWS
DEPTH_SLOTS = 4


def depth_kernel(coef_ref, flag_ref, vol_ref, *refs):
    out_ref, inbuf, outbuf, insem, outsem = refs[-5:]
    q = [coef_ref[3, k] * DENSITY for k in range(4)]
    flag = flag_ref[0, 0].astype(jnp.float32)
    width = 512

    def fetch(i):
        return pltpu.make_async_copy(
            vol_ref.at[:, pl.ds(i * DEPTH_ROWS, DEPTH_ROWS), :], inbuf.at[i % DEPTH_SLOTS], insem.at[i % DEPTH_SLOTS]
        )

    def store(i):
        return pltpu.make_async_copy(outbuf.at[i % 2], out_ref.at[pl.ds(i * DEPTH_ROWS, DEPTH_ROWS), :], outsem.at[i % 2])

    for i in range(DEPTH_SLOTS):
        fetch(i).start()
    for i in range(DEPTH_STEPS):
        fetch(i).wait()
        if i >= 2:
            store(i - 2).wait()

        def step(n, carry, i=i):
            block, cols = patch(n, width)
            total = None
            for s in range(SAMPLES):
                d = cubic(q, inbuf[i % DEPTH_SLOTS, s, block, cols])
                total = d * d if total is None else total + d * d
            outbuf[i % 2, block, cols] = total * flag
            return carry

        lax.fori_loop(0, (DEPTH_ROWS // 8) * (COLS // width), step, 0, unroll=2)
        store(i).start()
        if i + DEPTH_SLOTS < DEPTH_STEPS:
            fetch(i + DEPTH_SLOTS).start()
    for i in range(DEPTH_STEPS - 2, DEPTH_STEPS):
        store(i).wait()


def depth(coef, flag, volume, after):
    return pl.pallas_call(
        depth_kernel,
        in_specs=[SMEM_SPEC, SMEM_SPEC, HBM_SPEC, ANY_SPEC],
        out_specs=ANY_SPEC,
        out_shape=jax.ShapeDtypeStruct((ROWS, COLS), jnp.float32),
        scratch_shapes=[
            pltpu.VMEM((DEPTH_SLOTS, SAMPLES, DEPTH_ROWS, COLS), jnp.float32),
            pltpu.VMEM((2, DEPTH_ROWS, COLS), jnp.float32),
            pltpu.SemaphoreType.DMA((DEPTH_SLOTS,)),
            pltpu.SemaphoreType.DMA((2,)),
        ],
        compiler_params=params(),
        cost_estimate=pl.CostEstimate(flops=8 * SAMPLES * ROWS * COLS, bytes_accessed=36 * ROWS * COLS, transcendentals=0),
        name="depth",
    )(coef, flag, volume, after)


def march_kernel(coef_ref, flag_ref, vol_ref, *refs, call):
    count = len(call)
    outs, (inbuf, outbuf, insem, outsem) = refs[-4 - count:-4], refs[-4:]
    y, x, core = place()
    q = [[coef_ref[c, k] * (DENSITY if c == 3 else 0.5) for k in range(4)] for c in range(4)]
    half = 0.5 * flag_ref[0, 0].astype(jnp.float32)
    width = 512

    def fetch(i):
        swap, shift = call[i // SIDE]
        to = 1 - core if swap else core
        along_x = 2 * ((x + shift) & 3) + 8 * (i % SIDE)
        along_y = 8 * ((y + shift) & 3) + 2 * (i % SIDE) + 1
        tile = jnp.where(to == 0, along_x, along_y)
        return pltpu.make_async_copy(vol_ref.at[:, tile], inbuf.at[i], insem.at[i])

    def store(i):
        return pltpu.make_async_copy(outbuf.at[i], outs[i // SIDE].at[i % SIDE], outsem.at[i])

    tiles = SIDE * count
    for i in range(tiles):
        fetch(i).start()
    for i in range(tiles):
        fetch(i).wait()

        def step(n, carry, i=i):
            block, cols = patch(n, width)
            depth = clear = None
            acc = [None] * 3
            for s in range(SAMPLES):
                v = inbuf[i, s, block, cols]
                d = cubic(q[3], v)
                depth = -(d * d) if depth is None else depth - d * d
                ahead = jnp.exp2(depth)
                weight = 1.0 - ahead if clear is None else clear - ahead
                clear = ahead
                for ch in range(3):
                    term = weight * jnp.tanh(cubic(q[ch], v))
                    acc[ch] = term if acc[ch] is None else acc[ch] + term
            cover = 1.0 - clear
            for ch in range(3):
                outbuf[i, ch, block, cols] = (acc[ch] + cover) * half
            return carry

        lax.fori_loop(0, (TILE // 8) * (COLS // width), step, 0)
        store(i).start()
    for i in range(tiles):
        store(i).wait()


def march(coef, flag, view, call, after):
    tiles = SIDE * len(call)
    pixels = tiles * TILE * COLS
    return pl.pallas_call(
        functools.partial(march_kernel, call=call),
        in_specs=[SMEM_SPEC, SMEM_SPEC, HBM_SPEC] + [ANY_SPEC] * len(after),
        out_specs=[ANY_SPEC] * len(call),
        out_shape=[jax.ShapeDtypeStruct((SIDE, 3, TILE, COLS), jnp.float32)] * len(call),
        scratch_shapes=[
            pltpu.VMEM((tiles, SAMPLES, TILE, COLS), jnp.float32),
            pltpu.VMEM((tiles, 3, TILE, COLS), jnp.float32),
            pltpu.SemaphoreType.DMA((tiles,)),
            pltpu.SemaphoreType.DMA((tiles,)),
        ],
        compiler_params=params(),
        cost_estimate=pl.CostEstimate(
            flops=40 * SAMPLES * pixels, bytes_accessed=44 * pixels, transcendentals=4 * SAMPLES * pixels
        ),
        name="march",
    )(coef, flag, view, *after)


def prefix_kernel(rank_ref, depth_ref, after_ref, before_ref, total_ref, order_ref):
    grp = lax.axis_index("grp")
    core = lax.axis_index("mem") & 1
    for j in range(N_MEM):
        order_ref[rank_ref[grp, j]] = j

    def strip(i, carry):
        cols = pl.ds(pl.multiple_of(i * STRIP, 128), STRIP)

        def step(r, running):
            j = order_ref[r]
            across = 8 * ((j >> 1) & 3) + 2 * (j >> 3) + (j & 1)
            before_ref[jnp.where(core == 0, j, across), :, cols] = running
            return running + depth_ref[j, :, cols]

        total_ref[:, cols] = lax.fori_loop(0, N_MEM, step, jnp.zeros((TILE, STRIP), jnp.float32), unroll=4)
        return carry

    lax.fori_loop(0, COLS // STRIP, strip, 0)


def prefix(ranks, depths, after):
    return pl.pallas_call(
        prefix_kernel,
        in_specs=[SMEM_SPEC, VMEM_SPEC, ANY_SPEC],
        out_specs=[VMEM_SPEC] * 2,
        out_shape=[
            jax.ShapeDtypeStruct((N_MEM, TILE, COLS), jnp.float32),
            jax.ShapeDtypeStruct((TILE, COLS), jnp.float32),
        ],
        scratch_shapes=[pltpu.SMEM((N_MEM,), jnp.int32)],
        compiler_params=params(),
        cost_estimate=pl.CostEstimate(
            flops=N_MEM * TILE * COLS, bytes_accessed=8 * N_MEM * TILE * COLS, transcendentals=0
        ),
        name="prefix",
    )(ranks, depths, after)


def weigh_kernel(*refs, shifts):
    count = len(shifts)
    colours, before_ref = refs[:8], refs[8]
    outs = refs[9:9 + count]
    colbuf, depbuf, outbuf, colsem, depsem, outsem = refs[9 + count:]
    y, x, core = place()
    first, second = jnp.where(core == 0, x, y), jnp.where(core == 0, y, x)

    def fetch(i):
        spot = (second + shifts[i]) & 3
        return [pltpu.make_async_copy(before_ref.at[spot], depbuf.at[i], depsem.at[i])] + [
            pltpu.make_async_copy(colours[n].at[spot], colbuf.at[i, n], colsem.at[i, n]) for n in range(8)
        ]

    def store(i):
        return pltpu.make_async_copy(outbuf.at[i], outs[i], outsem.at[i])

    slots = [2 * ((first - shift) & 3) + (1 - core if swap else core) for swap, shift in SENDS]
    for i in range(count):
        for copy in fetch(i):
            copy.start()
    for i in range(count):
        for copy in fetch(i):
            copy.wait()

        def step(n, carry, i=i):
            block, cols = patch(n, 256)
            acc = [None] * 3
            for k in range(8):
                light = jnp.exp2(-depbuf[i, slots[k], block, cols])
                for ch in range(3):
                    term = light * colbuf[i, k, ch, block, cols]
                    acc[ch] = term if acc[ch] is None else acc[ch] + term
            for ch in range(3):
                outbuf[i, ch, block, cols] = acc[ch]
            return carry

        lax.fori_loop(0, 8, step, 0)
        store(i).start()
    for i in range(count):
        store(i).wait()


def weigh(colours, before, shifts):
    count = len(shifts)
    return pl.pallas_call(
        functools.partial(weigh_kernel, shifts=shifts),
        in_specs=[ANY_SPEC] * 9,
        out_specs=[ANY_SPEC] * count,
        out_shape=[jax.ShapeDtypeStruct((3, TILE, COLS), jnp.float32)] * count,
        scratch_shapes=[
            pltpu.VMEM((count, 8, 3, TILE, COLS), jnp.float32),
            pltpu.VMEM((count, 8, TILE, COLS), jnp.float32),
            pltpu.VMEM((count, 3, TILE, COLS), jnp.float32),
            pltpu.SemaphoreType.DMA((count, 8)),
            pltpu.SemaphoreType.DMA((count,)),
            pltpu.SemaphoreType.DMA((count,)),
        ],
        compiler_params=params(),
        cost_estimate=pl.CostEstimate(
            flops=56 * count * TILE * COLS, bytes_accessed=140 * count * TILE * COLS, transcendentals=8 * count * TILE * COLS
        ),
        name="weigh",
    )(*colours, before)


def slab_kernel(*refs):
    parts, total_ref, outs = refs[:4], refs[4], refs[5:]
    grp = lax.axis_index("grp")
    for shift in range(N_GRP):
        cols = pl.ds(pl.multiple_of(((grp + shift) & 3) * STRIP, 128), STRIP)
        for ch in range(3):
            outs[shift][ch] = (parts[0][ch, :, cols] + parts[1][ch, :, cols]) + (
                parts[2][ch, :, cols] + parts[3][ch, :, cols]
            )
        outs[shift][3] = 1.0 - jnp.exp2(-total_ref[:, cols])


def slab(parts, total):
    return pl.pallas_call(
        slab_kernel,
        in_specs=[VMEM_SPEC] * 5,
        out_specs=[VMEM_SPEC] * 4,
        out_shape=[jax.ShapeDtypeStruct((4, TILE, STRIP), jnp.float32)] * 4,
        compiler_params=params(),
        name="slab",
    )(*parts, total)


def final_kernel(rank_ref, *refs):
    layers, (out_ref, stack_ref, order_ref) = refs[:4], refs[4:]
    grp = lax.axis_index("grp")
    for j in range(N_GRP):
        order_ref[rank_ref[j]] = j
    for shift in range(N_GRP):
        stack_ref[(grp - shift) & 3] = layers[shift][...]
    pic = [jnp.zeros((TILE, STRIP), jnp.float32)] * 4
    for r in range(N_GRP):
        j = order_ref[r]
        free = 1.0 - pic[3]
        pic = [pic[c] + free * stack_ref[j, c] for c in range(4)]
    for c in range(4):
        out_ref[c] = pic[c]


def final(ranks, layers):
    return pl.pallas_call(
        final_kernel,
        in_specs=[SMEM_SPEC] + [VMEM_SPEC] * 4,
        out_specs=VMEM_SPEC,
        out_shape=jax.ShapeDtypeStruct((4, TILE, STRIP), jnp.float32),
        scratch_shapes=[pltpu.VMEM((N_GRP, 4, TILE, STRIP), jnp.float32), pltpu.SMEM((N_GRP,), jnp.int32)],
        compiler_params=params(),
        name="final",
    )(ranks, *layers)


def number(y, x, core):
    return 8 * (y % SIDE) + 2 * (x % SIDE) + core


def first_pairs(swap, shift):
    out = []
    for y in range(SIDE):
        for x in range(SIDE):
            for core in range(2):
                to = 1 - core if swap else core
                goal = number(y, x + shift, to) if to == 0 else number(y + shift, x, to)
                out.append((number(y, x, core), goal))
    return out


def second_pairs(shift):
    return [
        (number(y, x, core), number(y + shift, x, 0) if core == 0 else number(y, x + shift, 1))
        for y in range(SIDE)
        for x in range(SIDE)
        for core in range(2)
    ]


LINES = [[number(y, x, 0) for y in range(SIDE)] for x in range(SIDE)] + [
    [number(y, x, 1) for x in range(SIDE)] for y in range(SIDE)
]


def body(volume, transfer_coef, group_order, member_order, active_mask):
    view = volume.reshape(SAMPLES, N_MEM, TILE, COLS)
    raw, colours = [], []

    def send(call, after):
        for (swap, shift), tiles in zip(call, march(transfer_coef, active_mask, view, call, after)):
            raw.append(tiles)
            colours.append(lax.ppermute(tiles, "mem", first_pairs(swap, shift)) if swap or shift else tiles)

    send(CALLS[0], [])
    own = depth(transfer_coef, active_mask, volume.reshape(SAMPLES, ROWS, COLS), raw[-1])
    depths = lax.all_to_all(own.reshape(N_MEM, TILE, COLS), "mem", 0, 0, tiled=True)
    send(CALLS[1], [own])
    send(CALLS[2], [raw[-1]])
    send(CALLS[3], [raw[-1]])
    before, total = prefix(member_order, depths, raw[-1])
    before = before.reshape(SIDE, 8, TILE, COLS)
    send(CALLS[4], [total])
    before = lax.all_to_all(before, "mem", 0, 0, axis_index_groups=LINES, tiled=True)

    shifts = (2, 1, 3)
    parts = [lax.ppermute(p, "mem", second_pairs(s)) for s, p in zip(shifts, weigh(colours, before, shifts))]
    parts += weigh(colours, before, (0,))
    layers = slab(parts, total)
    layers = [layers[0]] + [
        lax.ppermute(layers[s], "grp", [(g, (g + s) % N_GRP) for g in range(N_GRP)]) for s in range(1, N_GRP)
    ]
    return final(group_order, layers)


def solution(mesh):
    in_specs = (P("grp", "mem", None, None, None), P(), P(), P(), P("grp", "mem"))
    out_specs = P(None, "mem", "grp")
    return jax.shard_map(body, mesh=mesh, in_specs=in_specs, out_specs=out_specs, check_vma=False)
```

```python
import functools
import math

import jax
import jax.numpy as jnp
from jax import lax
from jax.experimental import pallas as pl
from jax.experimental.pallas import tpu as pltpu
from jax.sharding import PartitionSpec as P

SAMPLES = 8
ROWS = 512
COLS = 1024
N_GRP = 4
N_MEM = 32
SIDE = 4
TILE = ROWS // N_MEM
STRIP = COLS // N_GRP
VMEM = 60 << 20
DENSITY = math.sqrt(3.0 / (SAMPLES * N_GRP * N_MEM) * math.log2(math.e))


CALLS = [[(1, 2)], [(1, 1), (1, 3)], [(0, 2), (0, 1)], [(0, 3), (1, 0)], [(0, 0)]]
SENDS = [send for call in CALLS for send in call]

SMEM_SPEC = pl.BlockSpec(memory_space=pltpu.SMEM)
ANY_SPEC = pl.BlockSpec(memory_space=pl.ANY)
VMEM_SPEC = pl.BlockSpec(memory_space=pltpu.VMEM)
HBM_SPEC = pl.BlockSpec(memory_space=pltpu.HBM)


def params():
    return pltpu.CompilerParams(vmem_limit_bytes=VMEM)


def place():
    me = lax.axis_index("mem")
    return me >> 3, (me >> 1) & 3, me & 1


def cubic(q, v):
    return q[0] + v * (q[1] + v * (q[2] + v * q[3]))


def patch(i, width):
    per = COLS // width
    return pl.ds(pl.multiple_of((i // per) * 8, 8), 8), pl.ds(pl.multiple_of((i % per) * width, 128), width)


DEPTH_ROWS = 32
DEPTH_STEPS = ROWS // DEPTH_ROWS
DEPTH_SLOTS = 4


def depth_kernel(coef_ref, flag_ref, vol_ref, *refs):
    out_ref, inbuf, outbuf, insem, outsem = refs[-5:]
    q = [coef_ref[3, k] * DENSITY for k in range(4)]
    flag = flag_ref[0, 0].astype(jnp.float32)
    width = 512

    def fetch(i):
        return pltpu.make_async_copy(
            vol_ref.at[:, pl.ds(i * DEPTH_ROWS, DEPTH_ROWS), :], inbuf.at[i % DEPTH_SLOTS], insem.at[i % DEPTH_SLOTS]
        )

    def store(i):
        return pltpu.make_async_copy(outbuf.at[i % 2], out_ref.at[pl.ds(i * DEPTH_ROWS, DEPTH_ROWS), :], outsem.at[i % 2])

    for i in range(DEPTH_SLOTS):
        fetch(i).start()
    for i in range(DEPTH_STEPS):
        fetch(i).wait()
        if i >= 2:
            store(i - 2).wait()

        def step(n, carry, i=i):
            block, cols = patch(n, width)
            total = None
            for s in range(SAMPLES):
                d = cubic(q, inbuf[i % DEPTH_SLOTS, s, block, cols])
                total = d * d if total is None else total + d * d
            outbuf[i % 2, block, cols] = total * flag
            return carry

        lax.fori_loop(0, (DEPTH_ROWS // 8) * (COLS // width), step, 0, unroll=2)
        store(i).start()
        if i + DEPTH_SLOTS < DEPTH_STEPS:
            fetch(i + DEPTH_SLOTS).start()
    for i in range(DEPTH_STEPS - 2, DEPTH_STEPS):
        store(i).wait()


def depth(coef, flag, volume, after):
    return pl.pallas_call(
        depth_kernel,
        in_specs=[SMEM_SPEC, SMEM_SPEC, HBM_SPEC, ANY_SPEC],
        out_specs=ANY_SPEC,
        out_shape=jax.ShapeDtypeStruct((ROWS, COLS), jnp.float32),
        scratch_shapes=[
            pltpu.VMEM((DEPTH_SLOTS, SAMPLES, DEPTH_ROWS, COLS), jnp.float32),
            pltpu.VMEM((2, DEPTH_ROWS, COLS), jnp.float32),
            pltpu.SemaphoreType.DMA((DEPTH_SLOTS,)),
            pltpu.SemaphoreType.DMA((2,)),
        ],
        compiler_params=params(),
        cost_estimate=pl.CostEstimate(flops=8 * SAMPLES * ROWS * COLS, bytes_accessed=36 * ROWS * COLS, transcendentals=0),
        name="depth",
    )(coef, flag, volume, after)


def march_kernel(coef_ref, flag_ref, vol_ref, *refs, call):
    count = len(call)
    outs, (inbuf, outbuf, insem, outsem) = refs[-4 - count:-4], refs[-4:]
    y, x, core = place()
    q = [[coef_ref[c, k] * (DENSITY if c == 3 else 0.5) for k in range(4)] for c in range(4)]
    half = 0.5 * flag_ref[0, 0].astype(jnp.float32)
    width = 512

    def fetch(i):
        swap, shift = call[i // SIDE]
        to = 1 - core if swap else core
        along_x = 2 * ((x + shift) & 3) + 8 * (i % SIDE)
        along_y = 8 * ((y + shift) & 3) + 2 * (i % SIDE) + 1
        tile = jnp.where(to == 0, along_x, along_y)
        return pltpu.make_async_copy(vol_ref.at[:, tile], inbuf.at[i], insem.at[i])

    def store(i):
        return pltpu.make_async_copy(outbuf.at[i], outs[i // SIDE].at[i % SIDE], outsem.at[i])

    tiles = SIDE * count
    for i in range(tiles):
        fetch(i).start()
    for i in range(tiles):
        fetch(i).wait()

        def step(n, carry, i=i):
            block, cols = patch(n, width)
            depth = clear = None
            acc = [None] * 3
            for s in range(SAMPLES):
                v = inbuf[i, s, block, cols]
                d = cubic(q[3], v)
                depth = -(d * d) if depth is None else depth - d * d
                ahead = jnp.exp2(depth)
                weight = 1.0 - ahead if clear is None else clear - ahead
                clear = ahead
                for ch in range(3):
                    term = weight * jnp.tanh(cubic(q[ch], v))
                    acc[ch] = term if acc[ch] is None else acc[ch] + term
            cover = 1.0 - clear
            for ch in range(3):
                outbuf[i, ch, block, cols] = (acc[ch] + cover) * half
            return carry

        lax.fori_loop(0, (TILE // 8) * (COLS // width), step, 0)
        store(i).start()
    for i in range(tiles):
        store(i).wait()


def march(coef, flag, view, call, after):
    tiles = SIDE * len(call)
    pixels = tiles * TILE * COLS
    return pl.pallas_call(
        functools.partial(march_kernel, call=call),
        in_specs=[SMEM_SPEC, SMEM_SPEC, HBM_SPEC] + [ANY_SPEC] * len(after),
        out_specs=[ANY_SPEC] * len(call),
        out_shape=[jax.ShapeDtypeStruct((SIDE, 3, TILE, COLS), jnp.float32)] * len(call),
        scratch_shapes=[
            pltpu.VMEM((tiles, SAMPLES, TILE, COLS), jnp.float32),
            pltpu.VMEM((tiles, 3, TILE, COLS), jnp.float32),
            pltpu.SemaphoreType.DMA((tiles,)),
            pltpu.SemaphoreType.DMA((tiles,)),
        ],
        compiler_params=params(),
        cost_estimate=pl.CostEstimate(
            flops=40 * SAMPLES * pixels, bytes_accessed=44 * pixels, transcendentals=4 * SAMPLES * pixels
        ),
        name="march",
    )(coef, flag, view, *after)


def prefix_kernel(rank_ref, depth_ref, after_ref, before_ref, total_ref, order_ref):
    grp = lax.axis_index("grp")
    core = lax.axis_index("mem") & 1
    for j in range(N_MEM):
        order_ref[rank_ref[grp, j]] = j

    def strip(i, carry):
        cols = pl.ds(pl.multiple_of(i * STRIP, 128), STRIP)

        def step(r, running):
            j = order_ref[r]
            across = 8 * ((j >> 1) & 3) + 2 * (j >> 3) + (j & 1)
            before_ref[jnp.where(core == 0, j, across), :, cols] = running
            return running + depth_ref[j, :, cols]

        total_ref[:, cols] = lax.fori_loop(0, N_MEM, step, jnp.zeros((TILE, STRIP), jnp.float32), unroll=4)
        return carry

    lax.fori_loop(0, COLS // STRIP, strip, 0)


def prefix(ranks, depths, after):
    return pl.pallas_call(
        prefix_kernel,
        in_specs=[SMEM_SPEC, VMEM_SPEC, ANY_SPEC],
        out_specs=[VMEM_SPEC] * 2,
        out_shape=[
            jax.ShapeDtypeStruct((N_MEM, TILE, COLS), jnp.float32),
            jax.ShapeDtypeStruct((TILE, COLS), jnp.float32),
        ],
        scratch_shapes=[pltpu.SMEM((N_MEM,), jnp.int32)],
        compiler_params=params(),
        cost_estimate=pl.CostEstimate(
            flops=N_MEM * TILE * COLS, bytes_accessed=8 * N_MEM * TILE * COLS, transcendentals=0
        ),
        name="prefix",
    )(ranks, depths, after)


def weigh_kernel(*refs, shifts):
    count = len(shifts)
    colours, before_ref = refs[:8], refs[8]
    outs = refs[9:9 + count]
    colbuf, depbuf, outbuf, colsem, depsem, outsem = refs[9 + count:]
    y, x, core = place()
    first, second = jnp.where(core == 0, x, y), jnp.where(core == 0, y, x)

    def fetch(i):
        spot = (second + shifts[i]) & 3
        return [pltpu.make_async_copy(before_ref.at[spot], depbuf.at[i], depsem.at[i])] + [
            pltpu.make_async_copy(colours[n].at[spot], colbuf.at[i, n], colsem.at[i, n]) for n in range(8)
        ]

    def store(i):
        return pltpu.make_async_copy(outbuf.at[i], outs[i], outsem.at[i])

    slots = [2 * ((first - shift) & 3) + (1 - core if swap else core) for swap, shift in SENDS]
    for i in range(count):
        for copy in fetch(i):
            copy.start()
    for i in range(count):
        for copy in fetch(i):
            copy.wait()

        def step(n, carry, i=i):
            block, cols = patch(n, 256)
            acc = [None] * 3
            for k in range(8):
                light = jnp.exp2(-depbuf[i, slots[k], block, cols])
                for ch in range(3):
                    term = light * colbuf[i, k, ch, block, cols]
                    acc[ch] = term if acc[ch] is None else acc[ch] + term
            for ch in range(3):
                outbuf[i, ch, block, cols] = acc[ch]
            return carry

        lax.fori_loop(0, 8, step, 0)
        store(i).start()
    for i in range(count):
        store(i).wait()


def weigh(colours, before, shifts):
    count = len(shifts)
    return pl.pallas_call(
        functools.partial(weigh_kernel, shifts=shifts),
        in_specs=[ANY_SPEC] * 9,
        out_specs=[ANY_SPEC] * count,
        out_shape=[jax.ShapeDtypeStruct((3, TILE, COLS), jnp.float32)] * count,
        scratch_shapes=[
            pltpu.VMEM((count, 8, 3, TILE, COLS), jnp.float32),
            pltpu.VMEM((count, 8, TILE, COLS), jnp.float32),
            pltpu.VMEM((count, 3, TILE, COLS), jnp.float32),
            pltpu.SemaphoreType.DMA((count, 8)),
            pltpu.SemaphoreType.DMA((count,)),
            pltpu.SemaphoreType.DMA((count,)),
        ],
        compiler_params=params(),
        cost_estimate=pl.CostEstimate(
            flops=56 * count * TILE * COLS, bytes_accessed=140 * count * TILE * COLS, transcendentals=8 * count * TILE * COLS
        ),
        name="weigh",
    )(*colours, before)


def slab_kernel(*refs):
    parts, total_ref, outs = refs[:4], refs[4], refs[5:]
    grp = lax.axis_index("grp")
    for shift in range(N_GRP):
        cols = pl.ds(pl.multiple_of(((grp + shift) & 3) * STRIP, 128), STRIP)
        for ch in range(3):
            outs[shift][ch] = (parts[0][ch, :, cols] + parts[1][ch, :, cols]) + (
                parts[2][ch, :, cols] + parts[3][ch, :, cols]
            )
        outs[shift][3] = 1.0 - jnp.exp2(-total_ref[:, cols])


def slab(parts, total):
    return pl.pallas_call(
        slab_kernel,
        in_specs=[VMEM_SPEC] * 5,
        out_specs=[VMEM_SPEC] * 4,
        out_shape=[jax.ShapeDtypeStruct((4, TILE, STRIP), jnp.float32)] * 4,
        compiler_params=params(),
        name="slab",
    )(*parts, total)


def final_kernel(rank_ref, *refs):
    layers, (out_ref, stack_ref, order_ref) = refs[:4], refs[4:]
    grp = lax.axis_index("grp")
    for j in range(N_GRP):
        order_ref[rank_ref[j]] = j
    for shift in range(N_GRP):
        stack_ref[(grp - shift) & 3] = layers[shift][...]
    pic = [jnp.zeros((TILE, STRIP), jnp.float32)] * 4
    for r in range(N_GRP):
        j = order_ref[r]
        free = 1.0 - pic[3]
        pic = [pic[c] + free * stack_ref[j, c] for c in range(4)]
    for c in range(4):
        out_ref[c] = pic[c]


def final(ranks, layers):
    return pl.pallas_call(
        final_kernel,
        in_specs=[SMEM_SPEC] + [VMEM_SPEC] * 4,
        out_specs=VMEM_SPEC,
        out_shape=jax.ShapeDtypeStruct((4, TILE, STRIP), jnp.float32),
        scratch_shapes=[pltpu.VMEM((N_GRP, 4, TILE, STRIP), jnp.float32), pltpu.SMEM((N_GRP,), jnp.int32)],
        compiler_params=params(),
        name="final",
    )(ranks, *layers)


def number(y, x, core):
    return 8 * (y % SIDE) + 2 * (x % SIDE) + core


def first_pairs(swap, shift):
    out = []
    for y in range(SIDE):
        for x in range(SIDE):
            for core in range(2):
                to = 1 - core if swap else core
                goal = number(y, x + shift, to) if to == 0 else number(y + shift, x, to)
                out.append((number(y, x, core), goal))
    return out


def second_pairs(shift):
    return [
        (number(y, x, core), number(y + shift, x, 0) if core == 0 else number(y, x + shift, 1))
        for y in range(SIDE)
        for x in range(SIDE)
        for core in range(2)
    ]


LINES = [[number(y, x, 0) for y in range(SIDE)] for x in range(SIDE)] + [
    [number(y, x, 1) for x in range(SIDE)] for y in range(SIDE)
]


def body(volume, transfer_coef, group_order, member_order, active_mask):
    view = volume.reshape(SAMPLES, N_MEM, TILE, COLS)
    raw, colours = [], []

    def send(call, after):
        for (swap, shift), tiles in zip(call, march(transfer_coef, active_mask, view, call, after)):
            raw.append(tiles)
            colours.append(lax.ppermute(tiles, "mem", first_pairs(swap, shift)) if swap or shift else tiles)

    send(CALLS[0], [])
    own = depth(transfer_coef, active_mask, volume.reshape(SAMPLES, ROWS, COLS), raw[-1])
    depths = lax.all_to_all(own.reshape(N_MEM, TILE, COLS), "mem", 0, 0, tiled=True)
    send(CALLS[1], [own])
    send(CALLS[2], [raw[-1]])
    send(CALLS[3], [raw[-1]])
    before, total = prefix(member_order, depths, raw[-1])
    before = before.reshape(SIDE, 8, TILE, COLS)
    send(CALLS[4], [total])
    before = lax.all_to_all(before, "mem", 0, 0, axis_index_groups=LINES, tiled=True)

    shifts = (2, 1, 3)
    parts = [lax.ppermute(p, "mem", second_pairs(s)) for s, p in zip(shifts, weigh(colours, before, shifts))]
    parts += weigh(colours, before, (0,))
    layers = slab(parts, total)
    layers = [layers[0]] + [
        lax.ppermute(layers[s], "grp", [(g, (g + s) % N_GRP) for g in range(N_GRP)]) for s in range(1, N_GRP)
    ]
    return final(group_order, layers)


def solution(mesh):
    in_specs = (P("grp", "mem", None, None, None), P(), P(), P(), P("grp", "mem"))
    out_specs = P(None, "mem", "grp")
    return jax.shard_map(body, mesh=mesh, in_specs=in_specs, out_specs=out_specs, check_vma=False)
```

```python
import functools
import math

import jax
import jax.numpy as jnp
from jax import lax
from jax.experimental import pallas as pl
from jax.experimental.pallas import tpu as pltpu
from jax.sharding import PartitionSpec as P

SAMPLES = 8
ROWS = 512
COLS = 1024
N_GRP = 4
N_MEM = 32
SIDE = 4
TILE = ROWS // N_MEM
STRIP = COLS // N_GRP
VMEM = 60 << 20
SMALL = 24 << 20
DENSITY = math.sqrt(3.0 / (SAMPLES * N_GRP * N_MEM) * math.log2(math.e))


CALLS = [[(1, 2), (1, 1)], [(1, 3), (0, 2)], [(0, 1), (0, 3)], [(1, 0), (0, 0)]]
SENDS = [send for call in CALLS for send in call]

SMEM_SPEC = pl.BlockSpec(memory_space=pltpu.SMEM)
ANY_SPEC = pl.BlockSpec(memory_space=pl.ANY)
VMEM_SPEC = pl.BlockSpec(memory_space=pltpu.VMEM)
HBM_SPEC = pl.BlockSpec(memory_space=pltpu.HBM)


def params(limit=VMEM):
    return pltpu.CompilerParams(vmem_limit_bytes=limit)


def place():
    me = lax.axis_index("mem")
    return me >> 3, (me >> 1) & 3, me & 1


def cubic(q, v):
    return q[0] + v * (q[1] + v * (q[2] + v * q[3]))


def patch(i, width):
    per = COLS // width
    return pl.ds(pl.multiple_of((i // per) * 8, 8), 8), pl.ds(pl.multiple_of((i % per) * width, 128), width)


DEPTH_ROWS = 32
DEPTH_STEPS = ROWS // DEPTH_ROWS
DEPTH_SLOTS = 4


def depth_kernel(coef_ref, flag_ref, vol_ref, *refs):
    out_ref, inbuf, outbuf, insem, outsem = refs[-5:]
    q = [coef_ref[3, k] * DENSITY for k in range(4)]
    flag = flag_ref[0, 0].astype(jnp.float32)
    width = 512

    def fetch(i):
        return pltpu.make_async_copy(
            vol_ref.at[:, pl.ds(i * DEPTH_ROWS, DEPTH_ROWS), :], inbuf.at[i % DEPTH_SLOTS], insem.at[i % DEPTH_SLOTS]
        )

    def store(i):
        return pltpu.make_async_copy(outbuf.at[i % 2], out_ref.at[pl.ds(i * DEPTH_ROWS, DEPTH_ROWS), :], outsem.at[i % 2])

    for i in range(DEPTH_SLOTS):
        fetch(i).start()
    for i in range(DEPTH_STEPS):
        fetch(i).wait()
        if i >= 2:
            store(i - 2).wait()

        def step(n, carry, i=i):
            block, cols = patch(n, width)
            total = None
            for s in range(SAMPLES):
                d = cubic(q, inbuf[i % DEPTH_SLOTS, s, block, cols])
                total = d * d if total is None else total + d * d
            outbuf[i % 2, block, cols] = total * flag
            return carry

        lax.fori_loop(0, (DEPTH_ROWS // 8) * (COLS // width), step, 0, unroll=2)
        store(i).start()
        if i + DEPTH_SLOTS < DEPTH_STEPS:
            fetch(i + DEPTH_SLOTS).start()
    for i in range(DEPTH_STEPS - 2, DEPTH_STEPS):
        store(i).wait()


def depth(coef, flag, volume):
    return pl.pallas_call(
        depth_kernel,
        in_specs=[SMEM_SPEC, SMEM_SPEC, HBM_SPEC],
        out_specs=ANY_SPEC,
        out_shape=jax.ShapeDtypeStruct((ROWS, COLS), jnp.float32),
        scratch_shapes=[
            pltpu.VMEM((DEPTH_SLOTS, SAMPLES, DEPTH_ROWS, COLS), jnp.float32),
            pltpu.VMEM((2, DEPTH_ROWS, COLS), jnp.float32),
            pltpu.SemaphoreType.DMA((DEPTH_SLOTS,)),
            pltpu.SemaphoreType.DMA((2,)),
        ],
        compiler_params=params(),
        cost_estimate=pl.CostEstimate(flops=8 * SAMPLES * ROWS * COLS, bytes_accessed=36 * ROWS * COLS, transcendentals=0),
        name="depth",
    )(coef, flag, volume)


def march_kernel(coef_ref, flag_ref, vol_ref, *refs, call):
    count = len(call)
    outs, (inbuf, outbuf, insem, outsem) = refs[-4 - count:-4], refs[-4:]
    y, x, core = place()
    q = [[coef_ref[c, k] * (DENSITY if c == 3 else 0.5) for k in range(4)] for c in range(4)]
    half = 0.5 * flag_ref[0, 0].astype(jnp.float32)
    width = 512

    def fetch(i):
        swap, shift = call[i // SIDE]
        to = 1 - core if swap else core
        along_x = 2 * ((x + shift) & 3) + 8 * (i % SIDE)
        along_y = 8 * ((y + shift) & 3) + 2 * (i % SIDE) + 1
        tile = jnp.where(to == 0, along_x, along_y)
        return pltpu.make_async_copy(vol_ref.at[:, tile], inbuf.at[i], insem.at[i])

    def store(i):
        return pltpu.make_async_copy(outbuf.at[i], outs[i // SIDE].at[i % SIDE], outsem.at[i])

    tiles = SIDE * count
    for i in range(tiles):
        fetch(i).start()
    for i in range(tiles):
        fetch(i).wait()

        def step(n, carry, i=i):
            block, cols = patch(n, width)
            depth = clear = None
            acc = [None] * 3
            for s in range(SAMPLES):
                v = inbuf[i, s, block, cols]
                d = cubic(q[3], v)
                depth = -(d * d) if depth is None else depth - d * d
                ahead = jnp.exp2(depth)
                weight = 1.0 - ahead if clear is None else clear - ahead
                clear = ahead
                for ch in range(3):
                    term = weight * jnp.tanh(cubic(q[ch], v))
                    acc[ch] = term if acc[ch] is None else acc[ch] + term
            cover = 1.0 - clear
            for ch in range(3):
                outbuf[i, ch, block, cols] = (acc[ch] + cover) * half
            return carry

        lax.fori_loop(0, (TILE // 8) * (COLS // width), step, 0)
        store(i).start()
    for i in range(tiles):
        store(i).wait()


def march(coef, flag, view, call, after):
    tiles = SIDE * len(call)
    pixels = tiles * TILE * COLS
    return pl.pallas_call(
        functools.partial(march_kernel, call=call),
        in_specs=[SMEM_SPEC, SMEM_SPEC, HBM_SPEC] + [ANY_SPEC] * len(after),
        out_specs=[ANY_SPEC] * len(call),
        out_shape=[jax.ShapeDtypeStruct((SIDE, 3, TILE, COLS), jnp.float32)] * len(call),
        scratch_shapes=[
            pltpu.VMEM((tiles, SAMPLES, TILE, COLS), jnp.float32),
            pltpu.VMEM((tiles, 3, TILE, COLS), jnp.float32),
            pltpu.SemaphoreType.DMA((tiles,)),
            pltpu.SemaphoreType.DMA((tiles,)),
        ],
        compiler_params=params(),
        cost_estimate=pl.CostEstimate(
            flops=40 * SAMPLES * pixels, bytes_accessed=44 * pixels, transcendentals=4 * SAMPLES * pixels
        ),
        name="march",
    )(coef, flag, view, *after)


def prefix_kernel(rank_ref, depth_ref, *refs):
    before_ref, total_ref, inbuf, outbuf, order_ref, insem, outsem = refs[-7:]
    grp = lax.axis_index("grp")
    core = lax.axis_index("mem") & 1

    def fetch(i):
        return pltpu.make_async_copy(depth_ref.at[:, pl.ds(8 * i, 8), :], inbuf.at[i], insem.at[i])

    def store(i):
        return pltpu.make_async_copy(outbuf.at[i], before_ref.at[:, pl.ds(8 * i, 8), :], outsem.at[i])

    for i in range(2):
        fetch(i).start()
    for j in range(N_MEM):
        order_ref[rank_ref[grp, j]] = j
    for i in range(2):
        fetch(i).wait()

        def step(r, running, i=i):
            j = order_ref[r]
            across = 8 * ((j >> 1) & 3) + 2 * (j >> 3) + (j & 1)
            outbuf[i, jnp.where(core == 0, j, across)] = running
            return running + inbuf[i, j]

        total = lax.fori_loop(0, N_MEM, step, jnp.zeros((8, COLS), jnp.float32), unroll=2)
        store(i).start()
        total_ref[8 * i:8 * i + 8, :] = total
    for i in range(2):
        store(i).wait()


def prefix(ranks, depths, after):
    return pl.pallas_call(
        prefix_kernel,
        in_specs=[SMEM_SPEC, ANY_SPEC] + [ANY_SPEC] * len(after),
        out_specs=[ANY_SPEC, VMEM_SPEC],
        out_shape=[
            jax.ShapeDtypeStruct((N_MEM, TILE, COLS), jnp.float32),
            jax.ShapeDtypeStruct((TILE, COLS), jnp.float32),
        ],
        scratch_shapes=[
            pltpu.VMEM((2, N_MEM, 8, COLS), jnp.float32),
            pltpu.VMEM((2, N_MEM, 8, COLS), jnp.float32),
            pltpu.SMEM((N_MEM,), jnp.int32),
            pltpu.SemaphoreType.DMA((2,)),
            pltpu.SemaphoreType.DMA((2,)),
        ],
        compiler_params=params(),
        cost_estimate=pl.CostEstimate(
            flops=N_MEM * TILE * COLS, bytes_accessed=8 * N_MEM * TILE * COLS, transcendentals=0
        ),
        name="prefix",
    )(ranks, depths, *after)


def weigh_kernel(*refs, shifts):
    count = len(shifts)
    colours, before_ref = refs[:8], refs[8]
    outs = refs[9:9 + count]
    colbuf, depbuf, outbuf, colsem, depsem, outsem = refs[9 + count:]
    y, x, core = place()
    first, second = jnp.where(core == 0, x, y), jnp.where(core == 0, y, x)

    def fetch(i):
        spot = (second + shifts[i]) & 3
        return [pltpu.make_async_copy(before_ref.at[spot], depbuf.at[i], depsem.at[i])] + [
            pltpu.make_async_copy(colours[n].at[spot], colbuf.at[i, n], colsem.at[i, n]) for n in range(8)
        ]

    def store(i):
        return pltpu.make_async_copy(outbuf.at[i], outs[i], outsem.at[i])

    slots = [2 * ((first - shift) & 3) + (1 - core if swap else core) for swap, shift in SENDS]
    for i in range(count):
        for copy in fetch(i):
            copy.start()
    for i in range(count):
        for copy in fetch(i):
            copy.wait()

        def step(n, carry, i=i):
            block, cols = patch(n, 256)
            acc = [None] * 3
            for k in range(8):
                light = jnp.exp2(-depbuf[i, slots[k], block, cols])
                for ch in range(3):
                    term = light * colbuf[i, k, ch, block, cols]
                    acc[ch] = term if acc[ch] is None else acc[ch] + term
            for ch in range(3):
                outbuf[i, ch, block, cols] = acc[ch]
            return carry

        lax.fori_loop(0, 8, step, 0)
        store(i).start()
    for i in range(count):
        store(i).wait()


def weigh(colours, before, shifts):
    count = len(shifts)
    return pl.pallas_call(
        functools.partial(weigh_kernel, shifts=shifts),
        in_specs=[ANY_SPEC] * 9,
        out_specs=[ANY_SPEC] * count,
        out_shape=[jax.ShapeDtypeStruct((3, TILE, COLS), jnp.float32)] * count,
        scratch_shapes=[
            pltpu.VMEM((count, 8, 3, TILE, COLS), jnp.float32),
            pltpu.VMEM((count, 8, TILE, COLS), jnp.float32),
            pltpu.VMEM((count, 3, TILE, COLS), jnp.float32),
            pltpu.SemaphoreType.DMA((count, 8)),
            pltpu.SemaphoreType.DMA((count,)),
            pltpu.SemaphoreType.DMA((count,)),
        ],
        compiler_params=params(),
        cost_estimate=pl.CostEstimate(
            flops=56 * count * TILE * COLS, bytes_accessed=140 * count * TILE * COLS, transcendentals=8 * count * TILE * COLS
        ),
        name="weigh",
    )(*colours, before)


def slab_kernel(*refs):
    parts, total_ref, outs = refs[:4], refs[4], refs[5:]
    grp = lax.axis_index("grp")
    for shift in range(N_GRP):
        cols = pl.ds(pl.multiple_of(((grp + shift) & 3) * STRIP, 128), STRIP)
        for ch in range(3):
            outs[shift][ch] = (parts[0][ch, :, cols] + parts[1][ch, :, cols]) + (
                parts[2][ch, :, cols] + parts[3][ch, :, cols]
            )
        outs[shift][3] = 1.0 - jnp.exp2(-total_ref[:, cols])


def slab(parts, total):
    return pl.pallas_call(
        slab_kernel,
        in_specs=[VMEM_SPEC] * 5,
        out_specs=[VMEM_SPEC] * 4,
        out_shape=[jax.ShapeDtypeStruct((4, TILE, STRIP), jnp.float32)] * 4,
        compiler_params=params(SMALL),
        name="slab",
    )(*parts, total)


def final_kernel(rank_ref, *refs):
    layers, (out_ref, stack_ref, order_ref) = refs[:4], refs[4:]
    grp = lax.axis_index("grp")
    for j in range(N_GRP):
        order_ref[rank_ref[j]] = j
    for shift in range(N_GRP):
        stack_ref[(grp - shift) & 3] = layers[shift][...]
    pic = [jnp.zeros((TILE, STRIP), jnp.float32)] * 4
    for r in range(N_GRP):
        j = order_ref[r]
        free = 1.0 - pic[3]
        pic = [pic[c] + free * stack_ref[j, c] for c in range(4)]
    for c in range(4):
        out_ref[c] = pic[c]


def final(ranks, layers):
    return pl.pallas_call(
        final_kernel,
        in_specs=[SMEM_SPEC] + [VMEM_SPEC] * 4,
        out_specs=VMEM_SPEC,
        out_shape=jax.ShapeDtypeStruct((4, TILE, STRIP), jnp.float32),
        scratch_shapes=[pltpu.VMEM((N_GRP, 4, TILE, STRIP), jnp.float32), pltpu.SMEM((N_GRP,), jnp.int32)],
        compiler_params=params(SMALL),
        name="final",
    )(ranks, *layers)


def number(y, x, core):
    return 8 * (y % SIDE) + 2 * (x % SIDE) + core


def first_pairs(swap, shift):
    out = []
    for y in range(SIDE):
        for x in range(SIDE):
            for core in range(2):
                to = 1 - core if swap else core
                goal = number(y, x + shift, to) if to == 0 else number(y + shift, x, to)
                out.append((number(y, x, core), goal))
    return out


def second_pairs(shift):
    return [
        (number(y, x, core), number(y + shift, x, 0) if core == 0 else number(y, x + shift, 1))
        for y in range(SIDE)
        for x in range(SIDE)
        for core in range(2)
    ]


LINES = [[number(y, x, 0) for y in range(SIDE)] for x in range(SIDE)] + [
    [number(y, x, 1) for x in range(SIDE)] for y in range(SIDE)
]


def body(volume, transfer_coef, group_order, member_order, active_mask):
    view = volume.reshape(SAMPLES, N_MEM, TILE, COLS)
    raw, colours = [], []

    def send(call, after):
        for (swap, shift), tiles in zip(call, march(transfer_coef, active_mask, view, call, after)):
            raw.append(tiles)
            colours.append(lax.ppermute(tiles, "mem", first_pairs(swap, shift)) if swap or shift else tiles)

    own = depth(transfer_coef, active_mask, volume.reshape(SAMPLES, ROWS, COLS))
    depths = lax.all_to_all(own.reshape(N_MEM, TILE, COLS), "mem", 0, 0, tiled=True)
    send(CALLS[0], [own])
    for call in CALLS[1:]:
        send(call, [raw[-1]])
    before, total = prefix(member_order, depths, [raw[-1]] + colours[:4])
    before = before.reshape(SIDE, 8, TILE, COLS)
    before = lax.all_to_all(before, "mem", 0, 0, axis_index_groups=LINES, tiled=True)

    shifts = (2, 1, 3)
    parts = [lax.ppermute(p, "mem", second_pairs(s)) for s, p in zip(shifts, weigh(colours, before, shifts))]
    parts += weigh(colours, before, (0,))
    layers = slab(parts, total)
    layers = [layers[0]] + [
        lax.ppermute(layers[s], "grp", [(g, (g + s) % N_GRP) for g in range(N_GRP)]) for s in range(1, N_GRP)
    ]
    return final(group_order, layers)


def solution(mesh):
    in_specs = (P("grp", "mem", None, None, None), P(), P(), P(), P("grp", "mem"))
    out_specs = P(None, "mem", "grp")
    return jax.shard_map(body, mesh=mesh, in_specs=in_specs, out_specs=out_specs, check_vma=False)
```

```python
import functools
import math

import jax
import jax.numpy as jnp
from jax import lax
from jax.experimental import pallas as pl
from jax.experimental.pallas import tpu as pltpu
from jax.sharding import PartitionSpec as P

SAMPLES = 8
ROWS = 512
COLS = 1024
N_GRP = 4
N_MEM = 32
SIDE = 4
TILE = ROWS // N_MEM
STRIP = COLS // N_GRP
VMEM = 60 << 20
SMALL = 24 << 20
PREFIX = 50 << 20
DENSITY = math.sqrt(3.0 / (SAMPLES * N_GRP * N_MEM) * math.log2(math.e))


CALLS = [[(1, 2), (0, 2)], [(1, 1), (1, 3)], [(0, 1), (0, 3)], [(1, 0), (0, 0)]]
SENDS = [send for call in CALLS for send in call]

SMEM_SPEC = pl.BlockSpec(memory_space=pltpu.SMEM)
ANY_SPEC = pl.BlockSpec(memory_space=pl.ANY)
VMEM_SPEC = pl.BlockSpec(memory_space=pltpu.VMEM)
HBM_SPEC = pl.BlockSpec(memory_space=pltpu.HBM)


def params(limit=VMEM):
    return pltpu.CompilerParams(vmem_limit_bytes=limit)


def place():
    me = lax.axis_index("mem")
    return me >> 3, (me >> 1) & 3, me & 1


def cubic(q, v):
    return q[0] + v * (q[1] + v * (q[2] + v * q[3]))


def patch(i, width):
    per = COLS // width
    return pl.ds(pl.multiple_of((i // per) * 8, 8), 8), pl.ds(pl.multiple_of((i % per) * width, 128), width)


DEPTH_ROWS = 64
DEPTH_STEPS = ROWS // DEPTH_ROWS
DEPTH_SLOTS = 4


def depth_kernel(coef_ref, flag_ref, vol_ref, *refs):
    out_ref, inbuf, outbuf, insem, outsem = refs[-5:]
    q = [coef_ref[3, k] * DENSITY for k in range(4)]
    flag = flag_ref[0, 0].astype(jnp.float32)
    width = 512

    def fetch(i):
        return pltpu.make_async_copy(
            vol_ref.at[:, pl.ds(i * DEPTH_ROWS, DEPTH_ROWS), :], inbuf.at[i % DEPTH_SLOTS], insem.at[i % DEPTH_SLOTS]
        )

    def store(i):
        return pltpu.make_async_copy(outbuf.at[i % 2], out_ref.at[pl.ds(i * DEPTH_ROWS, DEPTH_ROWS), :], outsem.at[i % 2])

    for i in range(DEPTH_SLOTS):
        fetch(i).start()
    for i in range(DEPTH_STEPS):
        fetch(i).wait()
        if i >= 2:
            store(i - 2).wait()

        def step(n, carry, i=i):
            block, cols = patch(n, width)
            total = None
            for s in range(SAMPLES):
                d = cubic(q, inbuf[i % DEPTH_SLOTS, s, block, cols])
                total = d * d if total is None else total + d * d
            outbuf[i % 2, block, cols] = total * flag
            return carry

        lax.fori_loop(0, (DEPTH_ROWS // 8) * (COLS // width), step, 0, unroll=4)
        store(i).start()
        if i + DEPTH_SLOTS < DEPTH_STEPS:
            fetch(i + DEPTH_SLOTS).start()
    for i in range(DEPTH_STEPS - 2, DEPTH_STEPS):
        store(i).wait()


def depth(coef, flag, volume):
    return pl.pallas_call(
        depth_kernel,
        in_specs=[SMEM_SPEC, SMEM_SPEC, HBM_SPEC],
        out_specs=ANY_SPEC,
        out_shape=jax.ShapeDtypeStruct((ROWS, COLS), jnp.float32),
        scratch_shapes=[
            pltpu.VMEM((DEPTH_SLOTS, SAMPLES, DEPTH_ROWS, COLS), jnp.float32),
            pltpu.VMEM((2, DEPTH_ROWS, COLS), jnp.float32),
            pltpu.SemaphoreType.DMA((DEPTH_SLOTS,)),
            pltpu.SemaphoreType.DMA((2,)),
        ],
        compiler_params=params(),
        cost_estimate=pl.CostEstimate(flops=8 * SAMPLES * ROWS * COLS, bytes_accessed=36 * ROWS * COLS, transcendentals=0),
        name="depth",
    )(coef, flag, volume)


def march_kernel(coef_ref, flag_ref, vol_ref, *refs, call):
    count = len(call)
    outs, (inbuf, outbuf, insem, outsem) = refs[-4 - count:-4], refs[-4:]
    y, x, core = place()
    q = [[coef_ref[c, k] * (DENSITY if c == 3 else 0.5) for k in range(4)] for c in range(4)]
    half = 0.5 * flag_ref[0, 0].astype(jnp.float32)

    def fetch(k, i):
        swap, shift = call[k]
        to = 1 - core if swap else core
        along_x = 2 * ((x + shift) & 3) + 8 * i
        along_y = 8 * ((y + shift) & 3) + 2 * i + 1
        tile = jnp.where(to == 0, along_x, along_y)
        return pltpu.make_async_copy(vol_ref.at[:, tile], inbuf.at[k, i], insem.at[k, i])

    def store(k, i):
        return pltpu.make_async_copy(outbuf.at[k, i], outs[k].at[i], outsem.at[k, i])

    every = [(k, i) for k in range(count) for i in range(SIDE)]
    for k, i in every:
        fetch(k, i).start()
    for k in range(count):

        def tile_step(i, carry, k=k):
            fetch(k, i).wait()

            def step(n, carry):
                block = pl.ds(pl.multiple_of(n * 8, 8), 8)
                depth = clear = None
                acc = [None] * 3
                for s in range(SAMPLES):
                    v = inbuf[k, i, s, block, :]
                    d = cubic(q[3], v)
                    depth = -(d * d) if depth is None else depth - d * d
                    ahead = jnp.exp2(depth)
                    weight = 1.0 - ahead if clear is None else clear - ahead
                    clear = ahead
                    for ch in range(3):
                        term = weight * jnp.tanh(cubic(q[ch], v))
                        acc[ch] = term if acc[ch] is None else acc[ch] + term
                cover = 1.0 - clear
                for ch in range(3):
                    outbuf[k, i, ch, block, :] = (acc[ch] + cover) * half
                return carry

            lax.fori_loop(0, TILE // 8, step, 0)
            store(k, i).start()
            return carry

        lax.fori_loop(0, SIDE, tile_step, 0)
    for k, i in every:
        store(k, i).wait()


def march(coef, flag, view, call, after):
    tiles = SIDE * len(call)
    pixels = tiles * TILE * COLS
    return pl.pallas_call(
        functools.partial(march_kernel, call=call),
        in_specs=[SMEM_SPEC, SMEM_SPEC, HBM_SPEC] + [ANY_SPEC] * len(after),
        out_specs=[ANY_SPEC] * len(call),
        out_shape=[jax.ShapeDtypeStruct((SIDE, 3, TILE, COLS), jnp.float32)] * len(call),
        scratch_shapes=[
            pltpu.VMEM((len(call), SIDE, SAMPLES, TILE, COLS), jnp.float32),
            pltpu.VMEM((len(call), SIDE, 3, TILE, COLS), jnp.float32),
            pltpu.SemaphoreType.DMA((len(call), SIDE)),
            pltpu.SemaphoreType.DMA((len(call), SIDE)),
        ],
        compiler_params=params(),
        cost_estimate=pl.CostEstimate(
            flops=40 * SAMPLES * pixels, bytes_accessed=44 * pixels, transcendentals=4 * SAMPLES * pixels
        ),
        name="march",
    )(coef, flag, view, *after)


def prefix_kernel(rank_ref, depth_ref, *refs):
    outs, (total_ref, buf, order_ref, sem) = refs[-8:-4], refs[-4:]
    grp = lax.axis_index("grp")
    y, x, core = place()
    second = jnp.where(core == 0, y, x)
    for j in range(N_MEM):
        order_ref[rank_ref[grp, j]] = j

    def strip(i, carry):
        cols = pl.ds(pl.multiple_of(i * STRIP, 128), STRIP)

        def step(r, running):
            j = order_ref[r]
            across = 8 * ((j >> 1) & 3) + 2 * (j >> 3) + (j & 1)
            spot = jnp.where(core == 0, j, across)
            buf[spot >> 3, spot & 7, :, cols] = running
            return running + depth_ref[j, :, cols]

        total_ref[:, cols] = lax.fori_loop(0, N_MEM, step, jnp.zeros((TILE, STRIP), jnp.float32), unroll=4)
        return carry

    lax.fori_loop(0, COLS // STRIP, strip, 0)
    copies = [pltpu.make_async_copy(buf.at[(second + k) & 3], outs[k], sem.at[k]) for k in range(SIDE)]
    for copy in copies:
        copy.start()
    for copy in copies:
        copy.wait()


def prefix(ranks, depths, after):
    line = jax.ShapeDtypeStruct((8, TILE, COLS), jnp.float32)
    return pl.pallas_call(
        prefix_kernel,
        in_specs=[SMEM_SPEC, VMEM_SPEC] + [ANY_SPEC] * len(after),
        out_specs=[ANY_SPEC] * SIDE + [VMEM_SPEC],
        out_shape=[line] * SIDE + [jax.ShapeDtypeStruct((TILE, COLS), jnp.float32)],
        scratch_shapes=[
            pltpu.VMEM((SIDE, 8, TILE, COLS), jnp.float32),
            pltpu.SMEM((N_MEM,), jnp.int32),
            pltpu.SemaphoreType.DMA((SIDE,)),
        ],
        compiler_params=params(PREFIX),
        cost_estimate=pl.CostEstimate(
            flops=N_MEM * TILE * COLS, bytes_accessed=8 * N_MEM * TILE * COLS, transcendentals=0
        ),
        name="prefix",
    )(ranks, depths, *after)


def weigh_kernel(*refs, shifts):
    count = len(shifts)
    colours, befores, outs = refs[:8], refs[8:8 + count], refs[8 + count:8 + 2 * count]
    colbuf, depbuf, outbuf, colsem, depsem, outsem = refs[8 + 2 * count:]
    y, x, core = place()
    first, second = jnp.where(core == 0, x, y), jnp.where(core == 0, y, x)

    def fetch(i):
        spot = (second + shifts[i]) & 3
        return [pltpu.make_async_copy(befores[i], depbuf.at[i], depsem.at[i])] + [
            pltpu.make_async_copy(colours[n].at[spot], colbuf.at[i, n], colsem.at[i, n]) for n in range(8)
        ]

    def store(i):
        return pltpu.make_async_copy(outbuf.at[i], outs[i], outsem.at[i])

    slots = [2 * ((first - shift) & 3) + (1 - core if swap else core) for swap, shift in SENDS]
    for i in range(count):
        for copy in fetch(i):
            copy.start()
    for i in range(count):
        for copy in fetch(i):
            copy.wait()

        def step(n, carry, i=i):
            block, cols = patch(n, 256)
            acc = [None] * 3
            for k in range(8):
                light = jnp.exp2(-depbuf[i, slots[k], block, cols])
                for ch in range(3):
                    term = light * colbuf[i, k, ch, block, cols]
                    acc[ch] = term if acc[ch] is None else acc[ch] + term
            for ch in range(3):
                outbuf[i, ch, block, cols] = acc[ch]
            return carry

        lax.fori_loop(0, 8, step, 0)
        store(i).start()
    for i in range(count):
        store(i).wait()


def weigh(colours, befores, shifts):
    count = len(shifts)
    return pl.pallas_call(
        functools.partial(weigh_kernel, shifts=shifts),
        in_specs=[ANY_SPEC] * (8 + count),
        out_specs=[ANY_SPEC] * count,
        out_shape=[jax.ShapeDtypeStruct((3, TILE, COLS), jnp.float32)] * count,
        scratch_shapes=[
            pltpu.VMEM((count, 8, 3, TILE, COLS), jnp.float32),
            pltpu.VMEM((count, 8, TILE, COLS), jnp.float32),
            pltpu.VMEM((count, 3, TILE, COLS), jnp.float32),
            pltpu.SemaphoreType.DMA((count, 8)),
            pltpu.SemaphoreType.DMA((count,)),
            pltpu.SemaphoreType.DMA((count,)),
        ],
        compiler_params=params(),
        cost_estimate=pl.CostEstimate(
            flops=56 * count * TILE * COLS, bytes_accessed=140 * count * TILE * COLS, transcendentals=8 * count * TILE * COLS
        ),
        name="weigh",
    )(*colours, *[befores[-shift % SIDE] for shift in shifts])


def slab_kernel(*refs):
    parts, total_ref, outs = refs[:4], refs[4], refs[5:]
    grp = lax.axis_index("grp")
    for shift in range(N_GRP):
        cols = pl.ds(pl.multiple_of(((grp + shift) & 3) * STRIP, 128), STRIP)
        for ch in range(3):
            outs[shift][ch] = (parts[0][ch, :, cols] + parts[1][ch, :, cols]) + (
                parts[2][ch, :, cols] + parts[3][ch, :, cols]
            )
        outs[shift][3] = 1.0 - jnp.exp2(-total_ref[:, cols])


def slab(parts, total):
    return pl.pallas_call(
        slab_kernel,
        in_specs=[VMEM_SPEC] * 5,
        out_specs=[VMEM_SPEC] * 4,
        out_shape=[jax.ShapeDtypeStruct((4, TILE, STRIP), jnp.float32)] * 4,
        compiler_params=params(SMALL),
        name="slab",
    )(*parts, total)


def final_kernel(rank_ref, *refs):
    layers, (out_ref, stack_ref, order_ref) = refs[:4], refs[4:]
    grp = lax.axis_index("grp")
    for j in range(N_GRP):
        order_ref[rank_ref[j]] = j
    for shift in range(N_GRP):
        stack_ref[(grp - shift) & 3] = layers[shift][...]
    pic = [jnp.zeros((TILE, STRIP), jnp.float32)] * 4
    for r in range(N_GRP):
        j = order_ref[r]
        free = 1.0 - pic[3]
        pic = [pic[c] + free * stack_ref[j, c] for c in range(4)]
    for c in range(4):
        out_ref[c] = pic[c]


def final(ranks, layers):
    return pl.pallas_call(
        final_kernel,
        in_specs=[SMEM_SPEC] + [VMEM_SPEC] * 4,
        out_specs=VMEM_SPEC,
        out_shape=jax.ShapeDtypeStruct((4, TILE, STRIP), jnp.float32),
        scratch_shapes=[pltpu.VMEM((N_GRP, 4, TILE, STRIP), jnp.float32), pltpu.SMEM((N_GRP,), jnp.int32)],
        compiler_params=params(SMALL),
        name="final",
    )(ranks, *layers)


def number(y, x, core):
    return 8 * (y % SIDE) + 2 * (x % SIDE) + core


def first_pairs(swap, shift):
    out = []
    for y in range(SIDE):
        for x in range(SIDE):
            for core in range(2):
                to = 1 - core if swap else core
                goal = number(y, x + shift, to) if to == 0 else number(y + shift, x, to)
                out.append((number(y, x, core), goal))
    return out


def second_pairs(shift):
    return [
        (number(y, x, core), number(y + shift, x, 0) if core == 0 else number(y, x + shift, 1))
        for y in range(SIDE)
        for x in range(SIDE)
        for core in range(2)
    ]


def body(volume, transfer_coef, group_order, member_order, active_mask):
    view = volume.reshape(SAMPLES, N_MEM, TILE, COLS)
    raw, colours = [], []

    def send(call, after):
        for (swap, shift), tiles in zip(call, march(transfer_coef, active_mask, view, call, after)):
            raw.append(tiles)
            colours.append(lax.ppermute(tiles, "mem", first_pairs(swap, shift)) if swap or shift else tiles)

    own = depth(transfer_coef, active_mask, volume.reshape(SAMPLES, ROWS, COLS))
    depths = lax.all_to_all(own.reshape(N_MEM, TILE, COLS), "mem", 0, 0, tiled=True)
    send(CALLS[0], [own])
    for call in CALLS[1:]:
        send(call, [raw[-1]])
    *befores, total = prefix(member_order, depths, [raw[-1]] + colours[:4])
    befores = [befores[0]] + [lax.ppermute(befores[k], "mem", second_pairs(k)) for k in range(1, SIDE)]

    shifts = (2, 1, 3)
    parts = [lax.ppermute(p, "mem", second_pairs(k)) for k, p in zip(shifts, weigh(colours, befores, shifts))]
    parts += weigh(colours, befores, (0,))
    layers = slab(parts, total)
    layers = [layers[0]] + [
        lax.ppermute(layers[s], "grp", [(g, (g + s) % N_GRP) for g in range(N_GRP)]) for s in range(1, N_GRP)
    ]
    return final(group_order, layers)


def solution(mesh):
    in_specs = (P("grp", "mem", None, None, None), P(), P(), P(), P("grp", "mem"))
    out_specs = P(None, "mem", "grp")
    return jax.shard_map(body, mesh=mesh, in_specs=in_specs, out_specs=out_specs, check_vma=False)
```

```python
import functools
import math

import jax
import jax.numpy as jnp
from jax import lax
from jax.experimental import pallas as pl
from jax.experimental.pallas import tpu as pltpu
from jax.sharding import PartitionSpec as P

SAMPLES = 8
ROWS = 512
COLS = 1024
N_GRP = 4
N_MEM = 32
SIDE = 4
TILE = ROWS // N_MEM
STRIP = COLS // N_GRP
VMEM = 60 << 20
SMALL = 24 << 20
PREFIX = 50 << 20
DENSITY = math.sqrt(3.0 / (SAMPLES * N_GRP * N_MEM) * math.log2(math.e))


CALLS = [[(1, 2), (0, 2)], [(1, 1), (1, 3)], [(0, 1), (0, 3)], [(1, 0), (0, 0)]]
SENDS = [send for call in CALLS for send in call]

SMEM_SPEC = pl.BlockSpec(memory_space=pltpu.SMEM)
ANY_SPEC = pl.BlockSpec(memory_space=pl.ANY)
VMEM_SPEC = pl.BlockSpec(memory_space=pltpu.VMEM)
HBM_SPEC = pl.BlockSpec(memory_space=pltpu.HBM)


def params(limit=VMEM):
    return pltpu.CompilerParams(vmem_limit_bytes=limit)


def place():
    me = lax.axis_index("mem")
    return me >> 3, (me >> 1) & 3, me & 1


def cubic(q, v):
    return q[0] + v * (q[1] + v * (q[2] + v * q[3]))


def patch(i, width):
    per = COLS // width
    return pl.ds(pl.multiple_of((i // per) * 8, 8), 8), pl.ds(pl.multiple_of((i % per) * width, 128), width)


DEPTH_ROWS = 64
DEPTH_STEPS = ROWS // DEPTH_ROWS
DEPTH_SLOTS = 4


def depth_kernel(coef_ref, flag_ref, vol_ref, *refs):
    out_ref, inbuf, outbuf, insem, outsem = refs[-5:]
    q = [coef_ref[3, k] * DENSITY for k in range(4)]
    flag = flag_ref[0, 0].astype(jnp.float32)
    width = 512

    def fetch(i):
        return pltpu.make_async_copy(
            vol_ref.at[:, pl.ds(i * DEPTH_ROWS, DEPTH_ROWS), :], inbuf.at[i % DEPTH_SLOTS], insem.at[i % DEPTH_SLOTS]
        )

    def store(i):
        return pltpu.make_async_copy(outbuf.at[i % 2], out_ref.at[pl.ds(i * DEPTH_ROWS, DEPTH_ROWS), :], outsem.at[i % 2])

    for i in range(DEPTH_SLOTS):
        fetch(i).start()
    for i in range(DEPTH_STEPS):
        fetch(i).wait()
        if i >= 2:
            store(i - 2).wait()

        def step(n, carry, i=i):
            block, cols = patch(n, width)
            total = None
            for s in range(SAMPLES):
                d = cubic(q, inbuf[i % DEPTH_SLOTS, s, block, cols])
                total = d * d if total is None else total + d * d
            outbuf[i % 2, block, cols] = total * flag
            return carry

        lax.fori_loop(0, (DEPTH_ROWS // 8) * (COLS // width), step, 0, unroll=4)
        store(i).start()
        if i + DEPTH_SLOTS < DEPTH_STEPS:
            fetch(i + DEPTH_SLOTS).start()
    for i in range(DEPTH_STEPS - 2, DEPTH_STEPS):
        store(i).wait()


def depth(coef, flag, volume):
    return pl.pallas_call(
        depth_kernel,
        in_specs=[SMEM_SPEC, SMEM_SPEC, HBM_SPEC],
        out_specs=ANY_SPEC,
        out_shape=jax.ShapeDtypeStruct((ROWS, COLS), jnp.float32),
        scratch_shapes=[
            pltpu.VMEM((DEPTH_SLOTS, SAMPLES, DEPTH_ROWS, COLS), jnp.float32),
            pltpu.VMEM((2, DEPTH_ROWS, COLS), jnp.float32),
            pltpu.SemaphoreType.DMA((DEPTH_SLOTS,)),
            pltpu.SemaphoreType.DMA((2,)),
        ],
        compiler_params=params(),
        cost_estimate=pl.CostEstimate(flops=8 * SAMPLES * ROWS * COLS, bytes_accessed=36 * ROWS * COLS, transcendentals=0),
        name="depth",
    )(coef, flag, volume)


def march_kernel(coef_ref, flag_ref, vol_ref, *refs, call):
    count = len(call)
    outs, (inbuf, outbuf, insem, outsem) = refs[-4 - count:-4], refs[-4:]
    y, x, core = place()
    q = [[coef_ref[c, k] * (DENSITY if c == 3 else 0.5) for k in range(4)] for c in range(4)]
    half = 0.5 * flag_ref[0, 0].astype(jnp.float32)

    def fetch(k, i):
        swap, shift = call[k]
        to = 1 - core if swap else core
        along_x = 2 * ((x + shift) & 3) + 8 * i
        along_y = 8 * ((y + shift) & 3) + 2 * i + 1
        tile = jnp.where(to == 0, along_x, along_y)
        return pltpu.make_async_copy(vol_ref.at[:, tile], inbuf.at[k, i], insem.at[k, i])

    def store(k, i):
        return pltpu.make_async_copy(outbuf.at[k, i], outs[k].at[i], outsem.at[k, i])

    every = [(k, i) for k in range(count) for i in range(SIDE)]
    for k, i in every:
        fetch(k, i).start()
    for k in range(count):

        def tile_step(i, carry, k=k):
            fetch(k, i).wait()

            def step(n, carry):
                block = pl.ds(pl.multiple_of(n * 8, 8), 8)
                depth = clear = None
                acc = [None] * 3
                for s in range(SAMPLES):
                    v = inbuf[k, i, s, block, :]
                    d = cubic(q[3], v)
                    depth = -(d * d) if depth is None else depth - d * d
                    ahead = jnp.exp2(depth)
                    weight = 1.0 - ahead if clear is None else clear - ahead
                    clear = ahead
                    for ch in range(3):
                        term = weight * jnp.tanh(cubic(q[ch], v))
                        acc[ch] = term if acc[ch] is None else acc[ch] + term
                cover = 1.0 - clear
                for ch in range(3):
                    outbuf[k, i, ch, block, :] = (acc[ch] + cover) * half
                return carry

            lax.fori_loop(0, TILE // 8, step, 0)
            store(k, i).start()
            return carry

        lax.fori_loop(0, SIDE, tile_step, 0)
    for k, i in every:
        store(k, i).wait()


def march(coef, flag, view, call, after):
    tiles = SIDE * len(call)
    pixels = tiles * TILE * COLS
    return pl.pallas_call(
        functools.partial(march_kernel, call=call),
        in_specs=[SMEM_SPEC, SMEM_SPEC, HBM_SPEC] + [ANY_SPEC] * len(after),
        out_specs=[ANY_SPEC] * len(call),
        out_shape=[jax.ShapeDtypeStruct((SIDE, 3, TILE, COLS), jnp.float32)] * len(call),
        scratch_shapes=[
            pltpu.VMEM((len(call), SIDE, SAMPLES, TILE, COLS), jnp.float32),
            pltpu.VMEM((len(call), SIDE, 3, TILE, COLS), jnp.float32),
            pltpu.SemaphoreType.DMA((len(call), SIDE)),
            pltpu.SemaphoreType.DMA((len(call), SIDE)),
        ],
        compiler_params=params(),
        cost_estimate=pl.CostEstimate(
            flops=40 * SAMPLES * pixels, bytes_accessed=44 * pixels, transcendentals=4 * SAMPLES * pixels
        ),
        name="march",
    )(coef, flag, view, *after)


def prefix_kernel(rank_ref, depth_ref, *refs):
    outs, (total_ref, buf, order_ref, sem) = refs[-8:-4], refs[-4:]
    grp = lax.axis_index("grp")
    y, x, core = place()
    second = jnp.where(core == 0, y, x)
    for j in range(N_MEM):
        order_ref[rank_ref[grp, j]] = j

    def strip(i, carry):
        cols = pl.ds(pl.multiple_of(i * STRIP, 128), STRIP)

        def step(r, running):
            j = order_ref[r]
            across = 8 * ((j >> 1) & 3) + 2 * (j >> 3) + (j & 1)
            spot = jnp.where(core == 0, j, across)
            buf[spot >> 3, spot & 7, :, cols] = running
            return running + depth_ref[j, :, cols]

        total_ref[:, cols] = lax.fori_loop(0, N_MEM, step, jnp.zeros((TILE, STRIP), jnp.float32), unroll=4)
        return carry

    lax.fori_loop(0, COLS // STRIP, strip, 0)
    copies = [pltpu.make_async_copy(buf.at[(second + k) & 3], outs[k], sem.at[k]) for k in range(SIDE)]
    for copy in copies:
        copy.start()
    for copy in copies:
        copy.wait()


def prefix(ranks, depths, after):
    line = jax.ShapeDtypeStruct((8, TILE, COLS), jnp.float32)
    return pl.pallas_call(
        prefix_kernel,
        in_specs=[SMEM_SPEC, VMEM_SPEC] + [ANY_SPEC] * len(after),
        out_specs=[ANY_SPEC] * SIDE + [VMEM_SPEC],
        out_shape=[line] * SIDE + [jax.ShapeDtypeStruct((TILE, COLS), jnp.float32)],
        scratch_shapes=[
            pltpu.VMEM((SIDE, 8, TILE, COLS), jnp.float32),
            pltpu.SMEM((N_MEM,), jnp.int32),
            pltpu.SemaphoreType.DMA((SIDE,)),
        ],
        compiler_params=params(PREFIX),
        cost_estimate=pl.CostEstimate(
            flops=N_MEM * TILE * COLS, bytes_accessed=8 * N_MEM * TILE * COLS, transcendentals=0
        ),
        name="prefix",
    )(ranks, depths, *after)


def weigh_kernel(*refs, shifts):
    count = len(shifts)
    colours, befores, outs = refs[:8], refs[8:8 + count], refs[8 + count:8 + 2 * count]
    colbuf, depbuf, outbuf, colsem, depsem, outsem = refs[8 + 2 * count:]
    y, x, core = place()
    first, second = jnp.where(core == 0, x, y), jnp.where(core == 0, y, x)

    def fetch(i):
        spot = (second + shifts[i]) & 3
        return [pltpu.make_async_copy(befores[i], depbuf.at[i], depsem.at[i])] + [
            pltpu.make_async_copy(colours[n].at[spot], colbuf.at[i, n], colsem.at[i, n]) for n in range(8)
        ]

    def store(i):
        return pltpu.make_async_copy(outbuf.at[i], outs[i], outsem.at[i])

    slots = [2 * ((first - shift) & 3) + (1 - core if swap else core) for swap, shift in SENDS]
    for i in range(count):
        for copy in fetch(i):
            copy.start()
    for i in range(count):
        for copy in fetch(i):
            copy.wait()

        def step(n, carry, i=i):
            block, cols = patch(n, 256)
            acc = [None] * 3
            for k in range(8):
                light = jnp.exp2(-depbuf[i, slots[k], block, cols])
                for ch in range(3):
                    term = light * colbuf[i, k, ch, block, cols]
                    acc[ch] = term if acc[ch] is None else acc[ch] + term
            for ch in range(3):
                outbuf[i, ch, block, cols] = acc[ch]
            return carry

        lax.fori_loop(0, 8, step, 0)
        store(i).start()
    for i in range(count):
        store(i).wait()


def weigh(colours, befores, shifts):
    count = len(shifts)
    return pl.pallas_call(
        functools.partial(weigh_kernel, shifts=shifts),
        in_specs=[ANY_SPEC] * (8 + count),
        out_specs=[ANY_SPEC] * count,
        out_shape=[jax.ShapeDtypeStruct((3, TILE, COLS), jnp.float32)] * count,
        scratch_shapes=[
            pltpu.VMEM((count, 8, 3, TILE, COLS), jnp.float32),
            pltpu.VMEM((count, 8, TILE, COLS), jnp.float32),
            pltpu.VMEM((count, 3, TILE, COLS), jnp.float32),
            pltpu.SemaphoreType.DMA((count, 8)),
            pltpu.SemaphoreType.DMA((count,)),
            pltpu.SemaphoreType.DMA((count,)),
        ],
        compiler_params=params(),
        cost_estimate=pl.CostEstimate(
            flops=56 * count * TILE * COLS, bytes_accessed=140 * count * TILE * COLS, transcendentals=8 * count * TILE * COLS
        ),
        name="weigh",
    )(*colours, *[befores[-shift % SIDE] for shift in shifts])


def slab_kernel(*refs):
    parts, total_ref, outs = refs[:4], refs[4], refs[5:]
    grp = lax.axis_index("grp")
    for shift in range(N_GRP):
        cols = pl.ds(pl.multiple_of(((grp + shift) & 3) * STRIP, 128), STRIP)
        for ch in range(3):
            outs[shift][ch] = (parts[0][ch, :, cols] + parts[1][ch, :, cols]) + (
                parts[2][ch, :, cols] + parts[3][ch, :, cols]
            )
        outs[shift][3] = 1.0 - jnp.exp2(-total_ref[:, cols])


def slab(parts, total):
    return pl.pallas_call(
        slab_kernel,
        in_specs=[VMEM_SPEC] * 5,
        out_specs=[VMEM_SPEC] * 4,
        out_shape=[jax.ShapeDtypeStruct((4, TILE, STRIP), jnp.float32)] * 4,
        compiler_params=params(SMALL),
        name="slab",
    )(*parts, total)


def final_kernel(rank_ref, *refs):
    layers, (out_ref, stack_ref, order_ref) = refs[:4], refs[4:]
    grp = lax.axis_index("grp")
    for j in range(N_GRP):
        order_ref[rank_ref[j]] = j
    for shift in range(N_GRP):
        stack_ref[(grp - shift) & 3] = layers[shift][...]
    pic = [jnp.zeros((TILE, STRIP), jnp.float32)] * 4
    for r in range(N_GRP):
        j = order_ref[r]
        free = 1.0 - pic[3]
        pic = [pic[c] + free * stack_ref[j, c] for c in range(4)]
    for c in range(4):
        out_ref[c] = pic[c]


def final(ranks, layers):
    return pl.pallas_call(
        final_kernel,
        in_specs=[SMEM_SPEC] + [VMEM_SPEC] * 4,
        out_specs=VMEM_SPEC,
        out_shape=jax.ShapeDtypeStruct((4, TILE, STRIP), jnp.float32),
        scratch_shapes=[pltpu.VMEM((N_GRP, 4, TILE, STRIP), jnp.float32), pltpu.SMEM((N_GRP,), jnp.int32)],
        compiler_params=params(SMALL),
        name="final",
    )(ranks, *layers)


def number(y, x, core):
    return 8 * (y % SIDE) + 2 * (x % SIDE) + core


def first_pairs(swap, shift):
    out = []
    for y in range(SIDE):
        for x in range(SIDE):
            for core in range(2):
                to = 1 - core if swap else core
                goal = number(y, x + shift, to) if to == 0 else number(y + shift, x, to)
                out.append((number(y, x, core), goal))
    return out


def second_pairs(shift):
    return [
        (number(y, x, core), number(y + shift, x, 0) if core == 0 else number(y, x + shift, 1))
        for y in range(SIDE)
        for x in range(SIDE)
        for core in range(2)
    ]


def body(volume, transfer_coef, group_order, member_order, active_mask):
    view = volume.reshape(SAMPLES, N_MEM, TILE, COLS)
    raw = []

    def send(n):
        swap, shift = SENDS[n]
        return lax.ppermute(raw[n], "mem", first_pairs(swap, shift)) if swap or shift else raw[n]

    own = depth(transfer_coef, active_mask, volume.reshape(SAMPLES, ROWS, COLS))
    depths = lax.all_to_all(own.reshape(N_MEM, TILE, COLS), "mem", 0, 0, tiled=True)
    for call in CALLS:
        raw += march(transfer_coef, active_mask, view, call, raw[-1:] or [own])
    colours = [send(n) for n in range(4)]
    *befores, total = prefix(member_order, depths, raw[-1:] + colours[:2])
    raw[4], raw[5], total = lax.optimization_barrier((raw[4], raw[5], total))
    colours += [send(n) for n in range(4, 8)]
    befores = [befores[0]] + [lax.ppermute(befores[k], "mem", second_pairs(k)) for k in range(1, SIDE)]

    shifts = (2, 1, 3)
    parts = [lax.ppermute(p, "mem", second_pairs(k)) for k, p in zip(shifts, weigh(colours, befores, shifts))]
    parts += weigh(colours, befores, (0,))
    layers = slab(parts, total)
    layers = [layers[0]] + [
        lax.ppermute(layers[s], "grp", [(g, (g + s) % N_GRP) for g in range(N_GRP)]) for s in range(1, N_GRP)
    ]
    return final(group_order, layers)


def solution(mesh):
    in_specs = (P("grp", "mem", None, None, None), P(), P(), P(), P("grp", "mem"))
    out_specs = P(None, "mem", "grp")
    return jax.shard_map(body, mesh=mesh, in_specs=in_specs, out_specs=out_specs, check_vma=False)
```

```python
import functools
import math

import jax
import jax.numpy as jnp
from jax import lax
from jax.experimental import pallas as pl
from jax.experimental.pallas import tpu as pltpu
from jax.sharding import PartitionSpec as P

SAMPLES = 8
ROWS = 512
COLS = 1024
N_GRP = 4
N_MEM = 32
SIDE = 4
TILE = ROWS // N_MEM
STRIP = COLS // N_GRP
VMEM = 60 << 20
SMALL = 24 << 20
PREFIX = 50 << 20
WEIGH = 58 << 20
DENSITY = math.sqrt(3.0 / (SAMPLES * N_GRP * N_MEM) * math.log2(math.e))


CALLS = [[(1, 1), (1, 3)], [(1, 2), (0, 2), (1, 0)], [(0, 1), (0, 3)], [(0, 0)]]
SENDS = [send for call in CALLS for send in call]

SMEM_SPEC = pl.BlockSpec(memory_space=pltpu.SMEM)
ANY_SPEC = pl.BlockSpec(memory_space=pl.ANY)
VMEM_SPEC = pl.BlockSpec(memory_space=pltpu.VMEM)
HBM_SPEC = pl.BlockSpec(memory_space=pltpu.HBM)


def params(limit=VMEM):
    return pltpu.CompilerParams(vmem_limit_bytes=limit)


def place():
    me = lax.axis_index("mem")
    return me >> 3, (me >> 1) & 3, me & 1


def cubic(q, v):
    return q[0] + v * (q[1] + v * (q[2] + v * q[3]))


def patch(i, width):
    per = COLS // width
    return pl.ds(pl.multiple_of((i // per) * 8, 8), 8), pl.ds(pl.multiple_of((i % per) * width, 128), width)


DEPTH_ROWS = 64
DEPTH_STEPS = ROWS // DEPTH_ROWS
DEPTH_SLOTS = 4


def depth_kernel(coef_ref, flag_ref, vol_ref, *refs):
    out_ref, inbuf, outbuf, insem, outsem = refs[-5:]
    q = [coef_ref[3, k] * DENSITY for k in range(4)]
    flag = flag_ref[0, 0].astype(jnp.float32)
    width = 512

    def fetch(i):
        return pltpu.make_async_copy(
            vol_ref.at[:, pl.ds(i * DEPTH_ROWS, DEPTH_ROWS), :], inbuf.at[i % DEPTH_SLOTS], insem.at[i % DEPTH_SLOTS]
        )

    def store(i):
        return pltpu.make_async_copy(outbuf.at[i % 2], out_ref.at[pl.ds(i * DEPTH_ROWS, DEPTH_ROWS), :], outsem.at[i % 2])

    for i in range(DEPTH_SLOTS):
        fetch(i).start()
    for i in range(DEPTH_STEPS):
        fetch(i).wait()
        if i >= 2:
            store(i - 2).wait()

        def step(n, carry, i=i):
            block, cols = patch(n, width)
            total = None
            for s in range(SAMPLES):
                d = cubic(q, inbuf[i % DEPTH_SLOTS, s, block, cols])
                total = d * d if total is None else total + d * d
            outbuf[i % 2, block, cols] = total * flag
            return carry

        lax.fori_loop(0, (DEPTH_ROWS // 8) * (COLS // width), step, 0, unroll=4)
        store(i).start()
        if i + DEPTH_SLOTS < DEPTH_STEPS:
            fetch(i + DEPTH_SLOTS).start()
    for i in range(DEPTH_STEPS - 2, DEPTH_STEPS):
        store(i).wait()


def depth(coef, flag, volume):
    return pl.pallas_call(
        depth_kernel,
        in_specs=[SMEM_SPEC, SMEM_SPEC, HBM_SPEC],
        out_specs=ANY_SPEC,
        out_shape=jax.ShapeDtypeStruct((ROWS, COLS), jnp.float32),
        scratch_shapes=[
            pltpu.VMEM((DEPTH_SLOTS, SAMPLES, DEPTH_ROWS, COLS), jnp.float32),
            pltpu.VMEM((2, DEPTH_ROWS, COLS), jnp.float32),
            pltpu.SemaphoreType.DMA((DEPTH_SLOTS,)),
            pltpu.SemaphoreType.DMA((2,)),
        ],
        compiler_params=params(),
        cost_estimate=pl.CostEstimate(flops=8 * SAMPLES * ROWS * COLS, bytes_accessed=36 * ROWS * COLS, transcendentals=0),
        name="depth",
    )(coef, flag, volume)


def march_kernel(coef_ref, flag_ref, vol_ref, *refs, call):
    count = len(call)
    outs, (inbuf, outbuf, insem, outsem) = refs[-4 - count:-4], refs[-4:]
    y, x, core = place()
    q = [[coef_ref[c, k] * (DENSITY if c == 3 else 0.5) for k in range(4)] for c in range(4)]
    half = 0.5 * flag_ref[0, 0].astype(jnp.float32)

    def fetch(k, i):
        swap, shift = call[k]
        to = 1 - core if swap else core
        along_x = 2 * ((x + shift) & 3) + 8 * i
        along_y = 8 * ((y + shift) & 3) + 2 * i + 1
        tile = jnp.where(to == 0, along_x, along_y)
        return pltpu.make_async_copy(vol_ref.at[:, tile], inbuf.at[k, i], insem.at[k, i])

    def store(k, i):
        return pltpu.make_async_copy(outbuf.at[k, i], outs[k].at[i], outsem.at[k, i])

    every = [(k, i) for k in range(count) for i in range(SIDE)]
    for k, i in every:
        fetch(k, i).start()
    for k in range(count):

        def tile_step(i, carry, k=k):
            fetch(k, i).wait()

            def step(n, carry):
                block = pl.ds(pl.multiple_of(n * 8, 8), 8)
                depth = clear = None
                acc = [None] * 3
                for s in range(SAMPLES):
                    v = inbuf[k, i, s, block, :]
                    d = cubic(q[3], v)
                    depth = -(d * d) if depth is None else depth - d * d
                    ahead = jnp.exp2(depth)
                    weight = 1.0 - ahead if clear is None else clear - ahead
                    clear = ahead
                    for ch in range(3):
                        term = weight * jnp.tanh(cubic(q[ch], v))
                        acc[ch] = term if acc[ch] is None else acc[ch] + term
                cover = 1.0 - clear
                for ch in range(3):
                    outbuf[k, i, ch, block, :] = (acc[ch] + cover) * half
                return carry

            lax.fori_loop(0, TILE // 8, step, 0)
            store(k, i).start()
            return carry

        lax.fori_loop(0, SIDE, tile_step, 0)
    for k, i in every:
        store(k, i).wait()


def march(coef, flag, view, call, after):
    tiles = SIDE * len(call)
    pixels = tiles * TILE * COLS
    return pl.pallas_call(
        functools.partial(march_kernel, call=call),
        in_specs=[SMEM_SPEC, SMEM_SPEC, HBM_SPEC] + [ANY_SPEC] * len(after),
        out_specs=[ANY_SPEC] * len(call),
        out_shape=[jax.ShapeDtypeStruct((SIDE, 3, TILE, COLS), jnp.float32)] * len(call),
        scratch_shapes=[
            pltpu.VMEM((len(call), SIDE, SAMPLES, TILE, COLS), jnp.float32),
            pltpu.VMEM((len(call), SIDE, 3, TILE, COLS), jnp.float32),
            pltpu.SemaphoreType.DMA((len(call), SIDE)),
            pltpu.SemaphoreType.DMA((len(call), SIDE)),
        ],
        compiler_params=params(),
        cost_estimate=pl.CostEstimate(
            flops=40 * SAMPLES * pixels, bytes_accessed=44 * pixels, transcendentals=4 * SAMPLES * pixels
        ),
        name="march",
    )(coef, flag, view, *after)


def prefix_kernel(rank_ref, depth_ref, *refs):
    outs, (total_ref, buf, order_ref, sem) = refs[-8:-4], refs[-4:]
    grp = lax.axis_index("grp")
    y, x, core = place()
    second = jnp.where(core == 0, y, x)
    for j in range(N_MEM):
        order_ref[rank_ref[grp, j]] = j

    def strip(i, carry):
        cols = pl.ds(pl.multiple_of(i * STRIP, 128), STRIP)

        def step(r, running):
            j = order_ref[r]
            across = 8 * ((j >> 1) & 3) + 2 * (j >> 3) + (j & 1)
            spot = jnp.where(core == 0, j, across)
            buf[spot >> 3, spot & 7, :, cols] = running
            return running + depth_ref[j, :, cols]

        total_ref[:, cols] = lax.fori_loop(0, N_MEM, step, jnp.zeros((TILE, STRIP), jnp.float32), unroll=4)
        return carry

    lax.fori_loop(0, COLS // STRIP, strip, 0)
    copies = [pltpu.make_async_copy(buf.at[(second + k) & 3], outs[k], sem.at[k]) for k in range(SIDE)]
    for copy in copies:
        copy.start()
    for copy in copies:
        copy.wait()


def prefix(ranks, depths, after):
    line = jax.ShapeDtypeStruct((8, TILE, COLS), jnp.float32)
    return pl.pallas_call(
        prefix_kernel,
        in_specs=[SMEM_SPEC, VMEM_SPEC] + [ANY_SPEC] * len(after),
        out_specs=[ANY_SPEC] * SIDE + [VMEM_SPEC],
        out_shape=[line] * SIDE + [jax.ShapeDtypeStruct((TILE, COLS), jnp.float32)],
        scratch_shapes=[
            pltpu.VMEM((SIDE, 8, TILE, COLS), jnp.float32),
            pltpu.SMEM((N_MEM,), jnp.int32),
            pltpu.SemaphoreType.DMA((SIDE,)),
        ],
        compiler_params=params(PREFIX),
        cost_estimate=pl.CostEstimate(
            flops=N_MEM * TILE * COLS, bytes_accessed=8 * N_MEM * TILE * COLS, transcendentals=0
        ),
        name="prefix",
    )(ranks, depths, *after)


def weigh_kernel(*refs, shifts):
    count = len(shifts)
    colours, befores, outs = refs[:8], refs[8:8 + count], refs[8 + count:8 + 2 * count]
    colbuf, depbuf, outbuf, colsem, depsem, outsem = refs[8 + 2 * count:]
    y, x, core = place()
    first, second = jnp.where(core == 0, x, y), jnp.where(core == 0, y, x)

    def fetch(i):
        spot = (second + shifts[i]) & 3
        return [pltpu.make_async_copy(befores[i], depbuf.at[i], depsem.at[i])] + [
            pltpu.make_async_copy(colours[n].at[spot], colbuf.at[i, n], colsem.at[i, n]) for n in range(8)
        ]

    def store(i):
        return pltpu.make_async_copy(outbuf.at[i], outs[i], outsem.at[i])

    slots = [2 * ((first - shift) & 3) + (1 - core if swap else core) for swap, shift in SENDS]
    for i in range(count):
        for copy in fetch(i):
            copy.start()
    for i in range(count):
        for copy in fetch(i):
            copy.wait()

        def step(n, carry, i=i):
            block, cols = patch(n, 256)
            acc = [None] * 3
            for k in range(8):
                light = jnp.exp2(-depbuf[i, slots[k], block, cols])
                for ch in range(3):
                    term = light * colbuf[i, k, ch, block, cols]
                    acc[ch] = term if acc[ch] is None else acc[ch] + term
            for ch in range(3):
                outbuf[i, ch, block, cols] = acc[ch]
            return carry

        lax.fori_loop(0, 8, step, 0)
        store(i).start()
    for i in range(count):
        store(i).wait()


def weigh(colours, befores, shifts):
    count = len(shifts)
    return pl.pallas_call(
        functools.partial(weigh_kernel, shifts=shifts),
        in_specs=[ANY_SPEC] * (8 + count),
        out_specs=[ANY_SPEC] * count,
        out_shape=[jax.ShapeDtypeStruct((3, TILE, COLS), jnp.float32)] * count,
        scratch_shapes=[
            pltpu.VMEM((count, 8, 3, TILE, COLS), jnp.float32),
            pltpu.VMEM((count, 8, TILE, COLS), jnp.float32),
            pltpu.VMEM((count, 3, TILE, COLS), jnp.float32),
            pltpu.SemaphoreType.DMA((count, 8)),
            pltpu.SemaphoreType.DMA((count,)),
            pltpu.SemaphoreType.DMA((count,)),
        ],
        compiler_params=params(WEIGH),
        cost_estimate=pl.CostEstimate(
            flops=56 * count * TILE * COLS, bytes_accessed=140 * count * TILE * COLS, transcendentals=8 * count * TILE * COLS
        ),
        name="weigh",
    )(*colours, *[befores[-shift % SIDE] for shift in shifts])


def slab_kernel(*refs):
    parts, total_ref, outs = refs[:4], refs[4], refs[5:]
    grp = lax.axis_index("grp")
    for shift in range(N_GRP):
        cols = pl.ds(pl.multiple_of(((grp + shift) & 3) * STRIP, 128), STRIP)
        for ch in range(3):
            outs[shift][ch] = (parts[0][ch, :, cols] + parts[1][ch, :, cols]) + (
                parts[2][ch, :, cols] + parts[3][ch, :, cols]
            )
        outs[shift][3] = 1.0 - jnp.exp2(-total_ref[:, cols])


def slab(parts, total):
    return pl.pallas_call(
        slab_kernel,
        in_specs=[VMEM_SPEC] * 5,
        out_specs=[VMEM_SPEC] * 4,
        out_shape=[jax.ShapeDtypeStruct((4, TILE, STRIP), jnp.float32)] * 4,
        compiler_params=params(SMALL),
        name="slab",
    )(*parts, total)


def final_kernel(rank_ref, *refs):
    layers, (out_ref, stack_ref, order_ref) = refs[:4], refs[4:]
    grp = lax.axis_index("grp")
    for j in range(N_GRP):
        order_ref[rank_ref[j]] = j
    for shift in range(N_GRP):
        stack_ref[(grp - shift) & 3] = layers[shift][...]
    pic = [jnp.zeros((TILE, STRIP), jnp.float32)] * 4
    for r in range(N_GRP):
        j = order_ref[r]
        free = 1.0 - pic[3]
        pic = [pic[c] + free * stack_ref[j, c] for c in range(4)]
    for c in range(4):
        out_ref[c] = pic[c]


def final(ranks, layers):
    return pl.pallas_call(
        final_kernel,
        in_specs=[SMEM_SPEC] + [VMEM_SPEC] * 4,
        out_specs=VMEM_SPEC,
        out_shape=jax.ShapeDtypeStruct((4, TILE, STRIP), jnp.float32),
        scratch_shapes=[pltpu.VMEM((N_GRP, 4, TILE, STRIP), jnp.float32), pltpu.SMEM((N_GRP,), jnp.int32)],
        compiler_params=params(SMALL),
        name="final",
    )(ranks, *layers)


def number(y, x, core):
    return 8 * (y % SIDE) + 2 * (x % SIDE) + core


def first_pairs(swap, shift):
    out = []
    for y in range(SIDE):
        for x in range(SIDE):
            for core in range(2):
                to = 1 - core if swap else core
                goal = number(y, x + shift, to) if to == 0 else number(y + shift, x, to)
                out.append((number(y, x, core), goal))
    return out


def second_pairs(shift):
    return [
        (number(y, x, core), number(y + shift, x, 0) if core == 0 else number(y, x + shift, 1))
        for y in range(SIDE)
        for x in range(SIDE)
        for core in range(2)
    ]


def body(volume, transfer_coef, group_order, member_order, active_mask):
    view = volume.reshape(SAMPLES, N_MEM, TILE, COLS)
    raw = []

    def send(n):
        swap, shift = SENDS[n]
        return lax.ppermute(raw[n], "mem", first_pairs(swap, shift)) if swap or shift else raw[n]

    own = depth(transfer_coef, active_mask, volume.reshape(SAMPLES, ROWS, COLS))
    depths = lax.all_to_all(own.reshape(N_MEM, TILE, COLS), "mem", 0, 0, tiled=True)
    for call in CALLS:
        raw += march(transfer_coef, active_mask, view, call, raw[-1:] or [own])
    colours = [send(n) for n in range(8)]
    *befores, total = prefix(member_order, depths, raw[-1:] + [colours[0], colours[1], colours[4]])
    befores = [befores[0]] + [lax.ppermute(befores[k], "mem", second_pairs(k)) for k in range(1, SIDE)]

    shifts = (2, 1, 3)
    parts = [lax.ppermute(p, "mem", second_pairs(k)) for k, p in zip(shifts, weigh(colours, befores, shifts))]
    parts += weigh(colours, befores, (0,))
    layers = slab(parts, total)
    layers = [layers[0]] + [
        lax.ppermute(layers[s], "grp", [(g, (g + s) % N_GRP) for g in range(N_GRP)]) for s in range(1, N_GRP)
    ]
    return final(group_order, layers)


def solution(mesh):
    in_specs = (P("grp", "mem", None, None, None), P(), P(), P(), P("grp", "mem"))
    out_specs = P(None, "mem", "grp")
    return jax.shard_map(body, mesh=mesh, in_specs=in_specs, out_specs=out_specs, check_vma=False)
```

```python
import functools
import math

import jax
import jax.numpy as jnp
from jax import lax
from jax.experimental import pallas as pl
from jax.experimental.pallas import tpu as pltpu
from jax.sharding import PartitionSpec as P

SAMPLES = 8
ROWS = 512
COLS = 1024
N_GRP = 4
N_MEM = 32
SIDE = 4
TILE = ROWS // N_MEM
STRIP = COLS // N_GRP
VMEM = 50 << 20
SMALL = 24 << 20
PREFIX = 50 << 20
WEIGH = 50 << 20
DENSITY = math.sqrt(3.0 / (SAMPLES * N_GRP * N_MEM) * math.log2(math.e))


CALLS = [[(1, 1), (1, 3)], [(1, 2), (0, 2), (1, 0)], [(0, 1), (0, 3)], [(0, 0)]]
SENDS = [send for call in CALLS for send in call]

SMEM_SPEC = pl.BlockSpec(memory_space=pltpu.SMEM)
ANY_SPEC = pl.BlockSpec(memory_space=pl.ANY)
VMEM_SPEC = pl.BlockSpec(memory_space=pltpu.VMEM)
HBM_SPEC = pl.BlockSpec(memory_space=pltpu.HBM)


def params(limit=VMEM):
    return pltpu.CompilerParams(vmem_limit_bytes=limit)


def place():
    me = lax.axis_index("mem")
    return me >> 3, (me >> 1) & 3, me & 1


def cubic(q, v):
    return q[0] + v * (q[1] + v * (q[2] + v * q[3]))


def patch(i, width):
    per = COLS // width
    return pl.ds(pl.multiple_of((i // per) * 8, 8), 8), pl.ds(pl.multiple_of((i % per) * width, 128), width)


DEPTH_ROWS = 64
DEPTH_STEPS = ROWS // DEPTH_ROWS
DEPTH_SLOTS = 4


def depth_kernel(coef_ref, flag_ref, vol_ref, *refs):
    out_ref, inbuf, outbuf, insem, outsem = refs[-5:]
    q = [coef_ref[3, k] * DENSITY for k in range(4)]
    flag = flag_ref[0, 0].astype(jnp.float32)
    width = 512

    def fetch(i):
        return pltpu.make_async_copy(
            vol_ref.at[:, pl.ds(i * DEPTH_ROWS, DEPTH_ROWS), :], inbuf.at[i % DEPTH_SLOTS], insem.at[i % DEPTH_SLOTS]
        )

    def store(i):
        return pltpu.make_async_copy(outbuf.at[i % 2], out_ref.at[pl.ds(i * DEPTH_ROWS, DEPTH_ROWS), :], outsem.at[i % 2])

    for i in range(DEPTH_SLOTS):
        fetch(i).start()
    for i in range(DEPTH_STEPS):
        fetch(i).wait()
        if i >= 2:
            store(i - 2).wait()

        def step(n, carry, i=i):
            block, cols = patch(n, width)
            total = None
            for s in range(SAMPLES):
                d = cubic(q, inbuf[i % DEPTH_SLOTS, s, block, cols])
                total = d * d if total is None else total + d * d
            outbuf[i % 2, block, cols] = total * flag
            return carry

        lax.fori_loop(0, (DEPTH_ROWS // 8) * (COLS // width), step, 0, unroll=4)
        store(i).start()
        if i + DEPTH_SLOTS < DEPTH_STEPS:
            fetch(i + DEPTH_SLOTS).start()
    for i in range(DEPTH_STEPS - 2, DEPTH_STEPS):
        store(i).wait()


def depth(coef, flag, volume):
    return pl.pallas_call(
        depth_kernel,
        in_specs=[SMEM_SPEC, SMEM_SPEC, HBM_SPEC],
        out_specs=ANY_SPEC,
        out_shape=jax.ShapeDtypeStruct((ROWS, COLS), jnp.float32),
        scratch_shapes=[
            pltpu.VMEM((DEPTH_SLOTS, SAMPLES, DEPTH_ROWS, COLS), jnp.float32),
            pltpu.VMEM((2, DEPTH_ROWS, COLS), jnp.float32),
            pltpu.SemaphoreType.DMA((DEPTH_SLOTS,)),
            pltpu.SemaphoreType.DMA((2,)),
        ],
        compiler_params=params(),
        cost_estimate=pl.CostEstimate(flops=8 * SAMPLES * ROWS * COLS, bytes_accessed=36 * ROWS * COLS, transcendentals=0),
        name="depth",
    )(coef, flag, volume)


def march_kernel(coef_ref, flag_ref, vol_ref, *refs, call):
    count = len(call)
    outs, (inbuf, outbuf, insem, outsem) = refs[-4 - count:-4], refs[-4:]
    y, x, core = place()
    q = [[coef_ref[c, k] * (DENSITY if c == 3 else 0.5) for k in range(4)] for c in range(4)]
    half = 0.5 * flag_ref[0, 0].astype(jnp.float32)

    def fetch(k, i):
        swap, shift = call[k]
        to = 1 - core if swap else core
        along_x = 2 * ((x + shift) & 3) + 8 * i
        along_y = 8 * ((y + shift) & 3) + 2 * i + 1
        tile = jnp.where(to == 0, along_x, along_y)
        return pltpu.make_async_copy(vol_ref.at[:, tile], inbuf.at[k, i], insem.at[k, i])

    def store(k, i):
        return pltpu.make_async_copy(outbuf.at[k, i], outs[k].at[i], outsem.at[k, i])

    every = [(k, i) for k in range(count) for i in range(SIDE)]
    for k, i in every:
        fetch(k, i).start()
    for k in range(count):

        def tile_step(i, carry, k=k):
            fetch(k, i).wait()

            def step(n, carry):
                block = pl.ds(pl.multiple_of(n * 8, 8), 8)
                depth = clear = None
                acc = [None] * 3
                for s in range(SAMPLES):
                    v = inbuf[k, i, s, block, :]
                    d = cubic(q[3], v)
                    depth = -(d * d) if depth is None else depth - d * d
                    ahead = jnp.exp2(depth)
                    weight = 1.0 - ahead if clear is None else clear - ahead
                    clear = ahead
                    for ch in range(3):
                        term = weight * jnp.tanh(cubic(q[ch], v))
                        acc[ch] = term if acc[ch] is None else acc[ch] + term
                cover = 1.0 - clear
                for ch in range(3):
                    outbuf[k, i, ch, block, :] = (acc[ch] + cover) * half
                return carry

            lax.fori_loop(0, TILE // 8, step, 0)
            store(k, i).start()
            return carry

        lax.fori_loop(0, SIDE, tile_step, 0)
    for k, i in every:
        store(k, i).wait()


def march(coef, flag, view, call, after):
    tiles = SIDE * len(call)
    pixels = tiles * TILE * COLS
    return pl.pallas_call(
        functools.partial(march_kernel, call=call),
        in_specs=[SMEM_SPEC, SMEM_SPEC, HBM_SPEC] + [ANY_SPEC] * len(after),
        out_specs=[ANY_SPEC] * len(call),
        out_shape=[jax.ShapeDtypeStruct((SIDE, 3, TILE, COLS), jnp.float32)] * len(call),
        scratch_shapes=[
            pltpu.VMEM((len(call), SIDE, SAMPLES, TILE, COLS), jnp.float32),
            pltpu.VMEM((len(call), SIDE, 3, TILE, COLS), jnp.float32),
            pltpu.SemaphoreType.DMA((len(call), SIDE)),
            pltpu.SemaphoreType.DMA((len(call), SIDE)),
        ],
        compiler_params=params(),
        cost_estimate=pl.CostEstimate(
            flops=40 * SAMPLES * pixels, bytes_accessed=44 * pixels, transcendentals=4 * SAMPLES * pixels
        ),
        name="march",
    )(coef, flag, view, *after)


def prefix_kernel(rank_ref, depth_ref, *refs):
    outs, (total_ref, buf, order_ref, sem) = refs[-8:-4], refs[-4:]
    grp = lax.axis_index("grp")
    y, x, core = place()
    second = jnp.where(core == 0, y, x)
    for j in range(N_MEM):
        order_ref[rank_ref[grp, j]] = j

    def strip(i, carry):
        cols = pl.ds(pl.multiple_of(i * STRIP, 128), STRIP)

        def step(r, running):
            j = order_ref[r]
            across = 8 * ((j >> 1) & 3) + 2 * (j >> 3) + (j & 1)
            spot = jnp.where(core == 0, j, across)
            buf[spot >> 3, spot & 7, :, cols] = running
            return running + depth_ref[j, :, cols]

        total_ref[:, cols] = lax.fori_loop(0, N_MEM, step, jnp.zeros((TILE, STRIP), jnp.float32), unroll=4)
        return carry

    lax.fori_loop(0, COLS // STRIP, strip, 0)
    copies = [pltpu.make_async_copy(buf.at[(second + k) & 3], outs[k], sem.at[k]) for k in range(SIDE)]
    for copy in copies:
        copy.start()
    for copy in copies:
        copy.wait()


def prefix(ranks, depths, after):
    line = jax.ShapeDtypeStruct((8, TILE, COLS), jnp.float32)
    return pl.pallas_call(
        prefix_kernel,
        in_specs=[SMEM_SPEC, VMEM_SPEC] + [ANY_SPEC] * len(after),
        out_specs=[ANY_SPEC] * SIDE + [VMEM_SPEC],
        out_shape=[line] * SIDE + [jax.ShapeDtypeStruct((TILE, COLS), jnp.float32)],
        scratch_shapes=[
            pltpu.VMEM((SIDE, 8, TILE, COLS), jnp.float32),
            pltpu.SMEM((N_MEM,), jnp.int32),
            pltpu.SemaphoreType.DMA((SIDE,)),
        ],
        compiler_params=params(PREFIX),
        cost_estimate=pl.CostEstimate(
            flops=N_MEM * TILE * COLS, bytes_accessed=8 * N_MEM * TILE * COLS, transcendentals=0
        ),
        name="prefix",
    )(ranks, depths, *after)


def weigh_kernel(*refs, shifts):
    count = len(shifts)
    colours, befores, outs = refs[:8], refs[8:8 + count], refs[8 + count:8 + 2 * count]
    colbuf, depbuf, outbuf, colsem, depsem, outsem = refs[8 + 2 * count:]
    y, x, core = place()
    first, second = jnp.where(core == 0, x, y), jnp.where(core == 0, y, x)

    def fetch(i):
        spot = (second + shifts[i]) & 3
        return [pltpu.make_async_copy(befores[i], depbuf.at[i], depsem.at[i])] + [
            pltpu.make_async_copy(colours[n].at[spot], colbuf.at[i, n], colsem.at[i, n]) for n in range(8)
        ]

    def store(i):
        return pltpu.make_async_copy(outbuf.at[i], outs[i], outsem.at[i])

    slots = [2 * ((first - shift) & 3) + (1 - core if swap else core) for swap, shift in SENDS]
    for i in range(count):
        for copy in fetch(i):
            copy.start()
    for i in range(count):
        for copy in fetch(i):
            copy.wait()

        def step(n, carry, i=i):
            block, cols = patch(n, 256)
            acc = [None] * 3
            for k in range(8):
                light = jnp.exp2(-depbuf[i, slots[k], block, cols])
                for ch in range(3):
                    term = light * colbuf[i, k, ch, block, cols]
                    acc[ch] = term if acc[ch] is None else acc[ch] + term
            for ch in range(3):
                outbuf[i, ch, block, cols] = acc[ch]
            return carry

        lax.fori_loop(0, 8, step, 0)
        store(i).start()
    for i in range(count):
        store(i).wait()


def weigh(colours, befores, shifts):
    count = len(shifts)
    return pl.pallas_call(
        functools.partial(weigh_kernel, shifts=shifts),
        in_specs=[ANY_SPEC] * (8 + count),
        out_specs=[ANY_SPEC] * count,
        out_shape=[jax.ShapeDtypeStruct((3, TILE, COLS), jnp.float32)] * count,
        scratch_shapes=[
            pltpu.VMEM((count, 8, 3, TILE, COLS), jnp.float32),
            pltpu.VMEM((count, 8, TILE, COLS), jnp.float32),
            pltpu.VMEM((count, 3, TILE, COLS), jnp.float32),
            pltpu.SemaphoreType.DMA((count, 8)),
            pltpu.SemaphoreType.DMA((count,)),
            pltpu.SemaphoreType.DMA((count,)),
        ],
        compiler_params=params(WEIGH),
        cost_estimate=pl.CostEstimate(
            flops=56 * count * TILE * COLS, bytes_accessed=140 * count * TILE * COLS, transcendentals=8 * count * TILE * COLS
        ),
        name="weigh",
    )(*colours, *[befores[-shift % SIDE] for shift in shifts])


def slab_kernel(*refs):
    parts, total_ref, outs = refs[:4], refs[4], refs[5:]
    grp = lax.axis_index("grp")
    for shift in range(N_GRP):
        cols = pl.ds(pl.multiple_of(((grp + shift) & 3) * STRIP, 128), STRIP)
        for ch in range(3):
            outs[shift][ch] = (parts[0][ch, :, cols] + parts[1][ch, :, cols]) + (
                parts[2][ch, :, cols] + parts[3][ch, :, cols]
            )
        outs[shift][3] = 1.0 - jnp.exp2(-total_ref[:, cols])


def slab(parts, total):
    return pl.pallas_call(
        slab_kernel,
        in_specs=[VMEM_SPEC] * 5,
        out_specs=[VMEM_SPEC] * 4,
        out_shape=[jax.ShapeDtypeStruct((4, TILE, STRIP), jnp.float32)] * 4,
        compiler_params=params(SMALL),
        name="slab",
    )(*parts, total)


def final_kernel(rank_ref, *refs):
    layers, (out_ref, stack_ref, order_ref) = refs[:4], refs[4:]
    grp = lax.axis_index("grp")
    for j in range(N_GRP):
        order_ref[rank_ref[j]] = j
    for shift in range(N_GRP):
        stack_ref[(grp - shift) & 3] = layers[shift][...]
    pic = [jnp.zeros((TILE, STRIP), jnp.float32)] * 4
    for r in range(N_GRP):
        j = order_ref[r]
        free = 1.0 - pic[3]
        pic = [pic[c] + free * stack_ref[j, c] for c in range(4)]
    for c in range(4):
        out_ref[c] = pic[c]


def final(ranks, layers):
    return pl.pallas_call(
        final_kernel,
        in_specs=[SMEM_SPEC] + [VMEM_SPEC] * 4,
        out_specs=VMEM_SPEC,
        out_shape=jax.ShapeDtypeStruct((4, TILE, STRIP), jnp.float32),
        scratch_shapes=[pltpu.VMEM((N_GRP, 4, TILE, STRIP), jnp.float32), pltpu.SMEM((N_GRP,), jnp.int32)],
        compiler_params=params(SMALL),
        name="final",
    )(ranks, *layers)


def number(y, x, core):
    return 8 * (y % SIDE) + 2 * (x % SIDE) + core


def first_pairs(swap, shift):
    out = []
    for y in range(SIDE):
        for x in range(SIDE):
            for core in range(2):
                to = 1 - core if swap else core
                goal = number(y, x + shift, to) if to == 0 else number(y + shift, x, to)
                out.append((number(y, x, core), goal))
    return out


def second_pairs(shift):
    return [
        (number(y, x, core), number(y + shift, x, 0) if core == 0 else number(y, x + shift, 1))
        for y in range(SIDE)
        for x in range(SIDE)
        for core in range(2)
    ]


def body(volume, transfer_coef, group_order, member_order, active_mask):
    view = volume.reshape(SAMPLES, N_MEM, TILE, COLS)
    raw = []

    def send(n):
        swap, shift = SENDS[n]
        return lax.ppermute(raw[n], "mem", first_pairs(swap, shift)) if swap or shift else raw[n]

    own = depth(transfer_coef, active_mask, volume.reshape(SAMPLES, ROWS, COLS))
    depths = lax.all_to_all(own.reshape(N_MEM, TILE, COLS), "mem", 0, 0, tiled=True)
    for call in CALLS:
        raw += march(transfer_coef, active_mask, view, call, raw[-1:] or [own])
    colours = [send(n) for n in range(8)]
    *befores, total = prefix(member_order, depths, raw[-1:] + [colours[0], colours[1], colours[4]])
    befores = [befores[0]] + [lax.ppermute(befores[k], "mem", second_pairs(k)) for k in range(1, SIDE)]

    shifts = (2, 1, 3)
    parts = [lax.ppermute(p, "mem", second_pairs(k)) for k, p in zip(shifts, weigh(colours, befores, shifts))]
    parts += weigh(colours, befores, (0,))
    layers = slab(parts, total)
    layers = [layers[0]] + [
        lax.ppermute(layers[s], "grp", [(g, (g + s) % N_GRP) for g in range(N_GRP)]) for s in range(1, N_GRP)
    ]
    return final(group_order, layers)


def solution(mesh):
    in_specs = (P("grp", "mem", None, None, None), P(), P(), P(), P("grp", "mem"))
    out_specs = P(None, "mem", "grp")
    return jax.shard_map(body, mesh=mesh, in_specs=in_specs, out_specs=out_specs, check_vma=False)
```

```python
import functools
import math

import jax
import jax.numpy as jnp
from jax import lax
from jax.experimental import pallas as pl
from jax.experimental.pallas import tpu as pltpu
from jax.sharding import PartitionSpec as P

SAMPLES = 8
ROWS = 512
COLS = 1024
N_GRP = 4
N_MEM = 32
SIDE = 4
TILE = ROWS // N_MEM
STRIP = COLS // N_GRP
VMEM = 50 << 20
SMALL = 24 << 20
PREFIX = 50 << 20
WEIGH = 50 << 20
DENSITY = math.sqrt(3.0 / (SAMPLES * N_GRP * N_MEM) * math.log2(math.e))


CALLS = [[(1, 1), (1, 3)], [(1, 2), (0, 2), (1, 0)], [(0, 0)], [(0, 1), (0, 3)]]
SENDS = [send for call in CALLS for send in call]

SMEM_SPEC = pl.BlockSpec(memory_space=pltpu.SMEM)
ANY_SPEC = pl.BlockSpec(memory_space=pl.ANY)
VMEM_SPEC = pl.BlockSpec(memory_space=pltpu.VMEM)
HBM_SPEC = pl.BlockSpec(memory_space=pltpu.HBM)


def params(limit=VMEM):
    return pltpu.CompilerParams(vmem_limit_bytes=limit)


def place():
    me = lax.axis_index("mem")
    return me >> 3, (me >> 1) & 3, me & 1


def cubic(q, v):
    return q[0] + v * (q[1] + v * (q[2] + v * q[3]))


def patch(i, width):
    per = COLS // width
    return pl.ds(pl.multiple_of((i // per) * 8, 8), 8), pl.ds(pl.multiple_of((i % per) * width, 128), width)


DEPTH_ROWS = 64
DEPTH_STEPS = ROWS // DEPTH_ROWS
DEPTH_SLOTS = 4


def depth_kernel(coef_ref, flag_ref, vol_ref, *refs):
    out_ref, inbuf, outbuf, insem, outsem = refs[-5:]
    q = [coef_ref[3, k] * DENSITY for k in range(4)]
    flag = flag_ref[0, 0].astype(jnp.float32)
    width = 512

    def fetch(i):
        return pltpu.make_async_copy(
            vol_ref.at[:, pl.ds(i * DEPTH_ROWS, DEPTH_ROWS), :], inbuf.at[i % DEPTH_SLOTS], insem.at[i % DEPTH_SLOTS]
        )

    def store(i):
        return pltpu.make_async_copy(outbuf.at[i % 2], out_ref.at[pl.ds(i * DEPTH_ROWS, DEPTH_ROWS), :], outsem.at[i % 2])

    for i in range(DEPTH_SLOTS):
        fetch(i).start()
    for i in range(DEPTH_STEPS):
        fetch(i).wait()
        if i >= 2:
            store(i - 2).wait()

        def step(n, carry, i=i):
            block, cols = patch(n, width)
            total = None
            for s in range(SAMPLES):
                d = cubic(q, inbuf[i % DEPTH_SLOTS, s, block, cols])
                total = d * d if total is None else total + d * d
            outbuf[i % 2, block, cols] = total * flag
            return carry

        lax.fori_loop(0, (DEPTH_ROWS // 8) * (COLS // width), step, 0, unroll=4)
        store(i).start()
        if i + DEPTH_SLOTS < DEPTH_STEPS:
            fetch(i + DEPTH_SLOTS).start()
    for i in range(DEPTH_STEPS - 2, DEPTH_STEPS):
        store(i).wait()


def depth(coef, flag, volume):
    return pl.pallas_call(
        depth_kernel,
        in_specs=[SMEM_SPEC, SMEM_SPEC, HBM_SPEC],
        out_specs=ANY_SPEC,
        out_shape=jax.ShapeDtypeStruct((ROWS, COLS), jnp.float32),
        scratch_shapes=[
            pltpu.VMEM((DEPTH_SLOTS, SAMPLES, DEPTH_ROWS, COLS), jnp.float32),
            pltpu.VMEM((2, DEPTH_ROWS, COLS), jnp.float32),
            pltpu.SemaphoreType.DMA((DEPTH_SLOTS,)),
            pltpu.SemaphoreType.DMA((2,)),
        ],
        compiler_params=params(),
        cost_estimate=pl.CostEstimate(flops=8 * SAMPLES * ROWS * COLS, bytes_accessed=36 * ROWS * COLS, transcendentals=0),
        name="depth",
    )(coef, flag, volume)


def march_kernel(coef_ref, flag_ref, vol_ref, *refs, call):
    count = len(call)
    outs, (inbuf, outbuf, insem, outsem) = refs[-4 - count:-4], refs[-4:]
    y, x, core = place()
    q = [[coef_ref[c, k] * (DENSITY if c == 3 else 0.5) for k in range(4)] for c in range(4)]
    half = 0.5 * flag_ref[0, 0].astype(jnp.float32)

    def fetch(k, i):
        swap, shift = call[k]
        to = 1 - core if swap else core
        along_x = 2 * ((x + shift) & 3) + 8 * i
        along_y = 8 * ((y + shift) & 3) + 2 * i + 1
        tile = jnp.where(to == 0, along_x, along_y)
        return pltpu.make_async_copy(vol_ref.at[:, tile], inbuf.at[k, i], insem.at[k, i])

    def store(k, i):
        return pltpu.make_async_copy(outbuf.at[k, i], outs[k].at[i], outsem.at[k, i])

    every = [(k, i) for k in range(count) for i in range(SIDE)]
    for k, i in every:
        fetch(k, i).start()
    for k in range(count):

        def tile_step(i, carry, k=k):
            fetch(k, i).wait()

            def step(n, carry):
                block = pl.ds(pl.multiple_of(n * 8, 8), 8)
                depth = clear = None
                acc = [None] * 3
                for s in range(SAMPLES):
                    v = inbuf[k, i, s, block, :]
                    d = cubic(q[3], v)
                    depth = -(d * d) if depth is None else depth - d * d
                    ahead = jnp.exp2(depth)
                    weight = 1.0 - ahead if clear is None else clear - ahead
                    clear = ahead
                    for ch in range(3):
                        term = weight * jnp.tanh(cubic(q[ch], v))
                        acc[ch] = term if acc[ch] is None else acc[ch] + term
                cover = 1.0 - clear
                for ch in range(3):
                    outbuf[k, i, ch, block, :] = (acc[ch] + cover) * half
                return carry

            lax.fori_loop(0, TILE // 8, step, 0)
            store(k, i).start()
            return carry

        lax.fori_loop(0, SIDE, tile_step, 0)
    for k, i in every:
        store(k, i).wait()


def march(coef, flag, view, call, after):
    tiles = SIDE * len(call)
    pixels = tiles * TILE * COLS
    return pl.pallas_call(
        functools.partial(march_kernel, call=call),
        in_specs=[SMEM_SPEC, SMEM_SPEC, HBM_SPEC] + [ANY_SPEC] * len(after),
        out_specs=[ANY_SPEC] * len(call),
        out_shape=[jax.ShapeDtypeStruct((SIDE, 3, TILE, COLS), jnp.float32)] * len(call),
        scratch_shapes=[
            pltpu.VMEM((len(call), SIDE, SAMPLES, TILE, COLS), jnp.float32),
            pltpu.VMEM((len(call), SIDE, 3, TILE, COLS), jnp.float32),
            pltpu.SemaphoreType.DMA((len(call), SIDE)),
            pltpu.SemaphoreType.DMA((len(call), SIDE)),
        ],
        compiler_params=params(),
        cost_estimate=pl.CostEstimate(
            flops=40 * SAMPLES * pixels, bytes_accessed=44 * pixels, transcendentals=4 * SAMPLES * pixels
        ),
        name="march",
    )(coef, flag, view, *after)


def prefix_kernel(rank_ref, depth_ref, *refs):
    outs, (total_ref, buf, order_ref, sem) = refs[-8:-4], refs[-4:]
    grp = lax.axis_index("grp")
    y, x, core = place()
    second = jnp.where(core == 0, y, x)
    for j in range(N_MEM):
        order_ref[rank_ref[grp, j]] = j

    def strip(i, carry):
        cols = pl.ds(pl.multiple_of(i * STRIP, 128), STRIP)

        def step(r, running):
            j = order_ref[r]
            across = 8 * ((j >> 1) & 3) + 2 * (j >> 3) + (j & 1)
            spot = jnp.where(core == 0, j, across)
            buf[spot >> 3, spot & 7, :, cols] = running
            return running + depth_ref[j, :, cols]

        total_ref[:, cols] = lax.fori_loop(0, N_MEM, step, jnp.zeros((TILE, STRIP), jnp.float32), unroll=4)
        return carry

    lax.fori_loop(0, COLS // STRIP, strip, 0)
    copies = [pltpu.make_async_copy(buf.at[(second + k) & 3], outs[k], sem.at[k]) for k in range(SIDE)]
    for copy in copies:
        copy.start()
    for copy in copies:
        copy.wait()


def prefix(ranks, depths, after):
    line = jax.ShapeDtypeStruct((8, TILE, COLS), jnp.float32)
    return pl.pallas_call(
        prefix_kernel,
        in_specs=[SMEM_SPEC, VMEM_SPEC] + [ANY_SPEC] * len(after),
        out_specs=[ANY_SPEC] * SIDE + [VMEM_SPEC],
        out_shape=[line] * SIDE + [jax.ShapeDtypeStruct((TILE, COLS), jnp.float32)],
        scratch_shapes=[
            pltpu.VMEM((SIDE, 8, TILE, COLS), jnp.float32),
            pltpu.SMEM((N_MEM,), jnp.int32),
            pltpu.SemaphoreType.DMA((SIDE,)),
        ],
        compiler_params=params(PREFIX),
        cost_estimate=pl.CostEstimate(
            flops=N_MEM * TILE * COLS, bytes_accessed=8 * N_MEM * TILE * COLS, transcendentals=0
        ),
        name="prefix",
    )(ranks, depths, *after)


def weigh_kernel(*refs, shifts):
    count = len(shifts)
    colours, befores, outs = refs[:8], refs[8:8 + count], refs[8 + count:8 + 2 * count]
    colbuf, depbuf, outbuf, colsem, depsem, outsem = refs[8 + 2 * count:]
    y, x, core = place()
    first, second = jnp.where(core == 0, x, y), jnp.where(core == 0, y, x)

    def fetch(i):
        spot = (second + shifts[i]) & 3
        return [pltpu.make_async_copy(befores[i], depbuf.at[i], depsem.at[i])] + [
            pltpu.make_async_copy(colours[n].at[spot], colbuf.at[i, n], colsem.at[i, n]) for n in range(8)
        ]

    def store(i):
        return pltpu.make_async_copy(outbuf.at[i], outs[i], outsem.at[i])

    slots = [2 * ((first - shift) & 3) + (1 - core if swap else core) for swap, shift in SENDS]
    for i in range(count):
        for copy in fetch(i):
            copy.start()
    for i in range(count):
        for copy in fetch(i):
            copy.wait()

        def step(n, carry, i=i):
            block, cols = patch(n, 256)
            acc = [None] * 3
            for k in range(8):
                light = jnp.exp2(-depbuf[i, slots[k], block, cols])
                for ch in range(3):
                    term = light * colbuf[i, k, ch, block, cols]
                    acc[ch] = term if acc[ch] is None else acc[ch] + term
            for ch in range(3):
                outbuf[i, ch, block, cols] = acc[ch]
            return carry

        lax.fori_loop(0, 8, step, 0)
        store(i).start()
    for i in range(count):
        store(i).wait()


def weigh(colours, befores, shifts):
    count = len(shifts)
    return pl.pallas_call(
        functools.partial(weigh_kernel, shifts=shifts),
        in_specs=[ANY_SPEC] * (8 + count),
        out_specs=[ANY_SPEC] * count,
        out_shape=[jax.ShapeDtypeStruct((3, TILE, COLS), jnp.float32)] * count,
        scratch_shapes=[
            pltpu.VMEM((count, 8, 3, TILE, COLS), jnp.float32),
            pltpu.VMEM((count, 8, TILE, COLS), jnp.float32),
            pltpu.VMEM((count, 3, TILE, COLS), jnp.float32),
            pltpu.SemaphoreType.DMA((count, 8)),
            pltpu.SemaphoreType.DMA((count,)),
            pltpu.SemaphoreType.DMA((count,)),
        ],
        compiler_params=params(WEIGH),
        cost_estimate=pl.CostEstimate(
            flops=56 * count * TILE * COLS, bytes_accessed=140 * count * TILE * COLS, transcendentals=8 * count * TILE * COLS
        ),
        name="weigh",
    )(*colours, *[befores[-shift % SIDE] for shift in shifts])


def slab_kernel(*refs):
    parts, total_ref, outs = refs[:4], refs[4], refs[5:]
    grp = lax.axis_index("grp")
    for shift in range(N_GRP):
        cols = pl.ds(pl.multiple_of(((grp + shift) & 3) * STRIP, 128), STRIP)
        for ch in range(3):
            outs[shift][ch] = (parts[0][ch, :, cols] + parts[1][ch, :, cols]) + (
                parts[2][ch, :, cols] + parts[3][ch, :, cols]
            )
        outs[shift][3] = 1.0 - jnp.exp2(-total_ref[:, cols])


def slab(parts, total):
    return pl.pallas_call(
        slab_kernel,
        in_specs=[VMEM_SPEC] * 5,
        out_specs=[VMEM_SPEC] * 4,
        out_shape=[jax.ShapeDtypeStruct((4, TILE, STRIP), jnp.float32)] * 4,
        compiler_params=params(SMALL),
        name="slab",
    )(*parts, total)


def final_kernel(rank_ref, *refs):
    layers, (out_ref, stack_ref, order_ref) = refs[:4], refs[4:]
    grp = lax.axis_index("grp")
    for j in range(N_GRP):
        order_ref[rank_ref[j]] = j
    for shift in range(N_GRP):
        stack_ref[(grp - shift) & 3] = layers[shift][...]
    pic = [jnp.zeros((TILE, STRIP), jnp.float32)] * 4
    for r in range(N_GRP):
        j = order_ref[r]
        free = 1.0 - pic[3]
        pic = [pic[c] + free * stack_ref[j, c] for c in range(4)]
    for c in range(4):
        out_ref[c] = pic[c]


def final(ranks, layers):
    return pl.pallas_call(
        final_kernel,
        in_specs=[SMEM_SPEC] + [VMEM_SPEC] * 4,
        out_specs=VMEM_SPEC,
        out_shape=jax.ShapeDtypeStruct((4, TILE, STRIP), jnp.float32),
        scratch_shapes=[pltpu.VMEM((N_GRP, 4, TILE, STRIP), jnp.float32), pltpu.SMEM((N_GRP,), jnp.int32)],
        compiler_params=params(SMALL),
        name="final",
    )(ranks, *layers)


def number(y, x, core):
    return 8 * (y % SIDE) + 2 * (x % SIDE) + core


def first_pairs(swap, shift):
    out = []
    for y in range(SIDE):
        for x in range(SIDE):
            for core in range(2):
                to = 1 - core if swap else core
                goal = number(y, x + shift, to) if to == 0 else number(y + shift, x, to)
                out.append((number(y, x, core), goal))
    return out


def second_pairs(shift):
    return [
        (number(y, x, core), number(y + shift, x, 0) if core == 0 else number(y, x + shift, 1))
        for y in range(SIDE)
        for x in range(SIDE)
        for core in range(2)
    ]


def body(volume, transfer_coef, group_order, member_order, active_mask):
    view = volume.reshape(SAMPLES, N_MEM, TILE, COLS)
    raw = []

    def send(n):
        swap, shift = SENDS[n]
        return lax.ppermute(raw[n], "mem", first_pairs(swap, shift)) if swap or shift else raw[n]

    own = depth(transfer_coef, active_mask, volume.reshape(SAMPLES, ROWS, COLS))
    depths = lax.all_to_all(own.reshape(N_MEM, TILE, COLS), "mem", 0, 0, tiled=True)
    for call in CALLS:
        raw += march(transfer_coef, active_mask, view, call, raw[-1:] or [own])
    colours = [send(n) for n in range(8)]
    *befores, total = prefix(member_order, depths, raw[-1:] + [colours[0], colours[1], colours[4]])
    befores = [befores[0]] + [lax.ppermute(befores[k], "mem", second_pairs(k)) for k in range(1, SIDE)]

    shifts = (2, 1, 3)
    parts = [lax.ppermute(p, "mem", second_pairs(k)) for k, p in zip(shifts, weigh(colours, befores, shifts))]
    parts += weigh(colours, befores, (0,))
    layers = slab(parts, total)
    layers = [layers[0]] + [
        lax.ppermute(layers[s], "grp", [(g, (g + s) % N_GRP) for g in range(N_GRP)]) for s in range(1, N_GRP)
    ]
    return final(group_order, layers)


def solution(mesh):
    in_specs = (P("grp", "mem", None, None, None), P(), P(), P(), P("grp", "mem"))
    out_specs = P(None, "mem", "grp")
    return jax.shard_map(body, mesh=mesh, in_specs=in_specs, out_specs=out_specs, check_vma=False)
```

```python
import functools
import math

import jax
import jax.numpy as jnp
from jax import lax
from jax.experimental import pallas as pl
from jax.experimental.pallas import tpu as pltpu
from jax.sharding import PartitionSpec as P

SAMPLES = 8
ROWS = 512
COLS = 1024
N_GRP = 4
N_MEM = 32
SIDE = 4
TILE = ROWS // N_MEM
STRIP = COLS // N_GRP
VMEM = 50 << 20
SMALL = 24 << 20
PREFIX = 50 << 20
WEIGH = 50 << 20
DENSITY = math.sqrt(3.0 / (SAMPLES * N_GRP * N_MEM) * math.log2(math.e))


CALLS = [[(1, 1), (1, 3)], [(0, 1), (0, 3), (1, 0)], [(1, 2), (0, 2)], [(0, 0)]]
SENDS = [send for call in CALLS for send in call]

SMEM_SPEC = pl.BlockSpec(memory_space=pltpu.SMEM)
ANY_SPEC = pl.BlockSpec(memory_space=pl.ANY)
VMEM_SPEC = pl.BlockSpec(memory_space=pltpu.VMEM)
HBM_SPEC = pl.BlockSpec(memory_space=pltpu.HBM)


def params(limit=VMEM):
    return pltpu.CompilerParams(vmem_limit_bytes=limit)


def place():
    me = lax.axis_index("mem")
    return me >> 3, (me >> 1) & 3, me & 1


def cubic(q, v):
    return q[0] + v * (q[1] + v * (q[2] + v * q[3]))


def patch(i, width):
    per = COLS // width
    return pl.ds(pl.multiple_of((i // per) * 8, 8), 8), pl.ds(pl.multiple_of((i % per) * width, 128), width)


DEPTH_ROWS = 64
DEPTH_STEPS = ROWS // DEPTH_ROWS
DEPTH_SLOTS = 4


def depth_kernel(coef_ref, flag_ref, vol_ref, *refs):
    out_ref, inbuf, outbuf, insem, outsem = refs[-5:]
    q = [coef_ref[3, k] * DENSITY for k in range(4)]
    flag = flag_ref[0, 0].astype(jnp.float32)
    width = 512

    def fetch(i):
        return pltpu.make_async_copy(
            vol_ref.at[:, pl.ds(i * DEPTH_ROWS, DEPTH_ROWS), :], inbuf.at[i % DEPTH_SLOTS], insem.at[i % DEPTH_SLOTS]
        )

    def store(i):
        return pltpu.make_async_copy(outbuf.at[i % 2], out_ref.at[pl.ds(i * DEPTH_ROWS, DEPTH_ROWS), :], outsem.at[i % 2])

    for i in range(DEPTH_SLOTS):
        fetch(i).start()
    for i in range(DEPTH_STEPS):
        fetch(i).wait()
        if i >= 2:
            store(i - 2).wait()

        def step(n, carry, i=i):
            block, cols = patch(n, width)
            total = None
            for s in range(SAMPLES):
                d = cubic(q, inbuf[i % DEPTH_SLOTS, s, block, cols])
                total = d * d if total is None else total + d * d
            outbuf[i % 2, block, cols] = total * flag
            return carry

        lax.fori_loop(0, (DEPTH_ROWS // 8) * (COLS // width), step, 0, unroll=4)
        store(i).start()
        if i + DEPTH_SLOTS < DEPTH_STEPS:
            fetch(i + DEPTH_SLOTS).start()
    for i in range(DEPTH_STEPS - 2, DEPTH_STEPS):
        store(i).wait()


def depth(coef, flag, volume):
    return pl.pallas_call(
        depth_kernel,
        in_specs=[SMEM_SPEC, SMEM_SPEC, HBM_SPEC],
        out_specs=ANY_SPEC,
        out_shape=jax.ShapeDtypeStruct((ROWS, COLS), jnp.float32),
        scratch_shapes=[
            pltpu.VMEM((DEPTH_SLOTS, SAMPLES, DEPTH_ROWS, COLS), jnp.float32),
            pltpu.VMEM((2, DEPTH_ROWS, COLS), jnp.float32),
            pltpu.SemaphoreType.DMA((DEPTH_SLOTS,)),
            pltpu.SemaphoreType.DMA((2,)),
        ],
        compiler_params=params(60 << 20),
        cost_estimate=pl.CostEstimate(flops=8 * SAMPLES * ROWS * COLS, bytes_accessed=36 * ROWS * COLS, transcendentals=0),
        name="depth",
    )(coef, flag, volume)


def march_kernel(coef_ref, flag_ref, vol_ref, *refs, call):
    count = len(call)
    outs, (inbuf, outbuf, insem, outsem) = refs[-4 - count:-4], refs[-4:]
    y, x, core = place()
    q = [[coef_ref[c, k] * (DENSITY if c == 3 else 0.5) for k in range(4)] for c in range(4)]
    half = 0.5 * flag_ref[0, 0].astype(jnp.float32)

    def fetch(k, i):
        swap, shift = call[k]
        to = 1 - core if swap else core
        along_x = 2 * ((x + shift) & 3) + 8 * i
        along_y = 8 * ((y + shift) & 3) + 2 * i + 1
        tile = jnp.where(to == 0, along_x, along_y)
        return pltpu.make_async_copy(vol_ref.at[:, tile], inbuf.at[k, i], insem.at[k, i])

    def store(k, i):
        return pltpu.make_async_copy(outbuf.at[k, i], outs[k].at[i], outsem.at[k, i])

    every = [(k, i) for k in range(count) for i in range(SIDE)]
    for k, i in every:
        fetch(k, i).start()
    for k in range(count):

        def tile_step(i, carry, k=k):
            fetch(k, i).wait()

            def step(n, carry):
                block = pl.ds(pl.multiple_of(n * 8, 8), 8)
                depth = clear = None
                acc = [None] * 3
                for s in range(SAMPLES):
                    v = inbuf[k, i, s, block, :]
                    d = cubic(q[3], v)
                    depth = -(d * d) if depth is None else depth - d * d
                    ahead = jnp.exp2(depth)
                    weight = 1.0 - ahead if clear is None else clear - ahead
                    clear = ahead
                    for ch in range(3):
                        term = weight * jnp.tanh(cubic(q[ch], v))
                        acc[ch] = term if acc[ch] is None else acc[ch] + term
                cover = 1.0 - clear
                for ch in range(3):
                    outbuf[k, i, ch, block, :] = (acc[ch] + cover) * half
                return carry

            lax.fori_loop(0, TILE // 8, step, 0)
            store(k, i).start()
            return carry

        lax.fori_loop(0, SIDE, tile_step, 0)
    for k, i in every:
        store(k, i).wait()


def march(coef, flag, view, call, after):
    tiles = SIDE * len(call)
    pixels = tiles * TILE * COLS
    return pl.pallas_call(
        functools.partial(march_kernel, call=call),
        in_specs=[SMEM_SPEC, SMEM_SPEC, HBM_SPEC] + [ANY_SPEC] * len(after),
        out_specs=[ANY_SPEC] * len(call),
        out_shape=[jax.ShapeDtypeStruct((SIDE, 3, TILE, COLS), jnp.float32)] * len(call),
        scratch_shapes=[
            pltpu.VMEM((len(call), SIDE, SAMPLES, TILE, COLS), jnp.float32),
            pltpu.VMEM((len(call), SIDE, 3, TILE, COLS), jnp.float32),
            pltpu.SemaphoreType.DMA((len(call), SIDE)),
            pltpu.SemaphoreType.DMA((len(call), SIDE)),
        ],
        compiler_params=params(),
        cost_estimate=pl.CostEstimate(
            flops=40 * SAMPLES * pixels, bytes_accessed=44 * pixels, transcendentals=4 * SAMPLES * pixels
        ),
        name="march",
    )(coef, flag, view, *after)


def prefix_kernel(rank_ref, depth_ref, *refs):
    outs, (total_ref, buf, order_ref, sem) = refs[-8:-4], refs[-4:]
    grp = lax.axis_index("grp")
    y, x, core = place()
    second = jnp.where(core == 0, y, x)
    for j in range(N_MEM):
        order_ref[rank_ref[grp, j]] = j

    def strip(i, carry):
        cols = pl.ds(pl.multiple_of(i * STRIP, 128), STRIP)

        def step(r, running):
            j = order_ref[r]
            across = 8 * ((j >> 1) & 3) + 2 * (j >> 3) + (j & 1)
            spot = jnp.where(core == 0, j, across)
            buf[spot >> 3, spot & 7, :, cols] = running
            return running + depth_ref[j, :, cols]

        total_ref[:, cols] = lax.fori_loop(0, N_MEM, step, jnp.zeros((TILE, STRIP), jnp.float32), unroll=4)
        return carry

    lax.fori_loop(0, COLS // STRIP, strip, 0)
    copies = [pltpu.make_async_copy(buf.at[(second + k) & 3], outs[k], sem.at[k]) for k in range(SIDE)]
    for copy in copies:
        copy.start()
    for copy in copies:
        copy.wait()


def prefix(ranks, depths, after):
    line = jax.ShapeDtypeStruct((8, TILE, COLS), jnp.float32)
    return pl.pallas_call(
        prefix_kernel,
        in_specs=[SMEM_SPEC, VMEM_SPEC] + [ANY_SPEC] * len(after),
        out_specs=[ANY_SPEC] * SIDE + [VMEM_SPEC],
        out_shape=[line] * SIDE + [jax.ShapeDtypeStruct((TILE, COLS), jnp.float32)],
        scratch_shapes=[
            pltpu.VMEM((SIDE, 8, TILE, COLS), jnp.float32),
            pltpu.SMEM((N_MEM,), jnp.int32),
            pltpu.SemaphoreType.DMA((SIDE,)),
        ],
        compiler_params=params(PREFIX),
        cost_estimate=pl.CostEstimate(
            flops=N_MEM * TILE * COLS, bytes_accessed=8 * N_MEM * TILE * COLS, transcendentals=0
        ),
        name="prefix",
    )(ranks, depths, *after)


def weigh_kernel(*refs, shifts):
    count = len(shifts)
    colours, befores, outs = refs[:8], refs[8:8 + count], refs[8 + count:8 + 2 * count]
    colbuf, depbuf, outbuf, colsem, depsem, outsem = refs[8 + 2 * count:]
    y, x, core = place()
    first, second = jnp.where(core == 0, x, y), jnp.where(core == 0, y, x)

    def fetch(i):
        spot = (second + shifts[i]) & 3
        return [pltpu.make_async_copy(befores[i], depbuf.at[i], depsem.at[i])] + [
            pltpu.make_async_copy(colours[n].at[spot], colbuf.at[i, n], colsem.at[i, n]) for n in range(8)
        ]

    def store(i):
        return pltpu.make_async_copy(outbuf.at[i], outs[i], outsem.at[i])

    slots = [2 * ((first - shift) & 3) + (1 - core if swap else core) for swap, shift in SENDS]
    for i in range(count):
        for copy in fetch(i):
            copy.start()
    for i in range(count):
        for copy in fetch(i):
            copy.wait()

        def step(n, carry, i=i):
            block, cols = patch(n, 256)
            acc = [None] * 3
            for k in range(8):
                light = jnp.exp2(-depbuf[i, slots[k], block, cols])
                for ch in range(3):
                    term = light * colbuf[i, k, ch, block, cols]
                    acc[ch] = term if acc[ch] is None else acc[ch] + term
            for ch in range(3):
                outbuf[i, ch, block, cols] = acc[ch]
            return carry

        lax.fori_loop(0, 8, step, 0)
        store(i).start()
    for i in range(count):
        store(i).wait()


def weigh(colours, befores, shifts):
    count = len(shifts)
    return pl.pallas_call(
        functools.partial(weigh_kernel, shifts=shifts),
        in_specs=[ANY_SPEC] * (8 + count),
        out_specs=[ANY_SPEC] * count,
        out_shape=[jax.ShapeDtypeStruct((3, TILE, COLS), jnp.float32)] * count,
        scratch_shapes=[
            pltpu.VMEM((count, 8, 3, TILE, COLS), jnp.float32),
            pltpu.VMEM((count, 8, TILE, COLS), jnp.float32),
            pltpu.VMEM((count, 3, TILE, COLS), jnp.float32),
            pltpu.SemaphoreType.DMA((count, 8)),
            pltpu.SemaphoreType.DMA((count,)),
            pltpu.SemaphoreType.DMA((count,)),
        ],
        compiler_params=params(WEIGH),
        cost_estimate=pl.CostEstimate(
            flops=56 * count * TILE * COLS, bytes_accessed=140 * count * TILE * COLS, transcendentals=8 * count * TILE * COLS
        ),
        name="weigh",
    )(*colours, *[befores[-shift % SIDE] for shift in shifts])


def slab_kernel(*refs):
    parts, total_ref, outs = refs[:4], refs[4], refs[5:]
    grp = lax.axis_index("grp")
    for shift in range(N_GRP):
        cols = pl.ds(pl.multiple_of(((grp + shift) & 3) * STRIP, 128), STRIP)
        for ch in range(3):
            outs[shift][ch] = (parts[0][ch, :, cols] + parts[1][ch, :, cols]) + (
                parts[2][ch, :, cols] + parts[3][ch, :, cols]
            )
        outs[shift][3] = 1.0 - jnp.exp2(-total_ref[:, cols])


def slab(parts, total):
    return pl.pallas_call(
        slab_kernel,
        in_specs=[VMEM_SPEC] * 5,
        out_specs=[VMEM_SPEC] * 4,
        out_shape=[jax.ShapeDtypeStruct((4, TILE, STRIP), jnp.float32)] * 4,
        compiler_params=params(SMALL),
        name="slab",
    )(*parts, total)


def final_kernel(rank_ref, *refs):
    layers, (out_ref, stack_ref, order_ref) = refs[:4], refs[4:]
    grp = lax.axis_index("grp")
    for j in range(N_GRP):
        order_ref[rank_ref[j]] = j
    for shift in range(N_GRP):
        stack_ref[(grp - shift) & 3] = layers[shift][...]
    pic = [jnp.zeros((TILE, STRIP), jnp.float32)] * 4
    for r in range(N_GRP):
        j = order_ref[r]
        free = 1.0 - pic[3]
        pic = [pic[c] + free * stack_ref[j, c] for c in range(4)]
    for c in range(4):
        out_ref[c] = pic[c]


def final(ranks, layers):
    return pl.pallas_call(
        final_kernel,
        in_specs=[SMEM_SPEC] + [VMEM_SPEC] * 4,
        out_specs=VMEM_SPEC,
        out_shape=jax.ShapeDtypeStruct((4, TILE, STRIP), jnp.float32),
        scratch_shapes=[pltpu.VMEM((N_GRP, 4, TILE, STRIP), jnp.float32), pltpu.SMEM((N_GRP,), jnp.int32)],
        compiler_params=params(SMALL),
        name="final",
    )(ranks, *layers)


def number(y, x, core):
    return 8 * (y % SIDE) + 2 * (x % SIDE) + core


def first_pairs(swap, shift):
    out = []
    for y in range(SIDE):
        for x in range(SIDE):
            for core in range(2):
                to = 1 - core if swap else core
                goal = number(y, x + shift, to) if to == 0 else number(y + shift, x, to)
                out.append((number(y, x, core), goal))
    return out


def second_pairs(shift):
    return [
        (number(y, x, core), number(y + shift, x, 0) if core == 0 else number(y, x + shift, 1))
        for y in range(SIDE)
        for x in range(SIDE)
        for core in range(2)
    ]


def body(volume, transfer_coef, group_order, member_order, active_mask):
    view = volume.reshape(SAMPLES, N_MEM, TILE, COLS)
    raw = []

    def send(n):
        swap, shift = SENDS[n]
        return lax.ppermute(raw[n], "mem", first_pairs(swap, shift)) if swap or shift else raw[n]

    own = depth(transfer_coef, active_mask, volume.reshape(SAMPLES, ROWS, COLS))
    depths = lax.all_to_all(own.reshape(N_MEM, TILE, COLS), "mem", 0, 0, tiled=True)
    for call in CALLS:
        raw += march(transfer_coef, active_mask, view, call, raw[-1:] or [own])
    colours = [send(n) for n in range(8)]
    *befores, total = prefix(member_order, depths, raw[-1:] + [colours[0], colours[1], colours[4]])
    befores = [befores[0]] + [lax.ppermute(befores[k], "mem", second_pairs(k)) for k in range(1, SIDE)]

    parts = weigh(colours, befores, (2, 1, 3, 0))
    parts = [lax.ppermute(p, "mem", second_pairs(k)) for k, p in zip((2, 1, 3), parts)] + list(parts[3:])
    layers = slab(parts, total)
    layers = [layers[0]] + [
        lax.ppermute(layers[s], "grp", [(g, (g + s) % N_GRP) for g in range(N_GRP)]) for s in range(1, N_GRP)
    ]
    return final(group_order, layers)


def solution(mesh):
    in_specs = (P("grp", "mem", None, None, None), P(), P(), P(), P("grp", "mem"))
    out_specs = P(None, "mem", "grp")
    return jax.shard_map(body, mesh=mesh, in_specs=in_specs, out_specs=out_specs, check_vma=False)
```

```python
import functools
import math

import jax
import jax.numpy as jnp
from jax import lax
from jax.experimental import pallas as pl
from jax.experimental.pallas import tpu as pltpu
from jax.sharding import PartitionSpec as P

SAMPLES = 8
ROWS = 512
COLS = 1024
N_GRP = 4
N_MEM = 32
SIDE = 4
TILE = ROWS // N_MEM
STRIP = COLS // N_GRP
VMEM = 50 << 20
SMALL = 24 << 20
PREFIX = 50 << 20
WEIGH = 50 << 20
DENSITY = math.sqrt(3.0 / (SAMPLES * N_GRP * N_MEM) * math.log2(math.e))


CALLS = [[(1, 1), (1, 3)], [(0, 1), (0, 3), (1, 0)], [(0, 0)], [(1, 2), (0, 2)]]
SENDS = [send for call in CALLS for send in call]

SMEM_SPEC = pl.BlockSpec(memory_space=pltpu.SMEM)
ANY_SPEC = pl.BlockSpec(memory_space=pl.ANY)
VMEM_SPEC = pl.BlockSpec(memory_space=pltpu.VMEM)
HBM_SPEC = pl.BlockSpec(memory_space=pltpu.HBM)


def params(limit=VMEM):
    return pltpu.CompilerParams(vmem_limit_bytes=limit)


def place():
    me = lax.axis_index("mem")
    return me >> 3, (me >> 1) & 3, me & 1


def cubic(q, v):
    return q[0] + v * (q[1] + v * (q[2] + v * q[3]))


def patch(i, width):
    per = COLS // width
    return pl.ds(pl.multiple_of((i // per) * 8, 8), 8), pl.ds(pl.multiple_of((i % per) * width, 128), width)


DEPTH_ROWS = 64
DEPTH_STEPS = ROWS // DEPTH_ROWS
DEPTH_SLOTS = 4


def depth_kernel(coef_ref, flag_ref, vol_ref, *refs):
    out_ref, inbuf, outbuf, insem, outsem = refs[-5:]
    q = [coef_ref[3, k] * DENSITY for k in range(4)]
    flag = flag_ref[0, 0].astype(jnp.float32)
    width = 512

    def fetch(i):
        return pltpu.make_async_copy(
            vol_ref.at[:, pl.ds(i * DEPTH_ROWS, DEPTH_ROWS), :], inbuf.at[i % DEPTH_SLOTS], insem.at[i % DEPTH_SLOTS]
        )

    def store(i):
        return pltpu.make_async_copy(outbuf.at[i % 2], out_ref.at[pl.ds(i * DEPTH_ROWS, DEPTH_ROWS), :], outsem.at[i % 2])

    for i in range(DEPTH_SLOTS):
        fetch(i).start()
    for i in range(DEPTH_STEPS):
        fetch(i).wait()
        if i >= 2:
            store(i - 2).wait()

        def step(n, carry, i=i):
            block, cols = patch(n, width)
            total = None
            for s in range(SAMPLES):
                d = cubic(q, inbuf[i % DEPTH_SLOTS, s, block, cols])
                total = d * d if total is None else total + d * d
            outbuf[i % 2, block, cols] = total * flag
            return carry

        lax.fori_loop(0, (DEPTH_ROWS // 8) * (COLS // width), step, 0, unroll=4)
        store(i).start()
        if i + DEPTH_SLOTS < DEPTH_STEPS:
            fetch(i + DEPTH_SLOTS).start()
    for i in range(DEPTH_STEPS - 2, DEPTH_STEPS):
        store(i).wait()


def depth(coef, flag, volume):
    return pl.pallas_call(
        depth_kernel,
        in_specs=[SMEM_SPEC, SMEM_SPEC, HBM_SPEC],
        out_specs=ANY_SPEC,
        out_shape=jax.ShapeDtypeStruct((ROWS, COLS), jnp.float32),
        scratch_shapes=[
            pltpu.VMEM((DEPTH_SLOTS, SAMPLES, DEPTH_ROWS, COLS), jnp.float32),
            pltpu.VMEM((2, DEPTH_ROWS, COLS), jnp.float32),
            pltpu.SemaphoreType.DMA((DEPTH_SLOTS,)),
            pltpu.SemaphoreType.DMA((2,)),
        ],
        compiler_params=params(60 << 20),
        cost_estimate=pl.CostEstimate(flops=8 * SAMPLES * ROWS * COLS, bytes_accessed=36 * ROWS * COLS, transcendentals=0),
        name="depth",
    )(coef, flag, volume)


def march_kernel(coef_ref, flag_ref, vol_ref, *refs, call):
    count = len(call)
    outs, (inbuf, outbuf, insem, outsem) = refs[-4 - count:-4], refs[-4:]
    y, x, core = place()
    q = [[coef_ref[c, k] * (DENSITY if c == 3 else 0.5) for k in range(4)] for c in range(4)]
    half = 0.5 * flag_ref[0, 0].astype(jnp.float32)

    def fetch(k, i):
        swap, shift = call[k]
        to = 1 - core if swap else core
        along_x = 2 * ((x + shift) & 3) + 8 * i
        along_y = 8 * ((y + shift) & 3) + 2 * i + 1
        tile = jnp.where(to == 0, along_x, along_y)
        return pltpu.make_async_copy(vol_ref.at[:, tile], inbuf.at[k, i], insem.at[k, i])

    def store(k, i):
        return pltpu.make_async_copy(outbuf.at[k, i], outs[k].at[i], outsem.at[k, i])

    every = [(k, i) for k in range(count) for i in range(SIDE)]
    for k, i in every:
        fetch(k, i).start()
    for k in range(count):

        def tile_step(i, carry, k=k):
            fetch(k, i).wait()

            def step(n, carry):
                block = pl.ds(pl.multiple_of(n * 8, 8), 8)
                depth = clear = None
                acc = [None] * 3
                for s in range(SAMPLES):
                    v = inbuf[k, i, s, block, :]
                    d = cubic(q[3], v)
                    depth = -(d * d) if depth is None else depth - d * d
                    ahead = jnp.exp2(depth)
                    weight = 1.0 - ahead if clear is None else clear - ahead
                    clear = ahead
                    for ch in range(3):
                        term = weight * jnp.tanh(cubic(q[ch], v))
                        acc[ch] = term if acc[ch] is None else acc[ch] + term
                cover = 1.0 - clear
                for ch in range(3):
                    outbuf[k, i, ch, block, :] = (acc[ch] + cover) * half
                return carry

            lax.fori_loop(0, TILE // 8, step, 0)
            store(k, i).start()
            return carry

        lax.fori_loop(0, SIDE, tile_step, 0)
    for k, i in every:
        store(k, i).wait()


def march(coef, flag, view, call, after):
    tiles = SIDE * len(call)
    pixels = tiles * TILE * COLS
    return pl.pallas_call(
        functools.partial(march_kernel, call=call),
        in_specs=[SMEM_SPEC, SMEM_SPEC, HBM_SPEC] + [ANY_SPEC] * len(after),
        out_specs=[ANY_SPEC] * len(call),
        out_shape=[jax.ShapeDtypeStruct((SIDE, 3, TILE, COLS), jnp.float32)] * len(call),
        scratch_shapes=[
            pltpu.VMEM((len(call), SIDE, SAMPLES, TILE, COLS), jnp.float32),
            pltpu.VMEM((len(call), SIDE, 3, TILE, COLS), jnp.float32),
            pltpu.SemaphoreType.DMA((len(call), SIDE)),
            pltpu.SemaphoreType.DMA((len(call), SIDE)),
        ],
        compiler_params=params(),
        cost_estimate=pl.CostEstimate(
            flops=40 * SAMPLES * pixels, bytes_accessed=44 * pixels, transcendentals=4 * SAMPLES * pixels
        ),
        name="march",
    )(coef, flag, view, *after)


def prefix_kernel(rank_ref, depth_ref, *refs):
    outs, (total_ref, buf, order_ref, sem) = refs[-8:-4], refs[-4:]
    grp = lax.axis_index("grp")
    y, x, core = place()
    second = jnp.where(core == 0, y, x)
    for j in range(N_MEM):
        order_ref[rank_ref[grp, j]] = j

    def strip(i, carry):
        cols = pl.ds(pl.multiple_of(i * STRIP, 128), STRIP)

        def step(r, running):
            j = order_ref[r]
            across = 8 * ((j >> 1) & 3) + 2 * (j >> 3) + (j & 1)
            spot = jnp.where(core == 0, j, across)
            buf[spot >> 3, spot & 7, :, cols] = running
            return running + depth_ref[j, :, cols]

        total_ref[:, cols] = lax.fori_loop(0, N_MEM, step, jnp.zeros((TILE, STRIP), jnp.float32), unroll=4)
        return carry

    lax.fori_loop(0, COLS // STRIP, strip, 0)
    copies = [pltpu.make_async_copy(buf.at[(second + k) & 3], outs[k], sem.at[k]) for k in range(SIDE)]
    for copy in copies:
        copy.start()
    for copy in copies:
        copy.wait()


def prefix(ranks, depths, after):
    line = jax.ShapeDtypeStruct((8, TILE, COLS), jnp.float32)
    return pl.pallas_call(
        prefix_kernel,
        in_specs=[SMEM_SPEC, VMEM_SPEC] + [ANY_SPEC] * len(after),
        out_specs=[ANY_SPEC] * SIDE + [VMEM_SPEC],
        out_shape=[line] * SIDE + [jax.ShapeDtypeStruct((TILE, COLS), jnp.float32)],
        scratch_shapes=[
            pltpu.VMEM((SIDE, 8, TILE, COLS), jnp.float32),
            pltpu.SMEM((N_MEM,), jnp.int32),
            pltpu.SemaphoreType.DMA((SIDE,)),
        ],
        compiler_params=params(PREFIX),
        cost_estimate=pl.CostEstimate(
            flops=N_MEM * TILE * COLS, bytes_accessed=8 * N_MEM * TILE * COLS, transcendentals=0
        ),
        name="prefix",
    )(ranks, depths, *after)


def weigh_kernel(*refs, shifts):
    count = len(shifts)
    colours, befores, outs = refs[:8], refs[8:8 + count], refs[8 + count:8 + 2 * count]
    colbuf, depbuf, outbuf, colsem, depsem, outsem = refs[8 + 2 * count:]
    y, x, core = place()
    first, second = jnp.where(core == 0, x, y), jnp.where(core == 0, y, x)

    def fetch(i):
        spot = (second + shifts[i]) & 3
        return [pltpu.make_async_copy(befores[i], depbuf.at[i], depsem.at[i])] + [
            pltpu.make_async_copy(colours[n].at[spot], colbuf.at[i, n], colsem.at[i, n]) for n in range(8)
        ]

    def store(i):
        return pltpu.make_async_copy(outbuf.at[i], outs[i], outsem.at[i])

    slots = [2 * ((first - shift) & 3) + (1 - core if swap else core) for swap, shift in SENDS]
    for i in range(count):
        for copy in fetch(i):
            copy.start()
    for i in range(count):
        for copy in fetch(i):
            copy.wait()

        def step(n, carry, i=i):
            block, cols = patch(n, 256)
            acc = [None] * 3
            for k in range(8):
                light = jnp.exp2(-depbuf[i, slots[k], block, cols])
                for ch in range(3):
                    term = light * colbuf[i, k, ch, block, cols]
                    acc[ch] = term if acc[ch] is None else acc[ch] + term
            for ch in range(3):
                outbuf[i, ch, block, cols] = acc[ch]
            return carry

        lax.fori_loop(0, 8, step, 0)
        store(i).start()
    for i in range(count):
        store(i).wait()


def weigh(colours, befores, shifts):
    count = len(shifts)
    return pl.pallas_call(
        functools.partial(weigh_kernel, shifts=shifts),
        in_specs=[ANY_SPEC] * (8 + count),
        out_specs=[ANY_SPEC] * count,
        out_shape=[jax.ShapeDtypeStruct((3, TILE, COLS), jnp.float32)] * count,
        scratch_shapes=[
            pltpu.VMEM((count, 8, 3, TILE, COLS), jnp.float32),
            pltpu.VMEM((count, 8, TILE, COLS), jnp.float32),
            pltpu.VMEM((count, 3, TILE, COLS), jnp.float32),
            pltpu.SemaphoreType.DMA((count, 8)),
            pltpu.SemaphoreType.DMA((count,)),
            pltpu.SemaphoreType.DMA((count,)),
        ],
        compiler_params=params(WEIGH),
        cost_estimate=pl.CostEstimate(
            flops=56 * count * TILE * COLS, bytes_accessed=140 * count * TILE * COLS, transcendentals=8 * count * TILE * COLS
        ),
        name="weigh",
    )(*colours, *[befores[-shift % SIDE] for shift in shifts])


def slab_kernel(*refs):
    parts, total_ref, outs = refs[:4], refs[4], refs[5:]
    grp = lax.axis_index("grp")
    for shift in range(N_GRP):
        cols = pl.ds(pl.multiple_of(((grp + shift) & 3) * STRIP, 128), STRIP)
        for ch in range(3):
            outs[shift][ch] = (parts[0][ch, :, cols] + parts[1][ch, :, cols]) + (
                parts[2][ch, :, cols] + parts[3][ch, :, cols]
            )
        outs[shift][3] = 1.0 - jnp.exp2(-total_ref[:, cols])


def slab(parts, total):
    return pl.pallas_call(
        slab_kernel,
        in_specs=[VMEM_SPEC] * 5,
        out_specs=[VMEM_SPEC] * 4,
        out_shape=[jax.ShapeDtypeStruct((4, TILE, STRIP), jnp.float32)] * 4,
        compiler_params=params(SMALL),
        name="slab",
    )(*parts, total)


def final_kernel(rank_ref, *refs):
    layers, (out_ref, stack_ref, order_ref) = refs[:4], refs[4:]
    grp = lax.axis_index("grp")
    for j in range(N_GRP):
        order_ref[rank_ref[j]] = j
    for shift in range(N_GRP):
        stack_ref[(grp - shift) & 3] = layers[shift][...]
    pic = [jnp.zeros((TILE, STRIP), jnp.float32)] * 4
    for r in range(N_GRP):
        j = order_ref[r]
        free = 1.0 - pic[3]
        pic = [pic[c] + free * stack_ref[j, c] for c in range(4)]
    for c in range(4):
        out_ref[c] = pic[c]


def final(ranks, layers):
    return pl.pallas_call(
        final_kernel,
        in_specs=[SMEM_SPEC] + [VMEM_SPEC] * 4,
        out_specs=VMEM_SPEC,
        out_shape=jax.ShapeDtypeStruct((4, TILE, STRIP), jnp.float32),
        scratch_shapes=[pltpu.VMEM((N_GRP, 4, TILE, STRIP), jnp.float32), pltpu.SMEM((N_GRP,), jnp.int32)],
        compiler_params=params(SMALL),
        name="final",
    )(ranks, *layers)


def number(y, x, core):
    return 8 * (y % SIDE) + 2 * (x % SIDE) + core


def first_pairs(swap, shift):
    out = []
    for y in range(SIDE):
        for x in range(SIDE):
            for core in range(2):
                to = 1 - core if swap else core
                goal = number(y, x + shift, to) if to == 0 else number(y + shift, x, to)
                out.append((number(y, x, core), goal))
    return out


def second_pairs(shift):
    return [
        (number(y, x, core), number(y + shift, x, 0) if core == 0 else number(y, x + shift, 1))
        for y in range(SIDE)
        for x in range(SIDE)
        for core in range(2)
    ]


def body(volume, transfer_coef, group_order, member_order, active_mask):
    view = volume.reshape(SAMPLES, N_MEM, TILE, COLS)
    raw = []

    def send(n):
        swap, shift = SENDS[n]
        return lax.ppermute(raw[n], "mem", first_pairs(swap, shift)) if swap or shift else raw[n]

    own = depth(transfer_coef, active_mask, volume.reshape(SAMPLES, ROWS, COLS))
    depths = lax.all_to_all(own.reshape(N_MEM, TILE, COLS), "mem", 0, 0, tiled=True)
    for call in CALLS:
        raw += march(transfer_coef, active_mask, view, call, raw[-1:] or [own])
    colours = [send(n) for n in range(8)]
    *befores, total = prefix(member_order, depths, raw[-1:] + [colours[0], colours[1], colours[4]])
    befores = [befores[0]] + [lax.ppermute(befores[k], "mem", second_pairs(k)) for k in range(1, SIDE)]

    parts = weigh(colours, befores, (2, 1, 3, 0))
    parts = [lax.ppermute(p, "mem", second_pairs(k)) for k, p in zip((2, 1, 3), parts)] + list(parts[3:])
    layers = slab(parts, total)
    layers = [layers[0]] + [
        lax.ppermute(layers[s], "grp", [(g, (g + s) % N_GRP) for g in range(N_GRP)]) for s in range(1, N_GRP)
    ]
    return final(group_order, layers)


def solution(mesh):
    in_specs = (P("grp", "mem", None, None, None), P(), P(), P(), P("grp", "mem"))
    out_specs = P(None, "mem", "grp")
    return jax.shard_map(body, mesh=mesh, in_specs=in_specs, out_specs=out_specs, check_vma=False)
```

```python
import functools
import math

import jax
import jax.numpy as jnp
from jax import lax
from jax.experimental import pallas as pl
from jax.experimental.pallas import tpu as pltpu
from jax.sharding import PartitionSpec as P

SAMPLES = 8
ROWS = 512
COLS = 1024
N_GRP = 4
N_MEM = 32
SIDE = 4
TILE = ROWS // N_MEM
STRIP = COLS // N_GRP
VMEM = 50 << 20
SMALL = 24 << 20
PREFIX = 50 << 20
WEIGH = 50 << 20
DENSITY = math.sqrt(3.0 / (SAMPLES * N_GRP * N_MEM) * math.log2(math.e))


CALLS = [[(1, 1), (1, 3)], [(0, 1), (0, 3), (1, 0)], [(1, 2), (0, 2)], [(0, 0)]]
SENDS = [send for call in CALLS for send in call]

SMEM_SPEC = pl.BlockSpec(memory_space=pltpu.SMEM)
ANY_SPEC = pl.BlockSpec(memory_space=pl.ANY)
VMEM_SPEC = pl.BlockSpec(memory_space=pltpu.VMEM)
HBM_SPEC = pl.BlockSpec(memory_space=pltpu.HBM)


def params(limit=VMEM):
    return pltpu.CompilerParams(vmem_limit_bytes=limit)


def place():
    me = lax.axis_index("mem")
    return me >> 3, (me >> 1) & 3, me & 1


def cubic(q, v):
    return q[0] + v * (q[1] + v * (q[2] + v * q[3]))


def patch(i, width):
    per = COLS // width
    return pl.ds(pl.multiple_of((i // per) * 8, 8), 8), pl.ds(pl.multiple_of((i % per) * width, 128), width)


DEPTH_ROWS = 64
DEPTH_STEPS = ROWS // DEPTH_ROWS
DEPTH_SLOTS = 4


def depth_kernel(coef_ref, flag_ref, vol_ref, *refs):
    out_ref, inbuf, outbuf, insem, outsem = refs[-5:]
    q = [coef_ref[3, k] * DENSITY for k in range(4)]
    flag = flag_ref[0, 0].astype(jnp.float32)
    width = 512

    def fetch(i):
        return pltpu.make_async_copy(
            vol_ref.at[:, pl.ds(i * DEPTH_ROWS, DEPTH_ROWS), :], inbuf.at[i % DEPTH_SLOTS], insem.at[i % DEPTH_SLOTS]
        )

    def store(i):
        return pltpu.make_async_copy(outbuf.at[i % 2], out_ref.at[pl.ds(i * DEPTH_ROWS, DEPTH_ROWS), :], outsem.at[i % 2])

    for i in range(DEPTH_SLOTS):
        fetch(i).start()
    for i in range(DEPTH_STEPS):
        fetch(i).wait()
        if i >= 2:
            store(i - 2).wait()

        def step(n, carry, i=i):
            block, cols = patch(n, width)
            total = None
            for s in range(SAMPLES):
                d = cubic(q, inbuf[i % DEPTH_SLOTS, s, block, cols])
                total = d * d if total is None else total + d * d
            outbuf[i % 2, block, cols] = total * flag
            return carry

        lax.fori_loop(0, (DEPTH_ROWS // 8) * (COLS // width), step, 0, unroll=4)
        store(i).start()
        if i + DEPTH_SLOTS < DEPTH_STEPS:
            fetch(i + DEPTH_SLOTS).start()
    for i in range(DEPTH_STEPS - 2, DEPTH_STEPS):
        store(i).wait()


def depth(coef, flag, volume):
    return pl.pallas_call(
        depth_kernel,
        in_specs=[SMEM_SPEC, SMEM_SPEC, HBM_SPEC],
        out_specs=ANY_SPEC,
        out_shape=jax.ShapeDtypeStruct((ROWS, COLS), jnp.float32),
        scratch_shapes=[
            pltpu.VMEM((DEPTH_SLOTS, SAMPLES, DEPTH_ROWS, COLS), jnp.float32),
            pltpu.VMEM((2, DEPTH_ROWS, COLS), jnp.float32),
            pltpu.SemaphoreType.DMA((DEPTH_SLOTS,)),
            pltpu.SemaphoreType.DMA((2,)),
        ],
        compiler_params=params(60 << 20),
        cost_estimate=pl.CostEstimate(flops=8 * SAMPLES * ROWS * COLS, bytes_accessed=36 * ROWS * COLS, transcendentals=0),
        name="depth",
    )(coef, flag, volume)


def march_kernel(coef_ref, flag_ref, vol_ref, *refs, call):
    count = len(call)
    outs, (inbuf, outbuf, insem, outsem) = refs[-4 - count:-4], refs[-4:]
    y, x, core = place()
    q = [[coef_ref[c, k] * (DENSITY if c == 3 else 0.5) for k in range(4)] for c in range(4)]
    half = 0.5 * flag_ref[0, 0].astype(jnp.float32)

    def fetch(k, i):
        swap, shift = call[k]
        to = 1 - core if swap else core
        along_x = 2 * ((x + shift) & 3) + 8 * i
        along_y = 8 * ((y + shift) & 3) + 2 * i + 1
        tile = jnp.where(to == 0, along_x, along_y)
        return pltpu.make_async_copy(vol_ref.at[:, tile], inbuf.at[k, i], insem.at[k, i])

    def store(k, i):
        return pltpu.make_async_copy(outbuf.at[k, i], outs[k].at[i], outsem.at[k, i])

    every = [(k, i) for k in range(count) for i in range(SIDE)]
    for k, i in every:
        fetch(k, i).start()
    for k in range(count):

        def tile_step(i, carry, k=k):
            fetch(k, i).wait()

            def step(n, carry):
                block = pl.ds(pl.multiple_of(n * 8, 8), 8)
                depth = clear = None
                acc = [None] * 3
                for s in range(SAMPLES):
                    v = inbuf[k, i, s, block, :]
                    d = cubic(q[3], v)
                    depth = -(d * d) if depth is None else depth - d * d
                    ahead = jnp.exp2(depth)
                    weight = 1.0 - ahead if clear is None else clear - ahead
                    clear = ahead
                    for ch in range(3):
                        term = weight * jnp.tanh(cubic(q[ch], v))
                        acc[ch] = term if acc[ch] is None else acc[ch] + term
                cover = 1.0 - clear
                for ch in range(3):
                    outbuf[k, i, ch, block, :] = (acc[ch] + cover) * half
                return carry

            lax.fori_loop(0, TILE // 8, step, 0)
            store(k, i).start()
            return carry

        lax.fori_loop(0, SIDE, tile_step, 0)
    for k, i in every:
        store(k, i).wait()


def march(coef, flag, view, call, after):
    tiles = SIDE * len(call)
    pixels = tiles * TILE * COLS
    return pl.pallas_call(
        functools.partial(march_kernel, call=call),
        in_specs=[SMEM_SPEC, SMEM_SPEC, HBM_SPEC] + [ANY_SPEC] * len(after),
        out_specs=[ANY_SPEC] * len(call),
        out_shape=[jax.ShapeDtypeStruct((SIDE, 3, TILE, COLS), jnp.float32)] * len(call),
        scratch_shapes=[
            pltpu.VMEM((len(call), SIDE, SAMPLES, TILE, COLS), jnp.float32),
            pltpu.VMEM((len(call), SIDE, 3, TILE, COLS), jnp.float32),
            pltpu.SemaphoreType.DMA((len(call), SIDE)),
            pltpu.SemaphoreType.DMA((len(call), SIDE)),
        ],
        compiler_params=params(),
        cost_estimate=pl.CostEstimate(
            flops=40 * SAMPLES * pixels, bytes_accessed=44 * pixels, transcendentals=4 * SAMPLES * pixels
        ),
        name="march",
    )(coef, flag, view, *after)


def prefix_kernel(rank_ref, depth_ref, *refs):
    outs, (total_ref, buf, order_ref, sem) = refs[-8:-4], refs[-4:]
    grp = lax.axis_index("grp")
    y, x, core = place()
    second = jnp.where(core == 0, y, x)
    for j in range(N_MEM):
        order_ref[rank_ref[grp, j]] = j

    def strip(i, carry):
        cols = pl.ds(pl.multiple_of(i * STRIP, 128), STRIP)

        def step(r, running):
            j = order_ref[r]
            across = 8 * ((j >> 1) & 3) + 2 * (j >> 3) + (j & 1)
            spot = jnp.where(core == 0, j, across)
            buf[spot >> 3, spot & 7, :, cols] = running
            return running + depth_ref[j, :, cols]

        total_ref[:, cols] = lax.fori_loop(0, N_MEM, step, jnp.zeros((TILE, STRIP), jnp.float32), unroll=4)
        return carry

    lax.fori_loop(0, COLS // STRIP, strip, 0)
    copies = [pltpu.make_async_copy(buf.at[(second + k) & 3], outs[k], sem.at[k]) for k in range(SIDE)]
    for copy in copies:
        copy.start()
    for copy in copies:
        copy.wait()


def prefix(ranks, depths, after):
    line = jax.ShapeDtypeStruct((8, TILE, COLS), jnp.float32)
    return pl.pallas_call(
        prefix_kernel,
        in_specs=[SMEM_SPEC, VMEM_SPEC] + [ANY_SPEC] * len(after),
        out_specs=[ANY_SPEC] * SIDE + [VMEM_SPEC],
        out_shape=[line] * SIDE + [jax.ShapeDtypeStruct((TILE, COLS), jnp.float32)],
        scratch_shapes=[
            pltpu.VMEM((SIDE, 8, TILE, COLS), jnp.float32),
            pltpu.SMEM((N_MEM,), jnp.int32),
            pltpu.SemaphoreType.DMA((SIDE,)),
        ],
        compiler_params=params(PREFIX),
        cost_estimate=pl.CostEstimate(
            flops=N_MEM * TILE * COLS, bytes_accessed=8 * N_MEM * TILE * COLS, transcendentals=0
        ),
        name="prefix",
    )(ranks, depths, *after)


def weigh_kernel(*refs, shifts):
    count = len(shifts)
    colours, befores, outs = refs[:8], refs[8:8 + count], refs[-6 - count:-6]
    colbuf, depbuf, outbuf, colsem, depsem, outsem = refs[-6:]
    y, x, core = place()
    first, second = jnp.where(core == 0, x, y), jnp.where(core == 0, y, x)

    def fetch(i):
        spot = (second + shifts[i]) & 3
        return [pltpu.make_async_copy(befores[i], depbuf.at[i], depsem.at[i])] + [
            pltpu.make_async_copy(colours[n].at[spot], colbuf.at[i, n], colsem.at[i, n]) for n in range(8)
        ]

    def store(i):
        return pltpu.make_async_copy(outbuf.at[i], outs[i], outsem.at[i])

    slots = [2 * ((first - shift) & 3) + (1 - core if swap else core) for swap, shift in SENDS]
    for i in range(count):
        for copy in fetch(i):
            copy.start()
    for i in range(count):
        for copy in fetch(i):
            copy.wait()

        def step(n, carry, i=i):
            block, cols = patch(n, 256)
            acc = [None] * 3
            for k in range(8):
                light = jnp.exp2(-depbuf[i, slots[k], block, cols])
                for ch in range(3):
                    term = light * colbuf[i, k, ch, block, cols]
                    acc[ch] = term if acc[ch] is None else acc[ch] + term
            for ch in range(3):
                outbuf[i, ch, block, cols] = acc[ch]
            return carry

        lax.fori_loop(0, 8, step, 0)
        store(i).start()
    for i in range(count):
        store(i).wait()


def weigh(colours, befores, shifts, after):
    count = len(shifts)
    return pl.pallas_call(
        functools.partial(weigh_kernel, shifts=shifts),
        in_specs=[ANY_SPEC] * (8 + count + len(after)),
        out_specs=[ANY_SPEC] * count,
        out_shape=[jax.ShapeDtypeStruct((3, TILE, COLS), jnp.float32)] * count,
        scratch_shapes=[
            pltpu.VMEM((count, 8, 3, TILE, COLS), jnp.float32),
            pltpu.VMEM((count, 8, TILE, COLS), jnp.float32),
            pltpu.VMEM((count, 3, TILE, COLS), jnp.float32),
            pltpu.SemaphoreType.DMA((count, 8)),
            pltpu.SemaphoreType.DMA((count,)),
            pltpu.SemaphoreType.DMA((count,)),
        ],
        compiler_params=params(WEIGH),
        cost_estimate=pl.CostEstimate(
            flops=56 * count * TILE * COLS, bytes_accessed=140 * count * TILE * COLS, transcendentals=8 * count * TILE * COLS
        ),
        name="weigh",
    )(*colours, *[befores[-shift % SIDE] for shift in shifts], *after)


def slab_kernel(*refs):
    parts, total_ref, outs = refs[:4], refs[4], refs[5:]
    grp = lax.axis_index("grp")
    for shift in range(N_GRP):
        cols = pl.ds(pl.multiple_of(((grp + shift) & 3) * STRIP, 128), STRIP)
        for ch in range(3):
            outs[shift][ch] = (parts[0][ch, :, cols] + parts[1][ch, :, cols]) + (
                parts[2][ch, :, cols] + parts[3][ch, :, cols]
            )
        outs[shift][3] = 1.0 - jnp.exp2(-total_ref[:, cols])


def slab(parts, total):
    return pl.pallas_call(
        slab_kernel,
        in_specs=[VMEM_SPEC] * 5,
        out_specs=[VMEM_SPEC] * 4,
        out_shape=[jax.ShapeDtypeStruct((4, TILE, STRIP), jnp.float32)] * 4,
        compiler_params=params(SMALL),
        name="slab",
    )(*parts, total)


def final_kernel(rank_ref, *refs):
    layers, (out_ref, stack_ref, order_ref) = refs[:4], refs[4:]
    grp = lax.axis_index("grp")
    for j in range(N_GRP):
        order_ref[rank_ref[j]] = j
    for shift in range(N_GRP):
        stack_ref[(grp - shift) & 3] = layers[shift][...]
    pic = [jnp.zeros((TILE, STRIP), jnp.float32)] * 4
    for r in range(N_GRP):
        j = order_ref[r]
        free = 1.0 - pic[3]
        pic = [pic[c] + free * stack_ref[j, c] for c in range(4)]
    for c in range(4):
        out_ref[c] = pic[c]


def final(ranks, layers):
    return pl.pallas_call(
        final_kernel,
        in_specs=[SMEM_SPEC] + [VMEM_SPEC] * 4,
        out_specs=VMEM_SPEC,
        out_shape=jax.ShapeDtypeStruct((4, TILE, STRIP), jnp.float32),
        scratch_shapes=[pltpu.VMEM((N_GRP, 4, TILE, STRIP), jnp.float32), pltpu.SMEM((N_GRP,), jnp.int32)],
        compiler_params=params(SMALL),
        name="final",
    )(ranks, *layers)


def number(y, x, core):
    return 8 * (y % SIDE) + 2 * (x % SIDE) + core


def first_pairs(swap, shift):
    out = []
    for y in range(SIDE):
        for x in range(SIDE):
            for core in range(2):
                to = 1 - core if swap else core
                goal = number(y, x + shift, to) if to == 0 else number(y + shift, x, to)
                out.append((number(y, x, core), goal))
    return out


def second_pairs(shift):
    return [
        (number(y, x, core), number(y + shift, x, 0) if core == 0 else number(y, x + shift, 1))
        for y in range(SIDE)
        for x in range(SIDE)
        for core in range(2)
    ]


def body(volume, transfer_coef, group_order, member_order, active_mask):
    view = volume.reshape(SAMPLES, N_MEM, TILE, COLS)
    raw = []

    def send(n):
        swap, shift = SENDS[n]
        return lax.ppermute(raw[n], "mem", first_pairs(swap, shift)) if swap or shift else raw[n]

    own = depth(transfer_coef, active_mask, volume.reshape(SAMPLES, ROWS, COLS))
    depths = lax.all_to_all(own.reshape(N_MEM, TILE, COLS), "mem", 0, 0, tiled=True)
    for call in CALLS:
        raw += march(transfer_coef, active_mask, view, call, raw[-1:] or [own])
    colours = [send(n) for n in range(8)]
    *befores, total = prefix(member_order, depths, raw[-1:] + [colours[0], colours[1], colours[4]])
    befores = [befores[0]] + [lax.ppermute(befores[k], "mem", second_pairs(k)) for k in range(1, SIDE)]

    parts = []
    for shifts in ((0,), (3,), (2, 1)):
        for shift, part in zip(shifts, weigh(colours, befores, shifts, raw[-1:])):
            raw.append(part)
            parts.append(lax.ppermute(part, "mem", second_pairs(shift)) if shift else part)
    layers = slab(parts, total)
    layers = [layers[0]] + [
        lax.ppermute(layers[s], "grp", [(g, (g + s) % N_GRP) for g in range(N_GRP)]) for s in range(1, N_GRP)
    ]
    return final(group_order, layers)


def solution(mesh):
    in_specs = (P("grp", "mem", None, None, None), P(), P(), P(), P("grp", "mem"))
    out_specs = P(None, "mem", "grp")
    return jax.shard_map(body, mesh=mesh, in_specs=in_specs, out_specs=out_specs, check_vma=False)
```
